32 devices in a mesh: dp: 2 (over y), ctx: 4 (over z), tp: 4 (over x, core).
Axes of the slice: x: 2, y: 2, z: 4, core: 2. Of those that a mesh axis runs over, the one named last changes fastest.
Arguments:
- tokens: bfloat16 [24576, 768], P(('dp', 'ctx', 'tp')), may hold values from -6 to 6
- cotangent: bfloat16 [24576, 768], P(('dp', 'ctx', 'tp')), may hold values from -6 to 6
- gains: float32 [2, 768], replicated, may hold values from 0.1 to 1.9
- qkv_weight: bfloat16 [3, 768, 768], P(None, ('dp', 'ctx'), 'tp'), may hold values from -0.21875 to 0.21875
- proj_weight: bfloat16 [768, 768], P('tp', ('dp', 'ctx')), may hold values from -3 to 3
- router_weight: bfloat16 [768, 8], P(('dp', 'ctx')), may hold values from -0.15625 to 0.15625
- expert_up: bfloat16 [8, 768, 3072], P(('dp', 'tp'), None, 'ctx'), may hold values from -0.21875 to 0.21875
- expert_down: bfloat16 [8, 3072, 768], P(('dp', 'tp'), 'ctx'), may hold values from -1.1953125 to 1.1953125
- expert_ids: int32 [24576, 1], P(('dp', 'ctx', 'tp')), may hold values from 0 to 7
- slot_order: int32 [32, 768], P(('dp', 'ctx', 'tp')), may hold values from 0 to 767, each once within a row
- segment_ids: int32 [96], P(('dp', 'ctx')), may hold values from 0 to 5
Outputs:
- output: bfloat16 [24576, 768], P(('dp', 'ctx', 'tp'))
- grad_tokens: float32 [24576, 768], P(('dp', 'ctx', 'tp'))
- grad_gains: float32 [2, 768], P(None, ('dp', 'ctx'))
- grad_qkv: float32 [3, 768, 768], P(None, ('dp', 'ctx'), 'tp')
- grad_proj: float32 [768, 768], P('tp', ('dp', 'ctx'))
- grad_router: float32 [768, 8], P(('dp', 'ctx'))
- grad_up: float32 [8, 768, 3072], P(('dp', 'tp'), None, 'ctx')
- grad_down: float32 [8, 3072, 768], P(('dp', 'tp'), 'ctx')
The draws below stay inside these ranges and needn't reach their ends.
Inputs may be any that keep to these rules, and one draw needn't show every extreme that they name: `slot_order`: each row lists the 768 tokens of one device, from the first to take a slot to the last. `segment_ids`: continuations are numbered within their index of dp, ctx index first.
All inputs are finite; a program needn't handle non-finite values.
Results may differ from the reference program's by a relative error of at most 0.017.
Values may be sent and summed in bfloat16 or wider, within the bound.
No kernel may reach another device: no remote copies, remote signals or barrier semaphores. Data moves between devices by JAX's collectives and lax.ppermute only.
A program may use at most 256 MiB of HBM per device.

```python
import jax
import jax.numpy as jnp
from jax import lax

D = 768
HEADS = 12
HD = 64
FF = 3072
PLEN = 1024
CLEN = 128
TOK_DEV = 768
EXPERTS = 8
PROMPTS = 6
PROW = 256
CPD = 12
ROWS = 3072
TOKENS = 24576
CONT_ALL = 96
CAP = 120
N_DP = 2
N_CTX = 4
DEVICES = 32


def place_ends(array, stream_key, smallest, top_value):
    longest = array.shape.index(max(array.shape))
    spots = []
    for shift in (0, 1):
        where = [jax.random.randint(jax.random.fold_in(stream_key, axis), (), 0, length) for axis, length in enumerate(array.shape)]
        where[longest] = (where[longest] + shift) % array.shape[longest]
        spots.append(tuple(where))
    return array.at[spots[0]].set(smallest).at[spots[1]].set(top_value)


def block_levels(rng, shape, cuts, least, high):
    factor_of = 1.0
    for axis_at, parts in cuts:
        heights = jax.random.uniform(jax.random.fold_in(jax.random.fold_in(rng, 6), axis_at), (parts,), jnp.float32, least / len(cuts), high / len(cuts))
        factor_of = factor_of * jnp.repeat(jnp.exp(heights), shape[axis_at] // parts).reshape((-1,) + (1,) * (len(shape) - 1 - axis_at))
    return factor_of


def choose_distinct(key, rows, amount, top, lift):
    ranking = jax.random.permutation(jax.random.fold_in(key, 1), amount)
    pull = ranking
    for power in range(3):
        pull = pull * pull // amount
    pull = pull * lift // amount
    tickets = jax.random.randint(jax.random.fold_in(key, 2), (rows, amount), 0, 4096) + pull
    sure = jax.random.permutation(jax.random.fold_in(key, 3), rows)[jnp.arange(amount) % rows]
    tickets = jnp.where(jnp.arange(rows)[:, None] == sure[None, :], 1 << 14, tickets)
    score = tickets * amount + jnp.arange(amount)
    return lax.top_k(score.astype(jnp.int32), top)[1].astype(jnp.int32)


def bell_draw(stream_key, shape, spread, limit, split=(), held_as=jnp.bfloat16):
    values = jax.random.normal(stream_key, shape, jnp.float32) * spread
    if len(split) > 0:
        values = block_levels(stream_key, shape, split, -0.22, 0.18) * values
    return jnp.clip(values, min=-limit, max=limit).astype(held_as)


def setup_inputs(seed: int = 0) -> dict:
    key_of = jax.random.split(jax.random.key(seed), 12)
    tokens = bell_draw(key_of[0], (TOKENS, D), 1.0, 6.0, ((0, 32),))
    cotangent = bell_draw(key_of[1], (TOKENS, D), 1.0, 6.0, ((0, 32),))
    gains = jnp.clip(1.0 + 0.18 * jax.random.normal(key_of[2], (2, D), jnp.float32), 0.1, 1.9)
    qkv_weight = bell_draw(key_of[3], (3, D, HEADS * HD), D ** -0.5, 0.21875, ((1, 8), (2, 4)))
    proj_weight = bell_draw(key_of[4], (HEADS * HD, D), (max(D // 192, 1)) ** -0.5, 3.0, ((0, 4), (1, 8)))
    router_weight = bell_draw(key_of[5], (D, EXPERTS), (2 * D) ** -0.5, 0.15625, ((0, 8),))
    expert_up = bell_draw(key_of[6], (EXPERTS, D, FF), D ** -0.5, 0.21875, ((0, 8), (2, 4)))
    expert_down = bell_draw(key_of[7], (EXPERTS, FF, D), (0.025 * EXPERTS), 1.1953125, ((0, 8), (1, 4)))
    expert_ids = choose_distinct(key_of[8], TOKENS, EXPERTS, 1, 1024)
    slot_order = jax.vmap(lambda own: jax.random.permutation(own, TOK_DEV))(jax.random.split(key_of[9], DEVICES)).reshape((DEVICES, TOK_DEV)).astype(jnp.int32)
    segment_ids = place_ends(jax.random.randint(key_of[10], (CONT_ALL,), 0, PROMPTS), jax.random.fold_in(key_of[10], 1), 0, PROMPTS - 1).astype(jnp.int32)
    return {"tokens": tokens, "cotangent": cotangent, "gains": gains, "qkv_weight": qkv_weight, "proj_weight": proj_weight, "router_weight": router_weight, "expert_up": expert_up, "expert_down": expert_down, "expert_ids": expert_ids, "slot_order": slot_order, "segment_ids": segment_ids}


EPSILON = 1e-06
NEGATIVE = -1e+30
PRECISE = lax.Precision.HIGHEST

@jax.custom_vjp
def low(v):
    return lax.optimization_barrier(v.astype(jnp.bfloat16)).astype(jnp.float32)

@jax.custom_vjp
def low_back(v):
    return v

def low_keep(v):
    return (low(v), None)

def low_pass(kept, grad):
    return (grad,)

def back_keep(v):
    return (v, None)

def back_low(kept, grad):
    return (low(grad),)
low.defvjp(low_keep, low_pass)
low_back.defvjp(back_keep, back_low)

def normed(values, gain):
    return gain * (values * lax.rsqrt(lax.optimization_barrier(jnp.mean(values * values, axis=-1, keepdims=True)) + EPSILON))

def attend(queries, key_rows, value_rows, visible):
    scores = low_back(jnp.einsum('rhe,khe->hrk', queries, key_rows, precision=PRECISE) * 0.125)
    scores = jnp.where(visible, scores, NEGATIVE)
    weights = low(jax.nn.softmax(scores, axis=-1))
    return low_back(low(jnp.einsum('hrk,khe->rhe', weights, value_rows, precision=PRECISE)))

def expert_one(element):
    expert_rows, weight_up, weight_down = element
    hidden_pre = low_back(jnp.dot(expert_rows, weight_up, precision=PRECISE))
    hidden = low(jax.nn.gelu(hidden_pre))
    return low_back(low(jnp.dot(hidden, weight_down, precision=PRECISE)))

def slot_index(block_ids, block_order):
    sorted_hot = (jnp.take(block_ids, block_order)[:, None] == jnp.arange(EXPERTS)[None, :]).astype(jnp.int32)
    earlier = jnp.cumsum(sorted_hot, axis=0).astype(jnp.int32) - sorted_hot
    sorted_rank = lax.optimization_barrier(jnp.sum(earlier * sorted_hot, axis=1)).astype(jnp.int32)
    slot_rank = jnp.zeros((TOK_DEV,), jnp.int32).at[block_order.astype(jnp.int32)].set(sorted_rank)
    return jnp.where(slot_rank < CAP, block_ids * CAP + slot_rank, EXPERTS * CAP).astype(jnp.int32)

def reference(tokens, cotangent, gains, qkv_weight, proj_weight, router_weight, expert_up, expert_down, expert_ids, slot_order, segment_ids):
    chosen = expert_ids[:, 0].astype(jnp.int32)
    chosen_hot = (chosen[:, None] == jnp.arange(EXPERTS)[None, :]).astype(jnp.float32)
    flat = jax.vmap(slot_index)(chosen.reshape(DEVICES, TOK_DEV), slot_order)
    device_rows = jnp.arange(DEVICES).astype(jnp.int32)[:, None]
    segments = segment_ids.reshape(N_DP, N_CTX * CPD).astype(jnp.int32)
    causal = jnp.arange(PLEN)[:, None] >= jnp.arange(PLEN)[None, :]
    columns = jnp.arange(PLEN + CLEN)
    cont_visible = (columns[None, :] < PLEN) | (columns[None, :] - PLEN <= jnp.arange(CLEN)[:, None])
    width = HEADS * HD

    def prompt_one(triple):
        return attend(triple[0], triple[1], triple[2], causal)

    def group(element):
        prompt_triples, cont_triples, group_segments = element
        prompt_out = lax.map(jax.checkpoint(prompt_one), prompt_triples)

        def cont_one(paired):
            triple, which = paired
            key_rows = jnp.concatenate([prompt_triples[which, 1], triple[1]], axis=0)
            value_rows = jnp.concatenate([prompt_triples[which, 2], triple[2]], axis=0)
            return attend(triple[0], key_rows, value_rows, cont_visible)
        cont_out = lax.map(jax.checkpoint(cont_one), (cont_triples, group_segments))
        return (prompt_out, cont_out)

    def forward(inputs, gain, qkv_full, proj_full, router_full, up_full, down_full):
        normed_one = low(normed(inputs, gain[0]))
        projected = low_back(low(jnp.einsum('td,jdc->jtc', normed_one, qkv_full, precision=PRECISE)))
        blocks = projected.reshape(3, N_DP, N_CTX, ROWS, HEADS, HD)
        prompt_part = blocks[:, :, :, :PROMPTS * PROW].reshape(3, N_DP, N_CTX, PROMPTS, PROW, HEADS, HD)
        prompt_part = prompt_part.transpose(1, 3, 0, 2, 4, 5, 6).reshape(N_DP, PROMPTS, 3, PLEN, HEADS, HD)
        cont_part = blocks[:, :, :, PROMPTS * PROW:].reshape(3, N_DP, N_CTX * CPD, CLEN, HEADS, HD)
        cont_part = cont_part.transpose(1, 2, 0, 3, 4, 5)
        prompt_out, cont_out = lax.map(group, (prompt_part, cont_part, segments))
        prompt_out = prompt_out.reshape(N_DP, PROMPTS, N_CTX, PROW, width).transpose(0, 2, 1, 3, 4)
        prompt_out = prompt_out.reshape(N_DP, N_CTX, PROMPTS * PROW, width)
        cont_out = cont_out.reshape(N_DP, N_CTX, CPD * CLEN, width)
        attended = jnp.concatenate([prompt_out, cont_out], axis=2).reshape(TOKENS, width)
        branch = low_back(jnp.dot(attended, proj_full, precision=PRECISE))
        middle = inputs + branch
        normed_two = low(normed(middle, gain[1]))
        logits = low_back(jnp.dot(normed_two, router_full, precision=PRECISE))
        gate_value = lax.optimization_barrier(jnp.sum(jax.nn.softmax(logits, axis=-1) * chosen_hot, axis=-1))
        stacked = jnp.zeros((DEVICES, EXPERTS * CAP + 1, D), jnp.float32)
        stacked = stacked.at[device_rows, flat].add(normed_two.reshape(DEVICES, TOK_DEV, D))
        slots = low_back(stacked[:, :EXPERTS * CAP])
        per_expert = slots.reshape(DEVICES, EXPERTS, CAP, D).transpose(1, 0, 2, 3).reshape(EXPERTS, DEVICES * CAP, D)
        made = lax.map(jax.checkpoint(expert_one), (per_expert, up_full, down_full))
        made = made.reshape(EXPERTS, DEVICES, CAP, D).transpose(1, 0, 2, 3).reshape(DEVICES, EXPERTS * CAP, D)
        made = jnp.concatenate([made, jnp.zeros((DEVICES, 1, D), jnp.float32)], axis=1)
        routed = jnp.take_along_axis(made, flat[:, :, None], axis=1).reshape(TOKENS, D)
        return middle + gate_value[:, None] * routed
    result, pullback = jax.vjp(forward, tokens.astype(jnp.float32), gains, qkv_weight.astype(jnp.float32), proj_weight.astype(jnp.float32), router_weight.astype(jnp.float32), expert_up.astype(jnp.float32), expert_down.astype(jnp.float32))
    grads = pullback(cotangent.astype(jnp.float32))
    return (result.astype(jnp.bfloat16), grads[0], grads[1], grads[2], grads[3], grads[4], grads[5], grads[6])
```

```python
import jax
import jax.numpy as jnp
from jax import lax
from jax.sharding import PartitionSpec as P

HD = 64
PLEN = 1024
CLEN = 128
CONTS = 8

EPSILON = 1e-06
NEGATIVE = -1e30
PRECISE = lax.Precision.HIGHEST
F32 = jnp.float32
BF16 = jnp.bfloat16


def xor_swap(value, axis, size, mask):
    return lax.ppermute(value, axis, [(place, place ^ mask) for place in range(size)])


def ring_step(value, axis, size, shift):
    return lax.ppermute(value, axis, [(place, (place + shift) % size) for place in range(size)])


def pick(stacked, index):
    return lax.dynamic_index_in_dim(stacked, index, 0, keepdims=False)


def xor_gather(value, axis, size, order=None):
    if order is None:
        order = [1 << bit for bit in range(size.bit_length() - 1)]
    have = {0: value}
    for mask in order:
        keys = sorted(have)
        moved = xor_swap(jnp.stack([have[key] for key in keys]), axis, size, mask)
        for place, key in enumerate(keys):
            have[key ^ mask] = moved[place]
    return [have[key] for key in range(size)]


def in_order(pieces, me):
    stacked = jnp.stack(pieces)
    return jnp.stack([pick(stacked, me ^ place) for place in range(len(pieces))])


def xor_exchange(pieces, axis, size):
    return [pieces[0]] + [xor_swap(pieces[mask], axis, size, mask) for mask in range(1, size)]


def rms_unit(values):
    factor = lax.rsqrt(jnp.mean(values * values, axis=-1, keepdims=True) + EPSILON)
    return (values * factor, factor)


def rms_backward(grad_normed, unit_part, factor, gain):
    scaled = grad_normed * gain
    inner = jnp.mean(scaled * unit_part, axis=-1, keepdims=True)
    return (factor * (scaled - unit_part * inner), jnp.sum(grad_normed * unit_part, axis=0))


def masked_scores(queries, key_rows, visible):
    scores = (
        jnp.einsum("brhe,bkhe->bhrk", queries, key_rows, preferred_element_type=F32) * 0.125
    )
    return jnp.where(visible, scores, NEGATIVE)


def attend_forward(queries, key_rows, value_rows, visible):
    scores = masked_scores(queries, key_rows, visible)
    peak = jnp.max(scores, axis=-1, keepdims=True)
    shifted = jnp.exp(scores - peak)
    total = jnp.sum(shifted, axis=-1, keepdims=True)
    weights = (shifted / total).astype(BF16)
    mixed = jnp.einsum("bhrk,bkhe->brhe", weights, value_rows, preferred_element_type=F32)
    return (mixed.astype(BF16), peak + jnp.log(total))


def attend_backward(queries, key_rows, value_rows, visible, log_total, grad_mixed):
    weights = jnp.exp(masked_scores(queries, key_rows, visible) - log_total)
    grad_weights = jnp.einsum("brhe,bkhe->bhrk", grad_mixed, value_rows, preferred_element_type=F32)
    centre = jnp.sum(weights * grad_weights, axis=-1, keepdims=True)
    grad_scores = (weights * (grad_weights - centre)).astype(BF16)
    grad_queries = (
        jnp.einsum("bhrk,bkhe->brhe", grad_scores, key_rows, preferred_element_type=F32) * 0.125
    )
    grad_keys = (
        jnp.einsum("bhrk,brhe->bkhe", grad_scores, queries, preferred_element_type=F32) * 0.125
    )
    grad_values = jnp.einsum(
        "bhrk,brhe->bkhe", weights.astype(BF16), grad_mixed, preferred_element_type=F32
    )
    return (grad_queries, grad_keys, grad_values)


def slot_dispatch(chosen, priority, first, expert_count, capacity):
    tokens = chosen.shape[0]
    expert_range = jnp.arange(expert_count)
    chosen_hot = chosen[:, None] == expert_range[None, :]
    order_hot = (priority[:, None] == jnp.arange(tokens)[None, :]).astype(BF16)
    sorted_hot = jnp.dot(order_hot, chosen_hot.astype(BF16), preferred_element_type=F32)
    places = jnp.arange(tokens)
    before = (places[:, None] > places[None, :]).astype(BF16)
    earlier = jnp.dot(before, sorted_hot.astype(BF16), preferred_element_type=F32)
    sorted_rank = jnp.minimum(jnp.sum(earlier * sorted_hot, axis=1), capacity)
    rank = jnp.einsum(
        "it,i->t", order_hot, sorted_rank.astype(BF16), preferred_element_type=F32
    ).astype(jnp.int32)
    place = jnp.where(rank < capacity, (chosen ^ first) * capacity + rank, -1)
    dispatch = place[:, None] == jnp.arange(expert_count * capacity)[None, :]
    return (chosen_hot, dispatch.astype(BF16))


def shards(
    tokens,
    cotangent,
    gains,
    qkv_weight,
    proj_weight,
    router_weight,
    expert_up,
    expert_down,
    expert_ids,
    slot_order,
    segment_ids,
):
    dp_count, ctx_count, tp_count = (lax.axis_size(name) for name in ("dp", "ctx", "tp"))
    dp_index, ctx_index, tp_index = (lax.axis_index(name) for name in ("dp", "ctx", "tp"))
    group = dp_count * tp_count
    group_index = dp_index * tp_count + tp_index
    tok_dev, width = tokens.shape
    expert_count = router_weight.shape[1]
    capacity = 5 * tok_dev // (4 * expert_count)
    prompt_rows = PLEN // ctx_count
    conts_here = segment_ids.shape[0]
    prompts_here = conts_here * ctx_count // CONTS
    head_rows = prompts_here * prompt_rows
    local_width = qkv_weight.shape[2]
    local_heads = local_width // HD
    shard_rows = qkv_weight.shape[1]
    tp_order = [2, 1]

    full_up = lax.all_gather(expert_up, "ctx", axis=2, tiled=True)[0]
    full_down = lax.all_gather(expert_down, "ctx", axis=1, tiled=True)[0]

    def gather_weights(part):
        by_ctx = in_order(xor_gather(part, "ctx", ctx_count), ctx_index)
        by_dp = in_order(xor_gather(by_ctx, "dp", dp_count), dp_index)
        return by_dp.reshape(dp_count * ctx_count * part.shape[0], part.shape[1])

    full_qkv = gather_weights(qkv_weight.transpose(1, 0, 2).reshape(shard_rows, 3 * local_width))
    proj_router = gather_weights(jnp.concatenate([proj_weight.T, router_weight], axis=1))
    full_router = proj_router[:, local_width:]
    proj_near = jnp.concatenate(
        xor_gather(proj_router[:, :local_width], "tp", tp_count, tp_order), axis=1
    )

    block_rows = in_order(xor_gather(tokens, "tp", tp_count, tp_order), tp_index).reshape(-1, width)
    unit_block, _ = rms_unit(block_rows.astype(F32))
    normed_one = (gains[0] * unit_block).astype(BF16)
    projected = jnp.dot(normed_one, full_qkv, preferred_element_type=F32).astype(BF16)
    query, key, value = (
        projected[:, part * local_width : (part + 1) * local_width] for part in range(3)
    )
    prompt_shape = (prompts_here, prompt_rows, local_heads, HD)
    cont_shape = (conts_here, CLEN, local_heads, HD)
    query_prompt = query[:head_rows].reshape(prompt_shape)
    query_cont = query[head_rows:].reshape(cont_shape)
    key_cont = key[head_rows:].reshape(cont_shape)
    value_cont = value[head_rows:].reshape(cont_shape)
    pair = jnp.stack([key[:head_rows], value[:head_rows]]).reshape((2,) + prompt_shape)
    ring = [pair]
    for _ in range(ctx_count - 1):
        ring.append(ring_step(ring[-1], "ctx", ctx_count, 1))
    pairs_all = jnp.concatenate(ring, axis=2)
    keys_all, values_all = pairs_all[0], pairs_all[1]
    columns = jnp.arange(PLEN + CLEN)
    ring_place = jnp.arange(PLEN) // prompt_rows
    row_range = jnp.arange(prompt_rows)
    prompt_visible = jnp.where(
        ring_place[None, :] == 0,
        row_range[:, None] >= jnp.arange(PLEN)[None, :],
        ring_place[None, :] <= ctx_index,
    )
    cont_visible = (columns[None, :] < PLEN) | (
        columns[None, :] - PLEN <= jnp.arange(CLEN)[:, None]
    )
    cont_keys = jnp.concatenate([jnp.take(keys_all, segment_ids, axis=0), key_cont], axis=1)
    cont_values = jnp.concatenate([jnp.take(values_all, segment_ids, axis=0), value_cont], axis=1)
    mixed_prompt, total_prompt = attend_forward(query_prompt, keys_all, values_all, prompt_visible)
    mixed_cont, total_cont = attend_forward(query_cont, cont_keys, cont_values, cont_visible)
    attended = jnp.concatenate(
        [mixed_prompt.reshape(head_rows, local_width), mixed_cont.reshape(-1, local_width)], axis=0
    ).reshape(tp_count, tok_dev, local_width)
    attended_near = jnp.concatenate(
        xor_exchange([pick(attended, tp_index ^ k) for k in range(tp_count)], "tp", tp_count),
        axis=1,
    )
    branch = jnp.einsum("rc,dc->rd", attended_near, proj_near, preferred_element_type=F32)
    tokens_wide = tokens.astype(F32)
    middle = tokens_wide + branch
    unit_two, factor_two = rms_unit(middle)
    normed_two = (gains[1] * unit_two).astype(BF16)
    logits = jnp.dot(normed_two, full_router, preferred_element_type=F32)
    router_probs = jax.nn.softmax(logits, axis=-1)
    chosen_hot, dispatch = slot_dispatch(
        expert_ids[:, 0], slot_order[0], group_index, expert_count, capacity
    )
    gate_value = jnp.sum(jnp.where(chosen_hot, router_probs, 0.0), axis=-1)

    def to_slots(rows):
        return jnp.einsum("tj,td->jd", dispatch, rows, preferred_element_type=F32).astype(BF16)

    def from_slots(rows):
        return jnp.dot(dispatch, rows, preferred_element_type=F32)

    def exchange_slots(rows):
        pieces = rows.reshape(group, -1, width)
        moved = xor_exchange([pieces[k] for k in range(group)], ("dp", "tp"), group)
        return jnp.concatenate(moved, axis=0)

    upstream = cotangent.astype(F32)
    weighted = (gate_value[:, None] * upstream).astype(BF16)
    arrived = exchange_slots(to_slots(normed_two))
    grad_arrived = exchange_slots(to_slots(weighted))
    hidden_pre = jnp.dot(arrived, full_up, preferred_element_type=F32)
    hidden = jax.nn.gelu(hidden_pre).astype(BF16)
    produced = jnp.dot(hidden, full_down, preferred_element_type=F32).astype(BF16)
    grad_hidden = jnp.einsum("cd,fd->cf", grad_arrived, full_down, preferred_element_type=F32)
    grad_pre = jax.vjp(jax.nn.gelu, hidden_pre)[1](grad_hidden)[0].astype(BF16)
    rows_grad = jnp.einsum("cf,df->cd", grad_pre, full_up, preferred_element_type=F32).astype(BF16)
    down_part = jnp.einsum("cf,cd->fd", hidden, grad_arrived, preferred_element_type=F32)
    up_part = jnp.einsum("cd,cf->df", arrived, grad_pre, preferred_element_type=F32)
    routed_rows = from_slots(exchange_slots(produced))
    grad_returned = from_slots(exchange_slots(rows_grad))
    grad_up = lax.psum_scatter(
        up_part.astype(BF16)[None], "ctx", scatter_dimension=2, tiled=True
    ).astype(F32)
    grad_down = lax.psum_scatter(
        down_part.astype(BF16)[None], "ctx", scatter_dimension=1, tiled=True
    ).astype(F32)

    output = (middle + gate_value[:, None] * routed_rows).astype(BF16)
    grad_gate = jnp.sum(upstream * routed_rows, axis=-1)
    grad_logits = (
        (grad_gate * gate_value)[:, None] * (chosen_hot.astype(F32) - router_probs)
    ).astype(BF16)
    router_part = jnp.einsum("td,te->de", normed_two, grad_logits, preferred_element_type=F32)
    grad_second = grad_returned + jnp.einsum(
        "te,de->td", grad_logits, full_router, preferred_element_type=F32
    )
    middle_part, gain_two = rms_backward(grad_second, unit_two, factor_two, gains[1])
    grad_middle = upstream + middle_part
    grad_low = grad_middle.astype(BF16)
    grad_near = jnp.dot(grad_low, proj_near, preferred_element_type=F32).astype(BF16)
    grad_attended = in_order(
        xor_exchange(
            [grad_near[:, k * local_width : (k + 1) * local_width] for k in range(tp_count)],
            "tp",
            tp_count,
        ),
        tp_index,
    ).reshape(-1, local_width)
    prompt_grads = attend_backward(
        query_prompt,
        keys_all,
        values_all,
        prompt_visible,
        total_prompt,
        grad_attended[:head_rows].reshape(prompt_shape),
    )
    cont_grads = attend_backward(
        query_cont,
        cont_keys,
        cont_values,
        cont_visible,
        total_cont,
        grad_attended[head_rows:].reshape(cont_shape),
    )
    segment_hot = (segment_ids[:, None] == jnp.arange(prompts_here)[None, :]).astype(F32)
    pair_total = [
        prompt_grads[part]
        + jnp.einsum("cp,ckhe->pkhe", segment_hot, cont_grads[part][:, :PLEN], precision=PRECISE)
        for part in (1, 2)
    ]
    pair_total = jnp.stack(pair_total).reshape(
        2, prompts_here, ctx_count, prompt_rows, local_width
    )
    running = pair_total[:, :, ctx_count - 1].astype(BF16)
    for place in range(ctx_count - 2, -1, -1):
        arriving = ring_step(running, "ctx", ctx_count, -1)
        running = (pair_total[:, :, place] + arriving.astype(F32)).astype(BF16)
    grad_projected = jnp.concatenate(
        [
            jnp.concatenate(
                [
                    prompt_grads[0].reshape(head_rows, local_width),
                    cont_grads[0].reshape(-1, local_width),
                ],
                axis=0,
            ).astype(BF16),
            jnp.concatenate(
                [
                    running[0].reshape(head_rows, local_width),
                    cont_grads[1][:, PLEN:].reshape(-1, local_width).astype(BF16),
                ],
                axis=0,
            ),
            jnp.concatenate(
                [
                    running[1].reshape(head_rows, local_width),
                    cont_grads[2][:, PLEN:].reshape(-1, local_width).astype(BF16),
                ],
                axis=0,
            ),
        ],
        axis=1,
    )
    qkv_part = jnp.einsum("rd,rc->dc", normed_one, grad_projected, preferred_element_type=F32)
    grad_blocks = grad_projected.reshape(tp_count, tok_dev, 3 * local_width)
    first_near = [
        jnp.einsum("rc,dc->rd", pick(grad_blocks, tp_index ^ k), full_qkv, preferred_element_type=F32)
        for k in range(tp_count)
    ]

    def scatter_near(pieces, order):
        pieces = dict(enumerate(pieces))
        for mask in order:
            sent = [key for key in sorted(pieces) if key & mask]
            moved = xor_swap(
                jnp.stack([pieces[key].astype(BF16) for key in sent]), "tp", tp_count, mask
            )
            for place, key in enumerate(sent):
                pieces[key ^ mask] = pieces[key ^ mask] + moved[place].astype(F32)
                del pieces[key]
        return pieces[0]

    scatter_order = tp_order[::-1]
    grad_first = scatter_near(first_near, scatter_order)
    unit_one, factor_one = rms_unit(tokens_wide)
    rows_part, gain_one = rms_backward(grad_first, unit_one, factor_one, gains[0])
    grad_tokens = rows_part + grad_middle

    proj_blocks = jnp.einsum("rc,rd->dc", attended_near, grad_low, preferred_element_type=F32)
    proj_part = scatter_near(
        [proj_blocks[:, k * local_width : (k + 1) * local_width] for k in range(tp_count)],
        scatter_order,
    )
    small_part = jnp.concatenate(
        [router_part, jnp.stack([gain_one, gain_two], axis=1)], axis=1
    )
    packed = jnp.concatenate([qkv_part, proj_part, small_part], axis=1)
    packed = packed.reshape(dp_count, ctx_count, shard_rows, -1).astype(BF16)

    def scatter_ordered(values, axis, size, me):
        moved = xor_exchange([pick(values, me ^ k) for k in range(size)], axis, size)
        return sum(piece.astype(F32) for piece in moved)

    summed = scatter_ordered(packed, "dp", dp_count, dp_index).astype(BF16)
    summed = scatter_ordered(summed, "ctx", ctx_count, ctx_index)
    small_sum = summed[:, 4 * local_width :]
    small_all = xor_exchange([small_sum.astype(BF16)] * tp_count, "tp", tp_count)
    small_sum = small_sum + sum(piece.astype(F32) for piece in small_all[1:])
    grad_qkv = summed[:, : 3 * local_width].reshape(shard_rows, 3, local_width).transpose(1, 0, 2)
    grad_proj = summed[:, 3 * local_width : 4 * local_width].T
    grad_router = small_sum[:, :expert_count]
    grad_gains = small_sum[:, expert_count:].T
    return (output, grad_tokens, grad_gains, grad_qkv, grad_proj, grad_router, grad_up, grad_down)


def solution(mesh):
    in_specs = (
        P(("dp", "ctx", "tp"), None),
        P(("dp", "ctx", "tp"), None),
        P(),
        P(None, ("dp", "ctx"), "tp"),
        P("tp", ("dp", "ctx")),
        P(("dp", "ctx"), None),
        P(("dp", "tp"), None, "ctx"),
        P(("dp", "tp"), "ctx", None),
        P(("dp", "ctx", "tp"), None),
        P(("dp", "ctx", "tp"), None),
        P(("dp", "ctx")),
    )
    out_specs = (
        P(("dp", "ctx", "tp"), None),
        P(("dp", "ctx", "tp"), None),
        P(None, ("dp", "ctx")),
        P(None, ("dp", "ctx"), "tp"),
        P("tp", ("dp", "ctx")),
        P(("dp", "ctx"), None),
        P(("dp", "tp"), None, "ctx"),
        P(("dp", "tp"), "ctx", None),
    )
    return jax.shard_map(shards, mesh=mesh, in_specs=in_specs, out_specs=out_specs, check_vma=False)
```

```python
import functools

import jax
import jax.numpy as jnp
from jax import lax
from jax.experimental import pallas as pl
from jax.experimental.pallas import tpu as pltpu
from jax.sharding import PartitionSpec as P

HD = 64
PLEN = 1024
CLEN = 128
CONTS = 8

EPSILON = 1e-06
NEGATIVE = -1e30
F32 = jnp.float32
BF16 = jnp.bfloat16
ROOT = 0.7978845608028654
CUBE = 0.044715
UNITS = 768


def xor_swap(value, axis, size, mask):
    return lax.ppermute(value, axis, [(place, place ^ mask) for place in range(size)])


def ring_step(value, axis, size, shift):
    return lax.ppermute(value, axis, [(place, (place + shift) % size) for place in range(size)])


def pick(stacked, index):
    return lax.dynamic_index_in_dim(stacked, index, 0, keepdims=False)


def xor_gather(value, axis, size, order=None):
    if order is None:
        order = [1 << bit for bit in range(size.bit_length() - 1)]
    have = {0: value}
    for mask in order:
        keys = sorted(have)
        moved = xor_swap(jnp.stack([have[key] for key in keys]), axis, size, mask)
        for place, key in enumerate(keys):
            have[key ^ mask] = moved[place]
    return [have[key] for key in range(size)]


def in_order(pieces, me):
    stacked = jnp.stack(pieces)
    return jnp.stack([pick(stacked, me ^ place) for place in range(len(pieces))])


def xor_exchange(pieces, axis, size):
    return [pieces[0]] + [xor_swap(pieces[mask], axis, size, mask) for mask in range(1, size)]


def rms_unit(values):
    factor = lax.rsqrt(jnp.mean(values * values, axis=-1, keepdims=True) + EPSILON)
    return (values * factor, factor)


def rms_backward(grad_normed, unit_part, factor, gain):
    scaled = grad_normed * gain
    inner = jnp.mean(scaled * unit_part, axis=-1, keepdims=True)
    return (factor * (scaled - unit_part * inner), jnp.sum(grad_normed * unit_part, axis=0))


def dot_last(left, right):
    return lax.dot_general(left, right, (((1,), (1,)), ((), ())), preferred_element_type=F32)

def dot_plain(left, right):
    return lax.dot_general(left, right, (((1,), (0,)), ((), ())), preferred_element_type=F32)

def add_all(parts):
    return functools.reduce(jnp.add, parts)

def key_lanes(rows, width):
    return rows[:, : width + (-width) % 128]

def value_lanes(rows, width):
    return rows[:, width - (-width) % 128 :]

def spread_heads(columns, ahead, behind):
    width, count = columns.shape
    groups = []
    for first in range(0, width, HD):
        pieces = [columns[first : first + HD]]
        above, below = ahead + first, width - first - HD + behind
        if above:
            pieces.insert(0, jnp.zeros((above, count), columns.dtype))
        if below:
            pieces.append(jnp.zeros((below, count), columns.dtype))
        groups.append(jnp.concatenate(pieces, axis=0))
    return jnp.concatenate(groups, axis=1)

def causal(scores, count):
    key_row = lax.broadcasted_iota(jnp.int32, scores.shape, 0)
    query_row = lax.broadcasted_iota(jnp.int32, scores.shape, 1) % count
    return jnp.where(key_row <= query_row, scores, NEGATIVE)

def attend_forward_kernel(prompts, scalars, segments, query, local, *rest):
    remote, (out, lse_prompt, lse_cont) = rest[:-3], rest[-3:]
    width = query.shape[0]
    rows = remote[0].shape[1]
    conts = segments.shape[0]
    clen = (local.shape[0] - prompts * rows) // conts
    pad = (-width) % 128

    def attend(start, count, blocks, mask):
        lanes = pl.ds(start, count)
        spread = spread_heads(query[:, lanes], 0, pad)
        scores = [mask(place, dot_plain(key_lanes(block, width), spread)) for place, block in enumerate(blocks)]
        peak = functools.reduce(jnp.maximum, [jnp.max(part, axis=0, keepdims=True) for part in scores])
        shifted = [jnp.exp(part - peak) for part in scores]
        total = add_all([jnp.sum(part, axis=0, keepdims=True) for part in shifted])
        weights = [part.astype(BF16) for part in shifted]
        flipped = [value_lanes(block, width).T for block in blocks]
        for head in range(width // HD):
            group = slice(head * count, (head + 1) * count)
            part = slice(pad + head * HD, pad + (head + 1) * HD)
            mixed = add_all([dot_plain(flip[part], one[:, group]) for flip, one in zip(flipped, weights)])
            out[head * HD : (head + 1) * HD, lanes] = (mixed / total[:, group]).astype(BF16)
        return peak + jnp.log(total)

    @pl.loop(0, prompts)
    def _(prompt):
        start = pl.multiple_of(prompt * rows, rows)
        blocks = [local[pl.ds(start, rows), :]] + [one[prompt] for one in remote]
        lse_prompt[prompt] = attend(start, rows, blocks,
            lambda place, scores: jnp.where(place <= scalars[0], scores, NEGATIVE) if place else causal(scores, rows))

    @pl.loop(0, conts)
    def _(cont):
        start = pl.multiple_of(prompts * rows + cont * clen, clen)
        segment = segments[cont]
        first = pl.multiple_of(segment * rows, rows)
        blocks = [local[pl.ds(start, clen), :], local[pl.ds(first, rows), :]] + [one[segment] for one in remote]
        lse_cont[cont] = attend(start, clen, blocks, lambda place, scores: scores if place else causal(scores, clen))

def attend_backward_kernel(prompts, scalars, segments, query, grad, lse_prompt, lse_cont, local, *rest):
    places = (len(rest) - 2) // 2 + 1
    remote, (grad_query, grad_local), grad_remote, sums = rest[: places - 1], rest[places - 1 : places + 1], rest[places + 1 : -1], rest[-1]
    width = query.shape[0]
    rows = remote[0].shape[1]
    conts = segments.shape[0]
    clen = (local.shape[0] - prompts * rows) // conts
    pad = (-width) % 128

    def attend(start, count, lse, blocks, mask):
        lanes = pl.ds(start, count)
        query_spread = spread_heads(query[:, lanes], 0, pad)
        grad_spread = spread_heads(grad[:, lanes], pad, 0)
        weights = [jnp.exp(mask(place, dot_plain(key_lanes(block, width), query_spread)) - lse) for place, block in enumerate(blocks)]
        slopes = [dot_plain(value_lanes(block, width), grad_spread) for block in blocks]
        centre = add_all([jnp.sum(part * slope, axis=0, keepdims=True) for part, slope in zip(weights, slopes)])
        grad_scores = [(part * (slope - centre)).astype(BF16) for part, slope in zip(weights, slopes)]
        flipped = [key_lanes(block, width).T for block in blocks]
        for head in range(width // HD):
            group = slice(head * count, (head + 1) * count)
            part = slice(head * HD, (head + 1) * HD)
            mixed = add_all([dot_plain(flip[part], one[:, group]) for flip, one in zip(flipped, grad_scores)])
            grad_query[part, lanes] = (mixed * 0.125).astype(BF16)
        results = []
        for part, one in zip(weights, grad_scores):
            key_part = dot_last(one, query_spread)
            value_part = dot_last(part.astype(BF16), grad_spread)
            if pad:
                edge = width - pad
                results.append(jnp.concatenate([key_part[:, :edge], key_part[:, edge:] + value_part[:, : 2 * pad], value_part[:, 2 * pad :]], axis=1))
            else:
                results.append(jnp.concatenate([key_part, value_part], axis=1))
        return results

    @pl.loop(0, prompts)
    def _(prompt):
        start = pl.multiple_of(prompt * rows, rows)
        blocks = [local[pl.ds(start, rows), :]] + [one[prompt] for one in remote]
        results = attend(start, rows, lse_prompt[prompt], blocks,
            lambda place, scores: jnp.where(place <= scalars[0], scores, NEGATIVE) if place else causal(scores, rows))
        for place in range(places):
            sums[place, prompt] = results[place]

    @pl.loop(0, conts)
    def _(cont):
        start = pl.multiple_of(prompts * rows + cont * clen, clen)
        segment = segments[cont]
        first = pl.multiple_of(segment * rows, rows)
        blocks = [local[pl.ds(start, clen), :], local[pl.ds(first, rows), :]] + [one[segment] for one in remote]
        results = attend(start, clen, lse_cont[cont], blocks, lambda place, scores: scores if place else causal(scores, clen))
        grad_local[pl.ds(start, clen), :] = results[0].astype(BF16)
        for place in range(places):
            sums[place, segment] += results[place + 1]

    @pl.loop(0, prompts)
    def _(prompt):
        grad_local[pl.ds(pl.multiple_of(prompt * rows, rows), rows), :] = sums[0, prompt].astype(BF16)
        for place in range(1, places):
            grad_remote[place - 1][prompt] = sums[place, prompt].astype(BF16)

VM = pl.BlockSpec(memory_space=pltpu.VMEM)
SM = pl.BlockSpec(memory_space=pltpu.SMEM)

def attend_forward(scalars, segments, query, local, remote):
    prompts, rows, _ = remote[0].shape
    conts = segments.shape[0]
    clen = (local.shape[0] - prompts * rows) // conts
    heads = query.shape[0] // HD
    scores = heads * (prompts * rows * (len(remote) + 1) * rows + conts * clen * ((len(remote) + 1) * rows + clen))
    return pl.pallas_call(functools.partial(attend_forward_kernel, prompts),
        out_shape=(jax.ShapeDtypeStruct(query.shape, BF16), jax.ShapeDtypeStruct((prompts, 1, heads * rows), F32), jax.ShapeDtypeStruct((conts, 1, heads * clen), F32)),
        in_specs=[SM, SM] + [VM] * (2 + len(remote)), out_specs=(VM,) * 3,
        compiler_params=pltpu.CompilerParams(vmem_limit_bytes=56 * 2**20),
        cost_estimate=pl.CostEstimate(flops=16 * HD * scores, bytes_accessed=10**7, transcendentals=scores),
    )(scalars, segments, query, local, *remote)

def attend_backward(scalars, segments, query, grad, lse_prompt, lse_cont, local, remote):
    prompts, rows, _ = remote[0].shape
    conts = segments.shape[0]
    clen = (local.shape[0] - prompts * rows) // conts
    heads = query.shape[0] // HD
    scores = heads * (prompts * rows * (len(remote) + 1) * rows + conts * clen * ((len(remote) + 1) * rows + clen))
    shape = lambda value: jax.ShapeDtypeStruct(value.shape, BF16)
    return pl.pallas_call(functools.partial(attend_backward_kernel, prompts),
        out_shape=(shape(query), shape(local)) + tuple(shape(one) for one in remote),
        in_specs=[SM, SM] + [VM] * (5 + len(remote)), out_specs=(VM,) * (2 + len(remote)),
        scratch_shapes=[pltpu.VMEM((len(remote) + 1,) + remote[0].shape, F32)],
        compiler_params=pltpu.CompilerParams(vmem_limit_bytes=60 * 2**20),
        cost_estimate=pl.CostEstimate(flops=40 * HD * scores, bytes_accessed=2 * 10**7, transcendentals=scores),
    )(scalars, segments, query, grad, lse_prompt, lse_cont, local, *remote)


def expert_forward_kernel(rows, up, down, produced, hidden_pre, total):
    step = pl.program_id(0)
    pre = dot_plain(rows[...], up[...])
    hidden_pre[...] = pre
    inner = ROOT * (pre + CUBE * (pre * pre * pre))
    hidden = (0.5 * pre * (1.0 + jnp.tanh(inner))).astype(BF16)
    part = dot_plain(hidden, down[...])
    @pl.when(step == 0)
    def _():
        total[...] = part
    @pl.when(step > 0)
    def _():
        total[...] += part
    @pl.when(step == pl.num_programs(0) - 1)
    def _():
        produced[...] = total[...].astype(BF16)

def expert_backward_kernel(rows, grads, hidden_pre, up, down, rows_grad, grad_up, grad_down, total, rows_flip, grads_flip):
    step = pl.program_id(0)
    @pl.when(step == 0)
    def _():
        rows_flip[...] = rows[...].T
        grads_flip[...] = grads[...].T
    pre = hidden_pre[...]
    square = pre * pre
    bend = jnp.tanh(ROOT * (pre + CUBE * (square * pre)))
    half = 0.5 * (1.0 + bend)
    hidden = (pre * half).astype(BF16)
    slope = half + (0.5 * ROOT) * pre * (1.0 - bend * bend) * (1.0 + (3.0 * CUBE) * square)
    grad_hidden = dot_last(grads[...], down[...])
    grad_pre = (grad_hidden * slope).astype(BF16)
    grad_down[...] = dot_plain(grads_flip[...], hidden).astype(BF16)
    grad_up[...] = dot_plain(rows_flip[...], grad_pre).astype(BF16)
    part = dot_last(grad_pre, up[...])
    @pl.when(step == 0)
    def _():
        total[...] = part
    @pl.when(step > 0)
    def _():
        total[...] += part
    @pl.when(step == pl.num_programs(0) - 1)
    def _():
        rows_grad[...] = total[...].astype(BF16)

def expert_forward(rows, up, down):
    n, width = rows.shape
    units = up.shape[1]
    return pl.pallas_call(expert_forward_kernel, grid=(units // UNITS,),
        in_specs=[pl.BlockSpec((n, width), lambda i: (0, 0)), pl.BlockSpec((width, UNITS), lambda i: (0, i)), pl.BlockSpec((UNITS, width), lambda i: (i, 0))],
        out_specs=(pl.BlockSpec((n, width), lambda i: (0, 0)), pl.BlockSpec((n, UNITS), lambda i: (0, i))),
        out_shape=(jax.ShapeDtypeStruct((n, width), BF16), jax.ShapeDtypeStruct((n, units), F32)),
        scratch_shapes=[pltpu.VMEM((n, width), F32)],
        compiler_params=pltpu.CompilerParams(vmem_limit_bytes=56 * 2**20),
    )(rows, up, down)

def expert_backward(rows, grads, pre, up, down):
    n, width = rows.shape
    units = up.shape[1]
    whole = pl.BlockSpec((n, width), lambda i: (0, 0))
    return pl.pallas_call(expert_backward_kernel, grid=(units // UNITS,),
        in_specs=[whole, whole, pl.BlockSpec((n, UNITS), lambda i: (0, i)), pl.BlockSpec((width, UNITS), lambda i: (0, i)), pl.BlockSpec((UNITS, width), lambda i: (i, 0))],
        out_specs=(whole, pl.BlockSpec((width, UNITS), lambda i: (0, i)), pl.BlockSpec((width, UNITS), lambda i: (0, i))),
        out_shape=(jax.ShapeDtypeStruct((n, width), BF16), jax.ShapeDtypeStruct((width, units), BF16), jax.ShapeDtypeStruct((width, units), BF16)),
        scratch_shapes=[pltpu.VMEM((n, width), F32), pltpu.VMEM((width, n), BF16), pltpu.VMEM((width, n), BF16)],
        compiler_params=pltpu.CompilerParams(vmem_limit_bytes=60 * 2**20),
    )(rows, grads, pre, up, down)


def slot_dispatch(chosen, priority, first, expert_count, capacity):
    tokens = chosen.shape[0]
    expert_range = jnp.arange(expert_count)
    chosen_hot = chosen[:, None] == expert_range[None, :]
    order_hot = (priority[:, None] == jnp.arange(tokens)[None, :]).astype(BF16)
    sorted_hot = jnp.dot(order_hot, chosen_hot.astype(BF16), preferred_element_type=F32)
    places = jnp.arange(tokens)
    before = (places[:, None] > places[None, :]).astype(BF16)
    earlier = jnp.dot(before, sorted_hot.astype(BF16), preferred_element_type=F32)
    sorted_rank = jnp.minimum(jnp.sum(earlier * sorted_hot, axis=1), capacity)
    rank = jnp.einsum(
        "it,i->t", order_hot, sorted_rank.astype(BF16), preferred_element_type=F32
    ).astype(jnp.int32)
    place = jnp.where(rank < capacity, (chosen ^ first) * capacity + rank, -1)
    dispatch = place[:, None] == jnp.arange(expert_count * capacity)[None, :]
    return (chosen_hot, dispatch.astype(BF16))


def shards(
    tokens,
    cotangent,
    gains,
    qkv_weight,
    proj_weight,
    router_weight,
    expert_up,
    expert_down,
    expert_ids,
    slot_order,
    segment_ids,
):
    dp_count, ctx_count, tp_count = (lax.axis_size(name) for name in ("dp", "ctx", "tp"))
    dp_index, ctx_index, tp_index = (lax.axis_index(name) for name in ("dp", "ctx", "tp"))
    group = dp_count * tp_count
    group_index = dp_index * tp_count + tp_index
    tok_dev, width = tokens.shape
    expert_count = router_weight.shape[1]
    capacity = 5 * tok_dev // (4 * expert_count)
    prompt_rows = PLEN // ctx_count
    conts_here = segment_ids.shape[0]
    prompts_here = conts_here * ctx_count // CONTS
    head_rows = prompts_here * prompt_rows
    local_width = qkv_weight.shape[2]
    shard_rows = qkv_weight.shape[1]
    tp_order = [2, 1]

    full_up = lax.all_gather(expert_up, "ctx", axis=2, tiled=True)[0]

    def gather_weights(part):
        by_ctx = in_order(xor_gather(part, "ctx", ctx_count), ctx_index)
        by_dp = in_order(xor_gather(by_ctx, "dp", dp_count), dp_index)
        return by_dp.reshape(dp_count * ctx_count * part.shape[0], part.shape[1])

    full_qkv = gather_weights(qkv_weight.transpose(1, 0, 2).reshape(shard_rows, 3 * local_width))
    proj_router = gather_weights(jnp.concatenate([proj_weight.T, router_weight], axis=1))
    full_router = proj_router[:, local_width:]
    proj_near = jnp.concatenate(
        xor_gather(proj_router[:, :local_width], "tp", tp_count, tp_order), axis=1
    )

    block_rows = in_order(xor_gather(tokens, "tp", tp_count, tp_order), tp_index).reshape(-1, width)
    unit_block, _ = rms_unit(block_rows.astype(F32))
    normed_one = (gains[0] * unit_block).astype(BF16)
    query_weight, pair_weight = full_qkv[:, :local_width], full_qkv[:, local_width:]
    query = (
        jnp.einsum("dc,rd->cr", query_weight, normed_one, preferred_element_type=F32) * 0.125
    ).astype(BF16)
    local = jnp.dot(normed_one, pair_weight, preferred_element_type=F32).astype(BF16)
    ring = [local[:head_rows].reshape(prompts_here, prompt_rows, 2 * local_width)]
    for _ in range(ctx_count - 1):
        ring.append(ring_step(ring[-1], "ctx", ctx_count, 1))
    remote = ring[1:]
    scalars = ctx_index.astype(jnp.int32).reshape(1)
    attended, lse_prompt, lse_cont = attend_forward(scalars, segment_ids, query, local, remote)
    down_after, _ = lax.optimization_barrier((expert_down, remote[-1]))
    full_down = lax.all_gather(down_after, "ctx", axis=1, tiled=True)[0]

    def row_block(columns, k):
        return lax.dynamic_slice_in_dim(columns, (tp_index ^ k) * tok_dev, tok_dev, 1)

    attended_near = jnp.concatenate(
        xor_exchange([row_block(attended, k) for k in range(tp_count)], "tp", tp_count), axis=0
    )
    branch = jnp.einsum("cr,dc->rd", attended_near, proj_near, preferred_element_type=F32)
    tokens_wide = tokens.astype(F32)
    middle = tokens_wide + branch
    unit_two, factor_two = rms_unit(middle)
    normed_two = (gains[1] * unit_two).astype(BF16)
    logits = jnp.dot(normed_two, full_router, preferred_element_type=F32)
    router_probs = jax.nn.softmax(logits, axis=-1)
    chosen_hot, dispatch = slot_dispatch(
        expert_ids[:, 0], slot_order[0], group_index, expert_count, capacity
    )
    gate_value = jnp.sum(jnp.where(chosen_hot, router_probs, 0.0), axis=-1)

    def to_slots(rows):
        return jnp.einsum("tj,td->jd", dispatch, rows, preferred_element_type=F32).astype(BF16)

    def from_slots(rows):
        return jnp.dot(dispatch, rows, preferred_element_type=F32)

    def exchange_slots(rows):
        pieces = rows.reshape(group, -1, width)
        moved = xor_exchange([pieces[k] for k in range(group)], ("dp", "tp"), group)
        return jnp.concatenate(moved, axis=0)

    upstream = cotangent.astype(F32)
    weighted = (gate_value[:, None] * upstream).astype(BF16)
    arrived = exchange_slots(to_slots(normed_two))
    grad_arrived = exchange_slots(to_slots(weighted))
    produced, hidden_pre = expert_forward(arrived, full_up, full_down)
    rows_grad, up_part, down_part = expert_backward(
        arrived, grad_arrived, hidden_pre, full_up, full_down
    )
    routed_rows = from_slots(exchange_slots(produced))
    grad_returned = from_slots(exchange_slots(rows_grad))
    grad_up = lax.psum_scatter(up_part, "ctx", scatter_dimension=1, tiled=True).astype(F32)[None]

    output = (middle + gate_value[:, None] * routed_rows).astype(BF16)
    grad_gate = jnp.sum(upstream * routed_rows, axis=-1)
    grad_logits = (
        (grad_gate * gate_value)[:, None] * (chosen_hot.astype(F32) - router_probs)
    ).astype(BF16)
    router_part = jnp.einsum("td,te->de", normed_two, grad_logits, preferred_element_type=F32)
    grad_second = grad_returned + jnp.einsum(
        "te,de->td", grad_logits, full_router, preferred_element_type=F32
    )
    middle_part, gain_two = rms_backward(grad_second, unit_two, factor_two, gains[1])
    grad_middle = upstream + middle_part
    grad_low = grad_middle.astype(BF16)
    grad_near = jnp.einsum("dc,rd->cr", proj_near, grad_low, preferred_element_type=F32)
    grad_near = grad_near.astype(BF16).reshape(tp_count, local_width, tok_dev)
    grad_rows = xor_exchange([grad_near[k] for k in range(tp_count)], "tp", tp_count)
    grad_rows = jnp.stack(grad_rows)
    grad_attended = jnp.concatenate(
        [pick(grad_rows, tp_index ^ place) for place in range(tp_count)], axis=1
    )
    grad_query, grad_local, *grad_remote = attend_backward(
        scalars, segment_ids, query, grad_attended, lse_prompt, lse_cont, local, remote
    )
    running = grad_remote[-1]
    own_pair = grad_local[:head_rows].reshape(running.shape)
    for before in ([own_pair] + grad_remote[:-1])[::-1]:
        arriving = ring_step(running, "ctx", ctx_count, -1)
        running = (before.astype(F32) + arriving.astype(F32)).astype(BF16)
    down_part, _ = lax.optimization_barrier((down_part, running))
    grad_down = lax.psum_scatter(down_part, "ctx", scatter_dimension=1, tiled=True)
    grad_down = grad_down.T.astype(F32)[None]
    grad_pair = jnp.concatenate(
        [running.reshape(head_rows, 2 * local_width), grad_local[head_rows:]], axis=0
    )
    qkv_part = jnp.concatenate(
        [
            jnp.einsum("rd,cr->dc", normed_one, grad_query, preferred_element_type=F32),
            jnp.einsum("rd,rc->dc", normed_one, grad_pair, preferred_element_type=F32),
        ],
        axis=1,
    )
    pair_blocks = grad_pair.reshape(tp_count, tok_dev, 2 * local_width)
    first_near = [
        jnp.einsum(
            "cr,dc->rd", row_block(grad_query, k), query_weight, preferred_element_type=F32
        )
        + jnp.einsum(
            "rc,dc->rd", pick(pair_blocks, tp_index ^ k), pair_weight, preferred_element_type=F32
        )
        for k in range(tp_count)
    ]

    def scatter_near(pieces, order):
        pieces = dict(enumerate(pieces))
        for mask in order:
            sent = [key for key in sorted(pieces) if key & mask]
            moved = xor_swap(
                jnp.stack([pieces[key].astype(BF16) for key in sent]), "tp", tp_count, mask
            )
            for place, key in enumerate(sent):
                pieces[key ^ mask] = pieces[key ^ mask] + moved[place].astype(F32)
                del pieces[key]
        return pieces[0]

    scatter_order = tp_order[::-1]
    grad_first = scatter_near(first_near, scatter_order)
    unit_one, factor_one = rms_unit(tokens_wide)
    rows_part, gain_one = rms_backward(grad_first, unit_one, factor_one, gains[0])
    grad_tokens = rows_part + grad_middle

    proj_blocks = jnp.einsum("cr,rd->dc", attended_near, grad_low, preferred_element_type=F32)
    proj_part = scatter_near(
        [proj_blocks[:, k * local_width : (k + 1) * local_width] for k in range(tp_count)],
        scatter_order,
    )
    small_part = jnp.concatenate(
        [router_part, jnp.stack([gain_one, gain_two], axis=1)], axis=1
    )
    packed = jnp.concatenate([qkv_part, proj_part, small_part], axis=1)
    packed = packed.reshape(dp_count, ctx_count, shard_rows, -1).astype(BF16)

    def scatter_ordered(values, axis, size, me):
        moved = xor_exchange([pick(values, me ^ k) for k in range(size)], axis, size)
        return sum(piece.astype(F32) for piece in moved)

    summed = scatter_ordered(packed, "dp", dp_count, dp_index).astype(BF16)
    summed = scatter_ordered(summed, "ctx", ctx_count, ctx_index)
    small_sum = summed[:, 4 * local_width :]
    small_all = xor_exchange([small_sum.astype(BF16)] * tp_count, "tp", tp_count)
    small_sum = small_sum + sum(piece.astype(F32) for piece in small_all[1:])
    grad_qkv = summed[:, : 3 * local_width].reshape(shard_rows, 3, local_width).transpose(1, 0, 2)
    grad_proj = summed[:, 3 * local_width : 4 * local_width].T
    grad_router = small_sum[:, :expert_count]
    grad_gains = small_sum[:, expert_count:].T
    return (output, grad_tokens, grad_gains, grad_qkv, grad_proj, grad_router, grad_up, grad_down)


def solution(mesh):
    in_specs = (
        P(("dp", "ctx", "tp"), None),
        P(("dp", "ctx", "tp"), None),
        P(),
        P(None, ("dp", "ctx"), "tp"),
        P("tp", ("dp", "ctx")),
        P(("dp", "ctx"), None),
        P(("dp", "tp"), None, "ctx"),
        P(("dp", "tp"), "ctx", None),
        P(("dp", "ctx", "tp"), None),
        P(("dp", "ctx", "tp"), None),
        P(("dp", "ctx")),
    )
    out_specs = (
        P(("dp", "ctx", "tp"), None),
        P(("dp", "ctx", "tp"), None),
        P(None, ("dp", "ctx")),
        P(None, ("dp", "ctx"), "tp"),
        P("tp", ("dp", "ctx")),
        P(("dp", "ctx"), None),
        P(("dp", "tp"), None, "ctx"),
        P(("dp", "tp"), "ctx", None),
    )
    return jax.shard_map(shards, mesh=mesh, in_specs=in_specs, out_specs=out_specs, check_vma=False)
```

```python
import functools

import jax
import jax.numpy as jnp
from jax import lax
from jax.experimental import pallas as pl
from jax.experimental.pallas import tpu as pltpu
from jax.sharding import PartitionSpec as P

HD = 64
PLEN = 1024
CLEN = 128
CONTS = 8
CHUNK = 128
UNITS = 768

EPSILON = 1e-06
NEGATIVE = -1e30
ROOT = 0.7978845608028654
CUBE = 0.044715
F32 = jnp.float32
BF16 = jnp.bfloat16
VM = pl.BlockSpec(memory_space=pltpu.VMEM)
SM = pl.BlockSpec(memory_space=pltpu.SMEM)
ROOM = pltpu.CompilerParams(vmem_limit_bytes=60 * 2**20)


def shape(dims, dtype=BF16):
    return jax.ShapeDtypeStruct(dims, dtype)


def low(value):
    return value.astype(BF16)


def dot_last(left, right):
    return lax.dot_general(left, right, (((1,), (1,)), ((), ())), preferred_element_type=F32)


def dot_plain(left, right):
    return lax.dot_general(left, right, (((1,), (0,)), ((), ())), preferred_element_type=F32)


def add_all(parts):
    return functools.reduce(jnp.add, parts)


def xor_swap(value, axis, size, mask):
    return lax.ppermute(value, axis, [(place, place ^ mask) for place in range(size)])


def ring_step(value, axis, size, shift):
    return lax.ppermute(value, axis, [(place, (place + shift) % size) for place in range(size)])


def pick(stacked, index):
    return lax.dynamic_index_in_dim(stacked, index, 0, keepdims=False)


def xor_gather(value, axis, size, order=None):
    if order is None:
        order = [1 << bit for bit in range(size.bit_length() - 1)]
    have = {0: value}
    for mask in order:
        keys = sorted(have)
        moved = xor_swap(jnp.stack([have[key] for key in keys]), axis, size, mask)
        for place, key in enumerate(keys):
            have[key ^ mask] = moved[place]
    return [have[key] for key in range(size)]


def xor_exchange(pieces, axis, size):
    return [pieces[0]] + [xor_swap(pieces[mask], axis, size, mask) for mask in range(1, size)]


def chunk_list(value, axis):
    return [
        lax.slice_in_dim(value, first, first + CHUNK, axis=axis)
        for first in range(0, value.shape[axis], CHUNK)
    ]


def split_order(value, axis=0):
    parts = chunk_list(value, axis)
    return jnp.concatenate(parts[0::2] + parts[1::2], axis=axis)


def plain_order(value, axis=0):
    parts = chunk_list(value, axis)
    half = len(parts) // 2
    return jnp.concatenate([parts[(at % 2) * half + at // 2] for at in range(2 * half)], axis=axis)


def rms_unit(values):
    factor = lax.rsqrt(jnp.mean(values * values, axis=-1, keepdims=True) + EPSILON)
    return (values * factor, factor)


def rms_backward(grad_normed, unit_part, factor, gain):
    scaled = grad_normed * gain
    inner = jnp.mean(scaled * unit_part, axis=-1, keepdims=True)
    return factor * (scaled - unit_part * inner)


def normalize_kernel(tokens, gains, own, second):
    unit, _ = rms_unit(tokens[...].astype(F32))
    own[...] = split_order(low(gains[0:1, :] * unit))
    second[...] = own[own.shape[0] // 2 :, :]


def normalize(tokens, gains):
    rows, width = tokens.shape
    return pl.pallas_call(
        normalize_kernel,
        out_shape=(shape((rows, width)), shape((rows // 2, width))),
        in_specs=[VM] * 2,
        out_specs=(VM,) * 2,
        compiler_params=ROOM,
        name="normalize",
    )(tokens, gains)


def key_lanes(rows, width):
    return rows[:, : width + (-width) % 128]


def value_lanes(rows, width):
    return rows[:, width - (-width) % 128 :]


def spread_heads(columns, ahead, behind):
    width, count = columns.shape
    groups = []
    for first in range(0, width, HD):
        pieces = [columns[first : first + HD]]
        above, below = ahead + first, width - first - HD + behind
        if above:
            pieces.insert(0, jnp.zeros((above, count), columns.dtype))
        if below:
            pieces.append(jnp.zeros((below, count), columns.dtype))
        groups.append(jnp.concatenate(pieces, axis=0))
    return jnp.concatenate(groups, axis=1)


def causal(scores, count):
    key_row = lax.broadcasted_iota(jnp.int32, scores.shape, 0)
    query_row = lax.broadcasted_iota(jnp.int32, scores.shape, 1) % count
    return jnp.where(key_row <= query_row, scores, NEGATIVE)


def work_items(info, sizes, attend):
    prompts, conts, places, per = sizes
    ctx_index = info[0]

    def prompt_chunks(prompt):
        return [info[1 + prompt * places * per + at] for at in range(places * per)]

    def prompt_mask(scores):
        count = per * CHUNK
        parts = [causal(scores[:count], count)]
        for place in range(1, places):
            part = scores[place * count : (place + 1) * count]
            parts.append(jnp.where(place <= ctx_index, part, NEGATIVE))
        return jnp.concatenate(parts, axis=0)

    def cont_mask(scores):
        return jnp.concatenate([causal(scores[:CLEN], CLEN), scores[CLEN:]], axis=0)

    @pl.loop(0, prompts)
    def _(prompt):
        chunks = prompt_chunks(prompt)
        attend(0, prompt, chunks[:per], chunks, prompt_mask)

    first = 1 + prompts * places * per

    @pl.loop(0, conts)
    def _(cont):
        own = info[first + cont]
        attend(1, cont, [own], [own] + prompt_chunks(info[first + conts + cont]), cont_mask)


def chunk_lanes(chunk):
    return pl.ds(pl.multiple_of(chunk * CHUNK, CHUNK), CHUNK)


def load_lanes(ref, chunks):
    return jnp.concatenate([ref[:, chunk_lanes(chunk)] for chunk in chunks], axis=1)


def attend_forward_kernel(sizes, inputs, info, query_weight, pair_weight, *rest):
    rows, (query, pairs, *outs, lse_prompt, lse_cont, mixed) = rest[:inputs], rest[inputs:]
    lse = (lse_prompt, lse_cont)
    width = query.shape[0]
    pad = (-width) % 128
    query_flip = query_weight[...].T
    at = 0
    for one in rows:
        value = one[...]
        count = value.shape[0]
        pair = low(dot_plain(value, pair_weight[...]))
        pairs[at // CHUNK : (at + count) // CHUNK] = pair.reshape(-1, CHUNK, 2 * width)
        if at < query.shape[1]:
            query[:, at : at + count] = low(dot_last(query_flip, value) * 0.125)
        at += count

    def attend(kind, index, own, chunks, mask):
        count = len(own) * CHUNK
        block = jnp.concatenate([pairs[chunk] for chunk in chunks], axis=0)
        spread = spread_heads(load_lanes(query, own), 0, pad)
        scores = mask(dot_plain(key_lanes(block, width), spread))
        peak = jnp.max(scores, axis=0, keepdims=True)
        shifted = jnp.exp(scores - peak)
        total = jnp.sum(shifted, axis=0, keepdims=True)
        weights = low(shifted)
        flip = value_lanes(block, width).T
        for head in range(width // HD):
            group = slice(head * count, (head + 1) * count)
            part = slice(pad + head * HD, pad + (head + 1) * HD)
            result = low(dot_plain(flip[part], weights[:, group]) / total[:, group])
            for place, chunk in enumerate(own):
                mixed[head * HD : (head + 1) * HD, chunk_lanes(chunk)] = result[
                    :, place * CHUNK : (place + 1) * CHUNK
                ]
        lse[kind][index] = peak + jnp.log(total)

    work_items(info, sizes, attend)
    each = outs[0].shape[1]
    for place, out in enumerate(outs):
        out[...] = mixed[:, place * each : (place + 1) * each]


def attend_backward_kernel(sizes, info, query, lse_prompt, lse_cont, pairs, *rest):
    *grads, grad_query, grad_pairs, grad, sums = rest
    lse = (lse_prompt, lse_cont)
    width = query.shape[0]
    pad = (-width) % 128
    each = grads[0].shape[1]
    for place, one in enumerate(grads):
        grad[:, place * each : (place + 1) * each] = one[...]

    def attend(kind, index, own, chunks, mask):
        count = len(own) * CHUNK
        block = jnp.concatenate([pairs[chunk] for chunk in chunks], axis=0)
        query_spread = spread_heads(load_lanes(query, own), 0, pad)
        grad_spread = spread_heads(load_lanes(grad, own), pad, 0)
        keys = key_lanes(block, width)
        weights = jnp.exp(mask(dot_plain(keys, query_spread)) - lse[kind][index])
        slopes = dot_plain(value_lanes(block, width), grad_spread)
        centre = jnp.sum(weights * slopes, axis=0, keepdims=True)
        grad_scores = low(weights * (slopes - centre))
        flip = keys.T
        for head in range(width // HD):
            group = slice(head * count, (head + 1) * count)
            part = slice(head * HD, (head + 1) * HD)
            result = low(dot_plain(flip[part], grad_scores[:, group]) * 0.125)
            for place, chunk in enumerate(own):
                grad_query[part, chunk_lanes(chunk)] = result[
                    :, place * CHUNK : (place + 1) * CHUNK
                ]
        key_part = dot_last(grad_scores, query_spread)
        value_part = dot_last(low(weights), grad_spread)
        if pad:
            edge = width - pad
            shared = key_part[:, edge:] + value_part[:, : 2 * pad]
            joined = [key_part[:, :edge], shared, value_part[:, 2 * pad :]]
        else:
            joined = [key_part, value_part]
        result = jnp.concatenate(joined, axis=1)
        for place, chunk in enumerate(chunks):
            part = result[place * CHUNK : (place + 1) * CHUNK]
            if kind == 0 or place == 0:
                sums[chunk] = part
            else:
                sums[chunk] += part

    work_items(info, sizes, attend)

    @pl.loop(0, pairs.shape[0], unroll=4)
    def _(chunk):
        grad_pairs[chunk] = low(sums[chunk])


def attend_cost(factor, sizes, heads):
    prompts, conts, places, per = sizes
    scores = heads * places * per * CHUNK * CHUNK * (prompts * per + conts)
    return pl.CostEstimate(flops=factor * HD * scores, bytes_accessed=10**7, transcendentals=scores)


def attend_forward(sizes, info, query_weight, pair_weight, rows, local_rows):
    prompts, conts, places, per = sizes
    width = query_weight.shape[1]
    heads = width // HD
    count = sum(one.shape[0] for one in rows)
    each = local_rows // 4
    return pl.pallas_call(
        functools.partial(attend_forward_kernel, sizes, len(rows)),
        out_shape=(
            shape((width, local_rows)),
            shape((count // CHUNK, CHUNK, 2 * width)),
            *([shape((width, each))] * 4),
            shape((prompts, 1, heads * per * CHUNK), F32),
            shape((conts, 1, heads * CLEN), F32),
        ),
        in_specs=[SM] + [VM] * (2 + len(rows)),
        out_specs=(VM,) * 8,
        scratch_shapes=[pltpu.VMEM((width, local_rows), BF16)],
        compiler_params=ROOM,
        cost_estimate=attend_cost(20, sizes, heads),
        name="attend_forward",
    )(info, query_weight, pair_weight, *rows)


def attend_backward(sizes, info, query, lse_prompt, lse_cont, pairs, grads):
    return pl.pallas_call(
        functools.partial(attend_backward_kernel, sizes),
        out_shape=(shape(query.shape), shape(pairs.shape)),
        in_specs=[SM] + [VM] * (4 + len(grads)),
        out_specs=(VM,) * 2,
        scratch_shapes=[pltpu.VMEM(query.shape, BF16), pltpu.VMEM(pairs.shape, F32)],
        compiler_params=ROOM,
        cost_estimate=attend_cost(40, sizes, query.shape[0] // HD),
        name="attend_backward",
    )(info, query, lse_prompt, lse_cont, pairs, *grads)


def rows_remote_kernel(grad_pairs, pair_weight, keep, send):
    half = grad_pairs.shape[0] // 2
    wide = grad_pairs.shape[2]
    keep[0] = dot_last(grad_pairs[:half].reshape(half * CHUNK, wide), pair_weight[...])
    send[0] = low(dot_last(grad_pairs[half:].reshape(half * CHUNK, wide), pair_weight[...]))


def rows_local_kernel(grad_pairs, grad_query, query_weight, pair_weight, keep, send):
    half = grad_pairs.shape[0] // 2
    wide = grad_pairs.shape[2]
    each = half * CHUNK
    query_rows = grad_query[...].T
    rows = dot_last(grad_pairs[...].reshape(2 * each, wide), pair_weight[...])
    rows = rows + dot_last(query_rows, query_weight[...])
    keep[0] = rows[:each]
    send[0] = low(rows[each:])


def rows_remote(grad_pairs, pair_weight, places, each):
    width = pair_weight.shape[0]
    chunks = 2 * each // CHUNK
    count = places - 1
    return pl.pallas_call(
        rows_remote_kernel,
        grid=(count,),
        in_specs=[
            pl.BlockSpec((chunks,) + grad_pairs.shape[1:], lambda at: (1 + count - at, 0, 0)),
            pl.BlockSpec(pair_weight.shape, lambda at: (0, 0)),
        ],
        out_specs=(
            pl.BlockSpec((1, each, width), lambda at: (at, 0, 0)),
            pl.BlockSpec((1, each, width), lambda at: (at, 0, 0)),
        ),
        out_shape=(shape((count, each, width), F32), shape((count, each, width))),
        compiler_params=ROOM,
        name="rows_remote",
    )(grad_pairs, pair_weight)


def rows_local(grad_pairs, grad_query, query_weight, pair_weight, each):
    width = pair_weight.shape[0]
    chunks = 2 * each // CHUNK
    return pl.pallas_call(
        rows_local_kernel,
        grid=(2,),
        in_specs=[
            pl.BlockSpec((chunks,) + grad_pairs.shape[1:], lambda at: (1 - at, 0, 0)),
            pl.BlockSpec((grad_query.shape[0], 2 * each), lambda at: (0, 1 - at)),
            pl.BlockSpec(query_weight.shape, lambda at: (0, 0)),
            pl.BlockSpec(pair_weight.shape, lambda at: (0, 0)),
        ],
        out_specs=(
            pl.BlockSpec((1, each, width), lambda at: (at, 0, 0)),
            pl.BlockSpec((1, each, width), lambda at: (at, 0, 0)),
        ),
        out_shape=(shape((2, each, width), F32), shape((2, each, width))),
        compiler_params=ROOM,
        name="rows_local",
    )(grad_pairs, grad_query, query_weight, pair_weight)


def qkv_grad_kernel(grad_query, grad_pairs, *rest):
    *rows, out = rest
    width, local_rows = grad_query.shape
    total_query = total_pair = None
    at = 0
    for one in rows:
        value = one[...]
        count = value.shape[0]
        chunks = slice(at // CHUNK, (at + count) // CHUNK)
        part = dot_plain(grad_pairs[chunks].reshape(count, 2 * width).T, value)
        total_pair = part if total_pair is None else total_pair + part
        if at < local_rows:
            part = dot_plain(grad_query[:, at : at + count], value)
            total_query = part if total_query is None else total_query + part
        at += count
    out[...] = low(jnp.concatenate([total_query, total_pair], axis=0).T)


def qkv_grad(grad_query, grad_pairs, rows):
    width = rows[0].shape[1]
    return pl.pallas_call(
        qkv_grad_kernel,
        out_shape=shape((width, 3 * grad_query.shape[0])),
        in_specs=[VM] * (2 + len(rows)),
        out_specs=VM,
        compiler_params=ROOM,
        name="qkv_grad",
    )(grad_query, grad_pairs, *rows)


def final_kernel(first, tokens, gains, grad_middle, kept, beside, across, own, far, out):
    unit, factor = rms_unit(tokens[...].astype(F32))
    rows = kept[0] + beside[0].astype(F32) + across[...].astype(F32)
    ring = jnp.concatenate([own[...], far[...]], axis=0).astype(F32)
    rows = plain_order(rows + jnp.where(first[0] == 0, ring, 0.0))
    out[...] = rms_backward(rows, unit, factor, gains[0:1, :]) + grad_middle[...]


def final_rows(side, tokens, gains, grad_middle, kept, beside, across, own, far):
    rows, width = tokens.shape
    last = pl.BlockSpec((1, rows, width), lambda at: (1, 0, 0))
    half = pl.BlockSpec((rows // 2, width), lambda at: (0, 0))
    whole = pl.BlockSpec((rows, width), lambda at: (0, 0))
    return pl.pallas_call(
        final_kernel,
        grid=(1,),
        in_specs=[
            SM,
            whole,
            pl.BlockSpec(gains.shape, lambda at: (0, 0)),
            whole,
            last,
            last,
            whole,
            half,
            half,
        ],
        out_specs=whole,
        out_shape=shape((rows, width), F32),
        compiler_params=ROOM,
        name="final_rows",
    )(side, tokens, gains, grad_middle, kept, beside, across, own, far)


def slot_places(chosen, priority, first, expert_count, capacity):
    tokens = chosen.shape[0]
    expert_range = jnp.arange(expert_count)
    chosen_hot = low(chosen[:, None] == expert_range[None, :])
    order_hot = low(priority[:, None] == jnp.arange(tokens)[None, :])
    sorted_hot = jnp.dot(order_hot, chosen_hot, preferred_element_type=F32)
    places = jnp.arange(tokens)
    before = low(places[:, None] > places[None, :])
    earlier = jnp.dot(before, low(sorted_hot), preferred_element_type=F32)
    sorted_rank = jnp.minimum(jnp.sum(earlier * sorted_hot, axis=1), capacity)
    rank = jnp.einsum("it,i->t", order_hot, low(sorted_rank), preferred_element_type=F32)
    rank = rank.astype(jnp.int32)
    near = chosen ^ first
    block = (near >> 1) + (near & 1) * (expert_count // 2)
    return jnp.where(rank < capacity, block * capacity + rank, -1)


def softmax_rows(logits):
    shifted = jnp.exp(logits - jnp.max(logits, axis=-1, keepdims=True))
    return shifted / jnp.sum(shifted, axis=-1, keepdims=True)


def one_hot_experts(ids, expert_count):
    return ids == lax.broadcasted_iota(jnp.int32, (ids.shape[0], expert_count), 1)


def middle_kernel(
    parts, tokens, cotangent, gains, router, ids, place_row, *rest
):
    attended, proj = rest[:parts], rest[parts : 2 * parts]
    even_rows, odd_rows, even_grads, odd_grads, middle, normed, probs = rest[2 * parts :]
    mixed = plain_order(jnp.concatenate([one[...] for one in attended], axis=0), 1)
    branch = dot_plain(mixed.T, jnp.concatenate([one[...] for one in proj], axis=0))
    total = tokens[...].astype(F32) + branch
    middle[...] = total
    unit, _ = rms_unit(total)
    normed_rows = low(gains[1:2, :] * unit)
    normed[...] = normed_rows
    chances = softmax_rows(dot_plain(normed_rows, router[...]))
    probs[...] = chances
    hot = one_hot_experts(ids[...], chances.shape[1])
    gate = jnp.sum(jnp.where(hot, chances, 0.0), axis=1, keepdims=True)
    weighted = low(gate * cotangent[...].astype(F32))
    half = even_rows.shape[0]
    for at, (row_slots, grad_slots) in enumerate(((even_rows, even_grads), (odd_rows, odd_grads))):
        slots = at * half + lax.broadcasted_iota(jnp.int32, (half, tokens.shape[0]), 0)
        dispatch = low(slots == place_row[...])
        row_slots[...] = low(dot_plain(dispatch, normed_rows))
        grad_slots[...] = low(dot_plain(dispatch, weighted))


def middle_rows(tokens, cotangent, gains, router, ids, place, slots, attended, proj):
    rows, width = tokens.shape
    half = shape((slots // 2, width))
    return pl.pallas_call(
        functools.partial(middle_kernel, len(attended)),
        out_shape=(
            half,
            half,
            half,
            half,
            shape((rows, width), F32),
            shape((rows, width)),
            shape((rows, router.shape[1]), F32),
        ),
        in_specs=[VM] * (6 + 2 * len(attended)),
        out_specs=(VM,) * 7,
        compiler_params=ROOM,
        name="middle_rows",
    )(tokens, cotangent, gains, router, ids, place[None, :], *attended, *proj)


def gather_slots(refs, capacity):
    own, beside, *pairs = refs
    even = [own[0:capacity, :]] + [pair[0:capacity, :] for pair in pairs]
    odd = [beside[0:capacity, :]] + [pair[capacity:, :] for pair in pairs]
    return jnp.concatenate(even + odd, axis=0)


def combine_kernel(
    parts, moved, capacity, *refs
):
    tokens_in, rest = refs[:8], refs[8:]
    cotangent, gains, router, ids, place_column, middle, normed, probs = tokens_in
    attended, proj, rest = rest[:parts], rest[parts : 2 * parts], rest[2 * parts :]
    row_refs, grad_refs, rest = rest[:moved], rest[moved : 2 * moved], rest[2 * moved :]
    output, grad_middle, *near, proj_keep, proj_send, small = rest
    rows, expert_count = probs.shape
    slots = 2 * (moved - 1) * capacity
    slot_range = lax.broadcasted_iota(jnp.int32, (rows, slots), 1)
    dispatch = low(slot_range == place_column[...])
    routed = dot_plain(dispatch, gather_slots(row_refs, capacity))
    returned = dot_plain(dispatch, gather_slots(grad_refs, capacity))
    chances = probs[...]
    hot = one_hot_experts(ids[...], expert_count)
    gate = jnp.sum(jnp.where(hot, chances, 0.0), axis=1, keepdims=True)
    total = middle[...]
    output[...] = low(total + gate * routed)
    upstream = cotangent[...].astype(F32)
    grad_gate = jnp.sum(upstream * routed, axis=1, keepdims=True)
    grad_logits = low((grad_gate * gate) * (hot.astype(F32) - chances))
    grad_second = returned + dot_last(grad_logits, router[...])
    unit, factor = rms_unit(total)
    gain_two = jnp.sum(grad_second * unit, axis=0, keepdims=True)
    grad_rows = upstream + rms_backward(grad_second, unit, factor, gains[1:2, :])
    grad_middle[...] = grad_rows
    grad_low = split_order(low(grad_rows))
    for place in range(parts):
        near[place][...] = low(dot_last(proj[place][...], grad_low))
        part = dot_plain(attended[place][...], grad_low)
        if place % 2:
            proj_send[place // 2] = low(part)
        else:
            proj_keep[place // 2] = part
    small[0:expert_count, :] = dot_plain(grad_logits.T, normed[...])
    small[expert_count:, :] = jnp.broadcast_to(gain_two, (small.shape[0] - expert_count, rows))


def combine_rows(
    cotangent, gains, router, ids, place, middle, normed, probs, attended, proj, row_slots, grad_slots
):
    rows, width = middle.shape
    capacity = 5 * rows // (4 * router.shape[1])
    local_width = proj[0].shape[0]
    parts = len(proj)
    inputs = [cotangent, gains, router, ids, place[:, None], middle, normed, probs]
    inputs += list(attended) + list(proj) + list(row_slots) + list(grad_slots)
    return pl.pallas_call(
        functools.partial(combine_kernel, parts, len(row_slots), capacity),
        out_shape=(
            shape((rows, width)),
            shape((rows, width), F32),
            *([shape((local_width, rows))] * parts),
            shape((parts // 2, local_width, width), F32),
            shape((parts // 2, local_width, width)),
            shape((router.shape[1] + 8, width), F32),
        ),
        in_specs=[VM] * len(inputs),
        out_specs=(VM,) * (5 + parts),
        compiler_params=ROOM,
        name="combine_rows",
    )(*inputs)


def expert_forward_kernel(moved, capacity, *refs):
    parts, (up, down, even, odd, hidden_pre, rows, total) = refs[:moved], refs[moved:]
    step = pl.program_id(0)

    @pl.when(step == 0)
    def _():
        rows[...] = gather_slots(parts, capacity)

    pre = dot_plain(rows[...], up[...])
    hidden_pre[...] = pre
    inner = ROOT * (pre + CUBE * (pre * pre * pre))
    hidden = low(0.5 * pre * (1.0 + jnp.tanh(inner)))
    part = dot_plain(hidden, down[...])

    @pl.when(step == 0)
    def _():
        total[...] = part

    @pl.when(step > 0)
    def _():
        total[...] += part

    @pl.when(step == pl.num_programs(0) - 1)
    def _():
        half = even.shape[0]
        even[...] = low(total[:half])
        odd[...] = low(total[half:])


def expert_backward_kernel(moved, capacity, *refs):
    row_parts, grad_parts, rest = refs[:moved], refs[moved : 2 * moved], refs[2 * moved :]
    hidden_pre, up, down, even, odd, grad_up, grad_down, total, grads, rows_flip, grads_flip = rest
    step = pl.program_id(0)

    @pl.when(step == 0)
    def _():
        arrived = gather_slots(grad_parts, capacity)
        grads[...] = arrived
        grads_flip[...] = arrived.T
        rows_flip[...] = gather_slots(row_parts, capacity).T

    pre = hidden_pre[...]
    square = pre * pre
    bend = jnp.tanh(ROOT * (pre + CUBE * (square * pre)))
    half = 0.5 * (1.0 + bend)
    hidden = low(pre * half)
    slope = half + (0.5 * ROOT) * pre * (1.0 - bend * bend) * (1.0 + (3.0 * CUBE) * square)
    grad_pre = low(dot_last(grads[...], down[...]) * slope)
    grad_down[...] = low(dot_plain(grads_flip[...], hidden))
    grad_up[...] = low(dot_plain(rows_flip[...], grad_pre))
    part = dot_last(grad_pre, up[...])

    @pl.when(step == 0)
    def _():
        total[...] = part

    @pl.when(step > 0)
    def _():
        total[...] += part

    @pl.when(step == pl.num_programs(0) - 1)
    def _():
        count = even.shape[0]
        even[...] = low(total[:count])
        odd[...] = low(total[count:])


def whole_specs(values):
    return [pl.BlockSpec(value.shape, lambda at: (0, 0)) for value in values]


def expert_forward(parts, up, down):
    width, units = up.shape
    half = parts[1].shape[0]
    capacity = half // (len(parts) - 1)
    block = pl.BlockSpec((half, width), lambda at: (0, 0))
    return pl.pallas_call(
        functools.partial(expert_forward_kernel, len(parts), capacity),
        grid=(units // UNITS,),
        in_specs=whole_specs(parts)
        + [
            pl.BlockSpec((width, UNITS), lambda at: (0, at)),
            pl.BlockSpec((UNITS, width), lambda at: (at, 0)),
        ],
        out_specs=(block, block, pl.BlockSpec((2 * half, UNITS), lambda at: (0, at))),
        out_shape=(shape((half, width)), shape((half, width)), shape((2 * half, units), F32)),
        scratch_shapes=[
            pltpu.VMEM((2 * half, width), BF16),
            pltpu.VMEM((2 * half, width), F32),
        ],
        compiler_params=ROOM,
        cost_estimate=pl.CostEstimate(
            flops=8 * half * width * units,
            bytes_accessed=12 * half * units,
            transcendentals=2 * half * units,
        ),
        name="expert_forward",
    )(*parts, up, down)


def expert_backward(row_parts, grad_parts, hidden_pre, up, down):
    width, units = up.shape
    half = row_parts[1].shape[0]
    capacity = half // (len(row_parts) - 1)
    block = pl.BlockSpec((half, width), lambda at: (0, 0))
    return pl.pallas_call(
        functools.partial(expert_backward_kernel, len(row_parts), capacity),
        grid=(units // UNITS,),
        in_specs=whole_specs(row_parts)
        + whole_specs(grad_parts)
        + [
            pl.BlockSpec((2 * half, UNITS), lambda at: (0, at)),
            pl.BlockSpec((width, UNITS), lambda at: (0, at)),
            pl.BlockSpec((UNITS, width), lambda at: (at, 0)),
        ],
        out_specs=(
            block,
            block,
            pl.BlockSpec((width, UNITS), lambda at: (0, at)),
            pl.BlockSpec((width, UNITS), lambda at: (0, at)),
        ),
        out_shape=(
            shape((half, width)),
            shape((half, width)),
            shape((width, units)),
            shape((width, units)),
        ),
        scratch_shapes=[
            pltpu.VMEM((2 * half, width), F32),
            pltpu.VMEM((2 * half, width), BF16),
            pltpu.VMEM((width, 2 * half), BF16),
            pltpu.VMEM((width, 2 * half), BF16),
        ],
        compiler_params=ROOM,
        cost_estimate=pl.CostEstimate(
            flops=16 * half * width * units,
            bytes_accessed=16 * half * units,
            transcendentals=2 * half * units,
        ),
        name="expert_backward",
    )(*row_parts, *grad_parts, hidden_pre, up, down)


def shards(
    tokens,
    cotangent,
    gains,
    qkv_weight,
    proj_weight,
    router_weight,
    expert_up,
    expert_down,
    expert_ids,
    slot_order,
    segment_ids,
):
    dp_count, ctx_count, tp_count = (lax.axis_size(name) for name in ("dp", "ctx", "tp"))
    dp_index, ctx_index, tp_index = (lax.axis_index(name) for name in ("dp", "ctx", "tp"))
    group = dp_count * tp_count
    group_index = dp_index * tp_count + tp_index
    tok_dev, width = tokens.shape
    half_rows = tok_dev // 2
    expert_count = router_weight.shape[1]
    capacity = 5 * tok_dev // (4 * expert_count)
    slots = expert_count * capacity
    per = PLEN // ctx_count // CHUNK
    conts_here = segment_ids.shape[0]
    prompts_here = conts_here * ctx_count // CONTS
    local_width = qkv_weight.shape[2]
    shard_rows = qkv_weight.shape[1]
    side, core = tp_index >> 1, tp_index & 1

    def across(value):
        return xor_swap(value, "tp", tp_count, 2)

    def beside(value):
        return xor_swap(value, "tp", tp_count, 1)

    full_up = lax.all_gather(expert_up, "ctx", axis=2, tiled=True)[0]

    own, own_second = normalize(tokens, gains)
    far_second = across(own_second)
    carried = jnp.where(side == 0, own[:half_rows], far_second)
    far_first = across(own[:half_rows])
    rows = [own, beside(own), far_first, far_second, beside(far_first), beside(far_second)]
    for _ in range(ctx_count - 1):
        carried = ring_step(carried, "ctx", ctx_count, 1)
        other = across(carried)
        rows += [carried, other, beside(carried), beside(other)]
    down_after, _ = lax.optimization_barrier((expert_down, carried))
    full_down = lax.all_gather(down_after, "ctx", axis=1, tiled=True)[0]

    packed = jnp.concatenate(
        [
            qkv_weight.transpose(1, 0, 2).reshape(shard_rows, 3 * local_width),
            proj_weight.T,
            router_weight,
        ],
        axis=1,
    )
    by_ctx = jnp.stack(xor_exchange([packed] * ctx_count, "ctx", ctx_count))
    by_dp = jnp.stack(xor_gather(by_ctx, "dp", dp_count)).reshape((-1,) + packed.shape)
    shard_index = dp_index * ctx_count + ctx_index
    weights = jnp.concatenate(
        [pick(by_dp, shard_index ^ place) for place in range(dp_count * ctx_count)], axis=0
    )
    query_weight = weights[:, :local_width]
    pair_weight = weights[:, local_width : 3 * local_width]
    router = weights[:, 4 * local_width :]
    proj = xor_gather(weights[:, 3 * local_width : 4 * local_width].T, "tp", tp_count, [2, 1])

    device_chunks = tok_dev // CHUNK

    def split_place(at):
        return (at % 2) * (device_chunks // 2) + at // 2

    at = jnp.arange(prompts_here * per)
    owner, inside = at // device_chunks, at % device_chunks
    local_at = (owner ^ tp_index) * device_chunks + split_place(inside)
    remote_at = ((owner ^ core) * 2 + ((inside % 2) ^ side)) * (device_chunks // 2) + inside // 2
    remote_first = (tp_count + 2 * jnp.arange(ctx_count - 1)) * device_chunks
    prompt_at = jnp.concatenate(
        [
            local_at.reshape(prompts_here, 1, per),
            remote_first[None, :, None] + remote_at.reshape(prompts_here, 1, per),
        ],
        axis=1,
    )
    at = jnp.arange(conts_here)
    cont_at = ((2 + at // device_chunks) ^ tp_index) * device_chunks + split_place(
        at % device_chunks
    )
    info = jnp.concatenate([ctx_index[None], prompt_at.reshape(-1), cont_at, segment_ids])
    info = info.astype(jnp.int32)
    sizes = (prompts_here, conts_here, ctx_count, per)

    query, pairs, *attended, lse_prompt, lse_cont = attend_forward(
        sizes, info, query_weight, pair_weight, rows, tp_count * tok_dev
    )
    attended = xor_exchange(attended, "tp", tp_count)
    place = slot_places(expert_ids[:, 0], slot_order[0], group_index, expert_count, capacity)

    def start_exchange(odd):
        return xor_swap(odd, ("dp", "tp"), group, 1)

    def finish_exchange(even, other):
        moved = [even, other]
        for at in range(1, group // 2):
            block = slice(at * capacity, (at + 1) * capacity)
            pair = jnp.concatenate([even[block], other[block]], axis=0)
            moved.append(xor_swap(pair, ("dp", "tp"), group, 2 * at))
        return moved

    even_rows, odd_rows, even_grads, odd_grads, middle, normed_two, probs = middle_rows(
        tokens, cotangent, gains, router, expert_ids, place, slots, attended, proj
    )
    row_slots = finish_exchange(even_rows, start_exchange(odd_rows))
    other_grads = start_exchange(odd_grads)
    row_slots, even_grads, other_grads = lax.optimization_barrier(
        (row_slots, even_grads, other_grads)
    )
    grad_slots = finish_exchange(even_grads, other_grads)
    even, odd, hidden_pre = expert_forward(row_slots, full_up, full_down)
    even, odd, hidden_pre, grad_slots = lax.optimization_barrier(
        (even, odd, hidden_pre, grad_slots)
    )
    even, other, hidden_pre = lax.optimization_barrier((even, start_exchange(odd), hidden_pre))
    made_slots = finish_exchange(even, other)
    even, odd, grad_up, grad_down = expert_backward(
        row_slots, grad_slots, hidden_pre, full_up, full_down
    )
    even, odd, made_slots = lax.optimization_barrier((even, odd, made_slots))
    back_slots = finish_exchange(even, start_exchange(odd))
    grad_up = lax.psum_scatter(grad_up, "ctx", scatter_dimension=1, tiled=True).astype(F32)[None]
    grad_down = lax.psum_scatter(grad_down, "ctx", scatter_dimension=1, tiled=True)
    grad_down = grad_down.T.astype(F32)[None]

    output, grad_middle, *grad_near, proj_keep, proj_send, small_part = combine_rows(
        cotangent,
        gains,
        router,
        expert_ids,
        place,
        middle,
        normed_two,
        probs,
        attended,
        proj,
        made_slots,
        back_slots,
    )
    grad_query, grad_pairs = attend_backward(
        sizes, info, query, lse_prompt, lse_cont, pairs, xor_exchange(grad_near, "tp", tp_count)
    )

    remote_keep, remote_send = rows_remote(grad_pairs, pair_weight, ctx_count, tok_dev)
    remote_send = beside(remote_send)
    local_keep, local_send = rows_local(
        grad_pairs, grad_query, query_weight, pair_weight, tok_dev
    )
    local_send = beside(local_send)
    pieces = []
    for at in range(ctx_count - 1):
        chip = remote_keep[at] + remote_send[at].astype(F32)
        pieces.append(chip[:half_rows] + across(low(chip[half_rows:])).astype(F32))
    running = low(pieces[0])
    for piece in pieces[1:]:
        running = low(piece + ring_step(running, "ctx", ctx_count, -1).astype(F32))
    running = ring_step(running, "ctx", ctx_count, -1)
    far_rows = across(low(local_keep[0] + local_send[0].astype(F32)))
    grad_tokens = final_rows(
        side.astype(jnp.int32).reshape(1),
        tokens,
        gains,
        grad_middle,
        local_keep,
        local_send,
        far_rows,
        running,
        across(running),
    )

    def scatter_weights(values):
        values = low(values).reshape(dp_count, ctx_count, shard_rows, -1)
        for axis, size, me in (("dp", dp_count, dp_index), ("ctx", ctx_count, ctx_index)):
            moved = xor_exchange([pick(values, me ^ k) for k in range(size)], axis, size)
            values = add_all([piece.astype(F32) for piece in moved])
            if axis == "dp":
                values = low(values)
        return values

    def sum_tp(values):
        moved = xor_exchange([low(values)] * tp_count, "tp", tp_count)
        return values + add_all([piece.astype(F32) for piece in moved[1:]])

    proj_chip = proj_keep + beside(proj_send).astype(F32)
    proj_sum = proj_chip[0] + across(low(proj_chip[1])).astype(F32)
    early = jnp.concatenate([low(proj_sum), low(small_part[: expert_count + 1])], axis=0).T
    early = scatter_weights(early)
    grad_proj = early[:, :local_width].T
    small = sum_tp(early[:, local_width:])
    grad_qkv = scatter_weights(qkv_grad(grad_query, grad_pairs, rows))
    grad_qkv = grad_qkv.reshape(shard_rows, 3, local_width).transpose(1, 0, 2)
    gain_range = lax.dynamic_slice_in_dim(gains[0], shard_index * shard_rows, shard_rows)
    gain_one = sum_tp(jnp.sum(qkv_weight.astype(F32) * grad_qkv, axis=(0, 2))) / gain_range
    grad_router = small[:, :expert_count]
    grad_gains = jnp.stack([gain_one, small[:, expert_count]])
    return (output, grad_tokens, grad_gains, grad_qkv, grad_proj, grad_router, grad_up, grad_down)


def solution(mesh):
    in_specs = (
        P(("dp", "ctx", "tp"), None),
        P(("dp", "ctx", "tp"), None),
        P(),
        P(None, ("dp", "ctx"), "tp"),
        P("tp", ("dp", "ctx")),
        P(("dp", "ctx"), None),
        P(("dp", "tp"), None, "ctx"),
        P(("dp", "tp"), "ctx", None),
        P(("dp", "ctx", "tp"), None),
        P(("dp", "ctx", "tp"), None),
        P(("dp", "ctx")),
    )
    out_specs = (
        P(("dp", "ctx", "tp"), None),
        P(("dp", "ctx", "tp"), None),
        P(None, ("dp", "ctx")),
        P(None, ("dp", "ctx"), "tp"),
        P("tp", ("dp", "ctx")),
        P(("dp", "ctx"), None),
        P(("dp", "tp"), None, "ctx"),
        P(("dp", "tp"), "ctx", None),
    )
    return jax.shard_map(shards, mesh=mesh, in_specs=in_specs, out_specs=out_specs, check_vma=False)
```

```python
import functools

import jax
import jax.numpy as jnp
from jax import lax
from jax.experimental import pallas as pl
from jax.experimental.pallas import tpu as pltpu
from jax.sharding import PartitionSpec as P

HD = 64
PLEN = 1024
CLEN = 128
CONTS = 8
CHUNK = 128
UNITS = 768

EPSILON = 1e-06
NEGATIVE = -1e30
ROOT = 0.7978845608028654
CUBE = 0.044715
F32 = jnp.float32
BF16 = jnp.bfloat16
VM = pl.BlockSpec(memory_space=pltpu.VMEM)
SM = pl.BlockSpec(memory_space=pltpu.SMEM)
ROOM = pltpu.CompilerParams(vmem_limit_bytes=60 * 2**20)


def shape(dims, dtype=BF16):
    return jax.ShapeDtypeStruct(dims, dtype)


def low(value):
    return value.astype(BF16)


def dot_last(left, right):
    return lax.dot_general(left, right, (((1,), (1,)), ((), ())), preferred_element_type=F32)


def dot_plain(left, right):
    return lax.dot_general(left, right, (((1,), (0,)), ((), ())), preferred_element_type=F32)


def add_all(parts):
    return functools.reduce(jnp.add, parts)


def xor_swap(value, axis, size, mask):
    return lax.ppermute(value, axis, [(place, place ^ mask) for place in range(size)])


def ring_step(value, axis, size, shift):
    return lax.ppermute(value, axis, [(place, (place + shift) % size) for place in range(size)])


def pick(stacked, index):
    return lax.dynamic_index_in_dim(stacked, index, 0, keepdims=False)


def xor_gather(value, axis, size, order=None):
    if order is None:
        order = [1 << bit for bit in range(size.bit_length() - 1)]
    have = {0: value}
    for mask in order:
        keys = sorted(have)
        moved = xor_swap(jnp.stack([have[key] for key in keys]), axis, size, mask)
        for place, key in enumerate(keys):
            have[key ^ mask] = moved[place]
    return [have[key] for key in range(size)]


def xor_exchange(pieces, axis, size):
    return [pieces[0]] + [xor_swap(pieces[mask], axis, size, mask) for mask in range(1, size)]


def chunk_list(value, axis):
    return [
        lax.slice_in_dim(value, first, first + CHUNK, axis=axis)
        for first in range(0, value.shape[axis], CHUNK)
    ]


def split_order(value, axis=0):
    parts = chunk_list(value, axis)
    return jnp.concatenate(parts[0::2] + parts[1::2], axis=axis)


def plain_order(value, axis=0):
    parts = chunk_list(value, axis)
    half = len(parts) // 2
    return jnp.concatenate([parts[(at % 2) * half + at // 2] for at in range(2 * half)], axis=axis)


def rms_unit(values):
    factor = lax.rsqrt(jnp.mean(values * values, axis=-1, keepdims=True) + EPSILON)
    return (values * factor, factor)


def rms_backward(grad_normed, unit_part, factor, gain):
    scaled = grad_normed * gain
    inner = jnp.mean(scaled * unit_part, axis=-1, keepdims=True)
    return factor * (scaled - unit_part * inner)


def normalize_kernel(tokens, gains, own, second):
    unit, _ = rms_unit(tokens[...].astype(F32))
    own[...] = split_order(low(gains[0:1, :] * unit))
    second[...] = own[own.shape[0] // 2 :, :]


def normalize(tokens, gains):
    rows, width = tokens.shape
    return pl.pallas_call(
        normalize_kernel,
        out_shape=(shape((rows, width)), shape((rows // 2, width))),
        in_specs=[VM] * 2,
        out_specs=(VM,) * 2,
        compiler_params=ROOM,
        name="normalize",
    )(tokens, gains)


def key_lanes(rows, width):
    return rows[:, : width + (-width) % 128]


def value_lanes(rows, width):
    return rows[:, width - (-width) % 128 :]


def spread_heads(columns, ahead, behind):
    width, count = columns.shape
    groups = []
    for first in range(0, width, HD):
        pieces = [columns[first : first + HD]]
        above, below = ahead + first, width - first - HD + behind
        if above:
            pieces.insert(0, jnp.zeros((above, count), columns.dtype))
        if below:
            pieces.append(jnp.zeros((below, count), columns.dtype))
        groups.append(jnp.concatenate(pieces, axis=0))
    return jnp.concatenate(groups, axis=1)


def causal(scores, count):
    key_row = lax.broadcasted_iota(jnp.int32, scores.shape, 0)
    query_row = lax.broadcasted_iota(jnp.int32, scores.shape, 1) % count
    return jnp.where(key_row <= query_row, scores, NEGATIVE)


def work_items(info, sizes, attend):
    prompts, conts, places, per = sizes
    ctx_index = info[0]

    def prompt_chunks(prompt):
        first = 1 + prompt * 2 * per
        return [info[first + at] for at in range(per)], [info[first + per + at] for at in range(per)]

    def prompt_mask(scores):
        count = per * CHUNK
        parts = [causal(scores[:count], count)]
        for place in range(1, places):
            part = scores[place * count : (place + 1) * count]
            parts.append(jnp.where(place <= ctx_index, part, NEGATIVE))
        return jnp.concatenate(parts, axis=0)

    def cont_mask(scores):
        return jnp.concatenate([causal(scores[:CLEN], CLEN), scores[CLEN:]], axis=0)

    @pl.loop(0, prompts)
    def _(prompt):
        own, far = prompt_chunks(prompt)
        attend(0, prompt, own, own, far, prompt_mask)

    first = 1 + prompts * 2 * per

    @pl.loop(0, conts)
    def _(cont):
        own = [info[first + cont]]
        near, far = prompt_chunks(info[first + conts + cont])
        attend(1, cont, own, own + near, far, cont_mask)


def chunk_lanes(chunk):
    return pl.ds(pl.multiple_of(chunk * CHUNK, CHUNK), CHUNK)


def load_lanes(ref, chunks):
    return jnp.concatenate([ref[:, chunk_lanes(chunk)] for chunk in chunks], axis=1)


def project_local_kernel(query_weight, pair_weight, *rest):
    *rows, query, pairs = rest
    width = query.shape[0]
    query_flip = query_weight[...].T
    at = 0
    for one in rows:
        value = one[...]
        count = value.shape[0]
        pair = low(dot_plain(value, pair_weight[...]))
        pairs[at // CHUNK : (at + count) // CHUNK] = pair.reshape(-1, CHUNK, 2 * width)
        query[:, at : at + count] = low(dot_last(query_flip, value) * 0.125)
        at += count


def project_remote_kernel(pair_weight, *rest):
    *rows, pairs = rest
    at = 0
    for one in rows:
        count = one.shape[0]
        pair = low(dot_plain(one[...], pair_weight[...]))
        pairs[at // CHUNK : (at + count) // CHUNK] = pair.reshape(-1, CHUNK, pairs.shape[2])
        at += count


def project_local(query_weight, pair_weight, rows):
    count = sum(one.shape[0] for one in rows)
    wide = pair_weight.shape[1]
    return pl.pallas_call(
        project_local_kernel,
        out_shape=(shape((query_weight.shape[1], count)), shape((count // CHUNK, CHUNK, wide))),
        in_specs=[VM] * (2 + len(rows)),
        out_specs=(VM,) * 2,
        compiler_params=ROOM,
        cost_estimate=pl.CostEstimate(
            flops=3 * count * pair_weight.size, bytes_accessed=10**7, transcendentals=0
        ),
        name="project_local",
    )(query_weight, pair_weight, *rows)


def project_remote(pair_weight, rows):
    count = sum(one.shape[0] for one in rows)
    return pl.pallas_call(
        project_remote_kernel,
        out_shape=shape((count // CHUNK, CHUNK, pair_weight.shape[1])),
        in_specs=[VM] * (1 + len(rows)),
        out_specs=VM,
        compiler_params=ROOM,
        cost_estimate=pl.CostEstimate(
            flops=2 * count * pair_weight.size, bytes_accessed=4 * 10**6, transcendentals=0
        ),
        name="project_remote",
    )(pair_weight, *rows)


def load_block(local, remote, near, far):
    blocks = [local[chunk] for chunk in near]
    blocks += [one[chunk] for one in remote for chunk in far]
    return jnp.concatenate(blocks, axis=0)


def attend_forward_kernel(sizes, info, query, local, *rest):
    remote, (*outs, lse_prompt, lse_cont, mixed) = rest[: sizes[2] - 1], rest[sizes[2] - 1 :]
    lse = (lse_prompt, lse_cont)
    width = query.shape[0]
    pad = (-width) % 128

    def attend(kind, index, own, near, far, mask):
        count = len(own) * CHUNK
        block = load_block(local, remote, near, far)
        spread = spread_heads(load_lanes(query, own), 0, pad)
        scores = mask(dot_plain(key_lanes(block, width), spread))
        peak = jnp.max(scores, axis=0, keepdims=True)
        shifted = jnp.exp(scores - peak)
        total = jnp.sum(shifted, axis=0, keepdims=True)
        weights = low(shifted)
        flip = value_lanes(block, width).T
        for head in range(width // HD):
            group = slice(head * count, (head + 1) * count)
            part = slice(pad + head * HD, pad + (head + 1) * HD)
            result = low(dot_plain(flip[part], weights[:, group]) / total[:, group])
            for place, chunk in enumerate(own):
                mixed[head * HD : (head + 1) * HD, chunk_lanes(chunk)] = result[
                    :, place * CHUNK : (place + 1) * CHUNK
                ]
        lse[kind][index] = peak + jnp.log(total)

    work_items(info, sizes, attend)
    each = outs[0].shape[1]
    for place, out in enumerate(outs):
        out[...] = mixed[:, place * each : (place + 1) * each]


def attend_backward_kernel(sizes, info, query, lse_prompt, lse_cont, local, *rest):
    count_remote = sizes[2] - 1
    remote, rest = rest[:count_remote], rest[count_remote:]
    query_weight, pair_weight, *grads = rest[:6]
    grad_query, grad_local, *rest, grad, sum_local, sum_remote = rest[6:]
    grad_remote, rest = rest[:count_remote], rest[count_remote:]
    *rest, keep_local, send_local = rest
    keep_remote, send_remote = rest[: len(rest) // 2], rest[len(rest) // 2 :]
    lse = (lse_prompt, lse_cont)
    width = query.shape[0]
    pad = (-width) % 128
    each = grads[0].shape[1]
    for place, one in enumerate(grads):
        grad[:, place * each : (place + 1) * each] = one[...]

    def attend(kind, index, own, near, far, mask):
        count = len(own) * CHUNK
        block = load_block(local, remote, near, far)
        query_spread = spread_heads(load_lanes(query, own), 0, pad)
        grad_spread = spread_heads(load_lanes(grad, own), pad, 0)
        keys = key_lanes(block, width)
        weights = jnp.exp(mask(dot_plain(keys, query_spread)) - lse[kind][index])
        slopes = dot_plain(value_lanes(block, width), grad_spread)
        centre = jnp.sum(weights * slopes, axis=0, keepdims=True)
        grad_scores = low(weights * (slopes - centre))
        flip = keys.T
        for head in range(width // HD):
            group = slice(head * count, (head + 1) * count)
            part = slice(head * HD, (head + 1) * HD)
            result = low(dot_plain(flip[part], grad_scores[:, group]) * 0.125)
            for place, chunk in enumerate(own):
                grad_query[part, chunk_lanes(chunk)] = result[
                    :, place * CHUNK : (place + 1) * CHUNK
                ]
        key_part = dot_last(grad_scores, query_spread)
        value_part = dot_last(low(weights), grad_spread)
        if pad:
            edge = width - pad
            shared = key_part[:, edge:] + value_part[:, : 2 * pad]
            joined = [key_part[:, :edge], shared, value_part[:, 2 * pad :]]
        else:
            joined = [key_part, value_part]
        result = jnp.concatenate(joined, axis=1)
        spots = [(sum_local, chunk) for chunk in near]
        spots += [(sum_remote.at[place], chunk) for place in range(count_remote) for chunk in far]
        for at, (sums, chunk) in enumerate(spots):
            part = result[at * CHUNK : (at + 1) * CHUNK]
            if kind == 0 or at == 0:
                sums[chunk] = part
            else:
                sums[chunk] += part

    work_items(info, sizes, attend)

    half = remote[0].shape[0] // 2
    for place in range(count_remote):
        for side, outs in enumerate((keep_remote, send_remote)):
            chunks = slice(side * half, (side + 1) * half)
            part = low(sum_remote[place, chunks])
            grad_remote[place][chunks] = part
            if outs:
                flat = part.reshape(half * CHUNK, 2 * width)
                outs[place][...] = low(dot_last(flat, pair_weight[...]))
    for at, out in enumerate((keep_local.at[1], send_local.at[1], keep_local.at[0], send_local.at[0])):
        chunks = slice(at * half, (at + 1) * half)
        part = low(sum_local[chunks])
        grad_local[chunks] = part
        flat = part.reshape(half * CHUNK, 2 * width)
        part = grad_query[:, at * each : (at + 1) * each].T
        out[...] = low(dot_last(flat, pair_weight[...]) + dot_last(part, query_weight[...]))


def attend_cost(factor, sizes, heads):
    prompts, conts, places, per = sizes
    scores = heads * places * per * CHUNK * CHUNK * (prompts * per + conts)
    return pl.CostEstimate(flops=factor * HD * scores, bytes_accessed=10**7, transcendentals=scores)


def attend_forward(sizes, info, query, local, remote):
    prompts, conts, places, per = sizes
    width, local_rows = query.shape
    heads = width // HD
    return pl.pallas_call(
        functools.partial(attend_forward_kernel, sizes),
        out_shape=(
            *([shape((width, local_rows // 4))] * 4),
            shape((prompts, 1, heads * per * CHUNK), F32),
            shape((conts, 1, heads * CLEN), F32),
        ),
        in_specs=[SM] + [VM] * (2 + len(remote)),
        out_specs=(VM,) * 6,
        scratch_shapes=[pltpu.VMEM((width, local_rows), BF16)],
        compiler_params=ROOM,
        cost_estimate=attend_cost(16, sizes, heads),
        name="attend_forward",
    )(info, query, local, *remote)


def attend_backward(
    sizes, info, query, lse_prompt, lse_cont, local, remote, query_weight, pair_weight, grads
):
    pairs = [local] + list(remote)
    remote_rows = 2 * len(remote) if len(remote) <= 4 else 0
    each = shape((grads[0].shape[1], query_weight.shape[0]))
    both = shape((2,) + each.shape)
    count = len(remote)
    return pl.pallas_call(
        functools.partial(attend_backward_kernel, sizes),
        out_shape=(
            shape(query.shape),
            *(shape(one.shape) for one in pairs),
            *([each] * remote_rows),
            both,
            both,
        ),
        in_specs=[SM] + [VM] * (5 + len(pairs) + len(grads)),
        out_specs=(VM,) * (3 + len(pairs) + remote_rows),
        scratch_shapes=[
            pltpu.VMEM(query.shape, BF16),
            pltpu.VMEM(local.shape, F32),
            pltpu.VMEM((count,) + remote[0].shape, F32),
        ],
        compiler_params=ROOM,
        cost_estimate=attend_cost(40, sizes, query.shape[0] // HD),
        name="attend_backward",
    )(info, query, lse_prompt, lse_cont, *pairs, query_weight, pair_weight, *grads)


def rows_remote_kernel(grad_pairs, pair_weight, keep, send):
    half = grad_pairs.shape[0] // 2
    wide = grad_pairs.shape[2]
    send[...] = low(dot_last(grad_pairs[half:].reshape(half * CHUNK, wide), pair_weight[...]))
    keep[...] = low(dot_last(grad_pairs[:half].reshape(half * CHUNK, wide), pair_weight[...]))


def rows_remote(grad_pairs, pair_weight):
    dims = (grad_pairs.shape[0] // 2 * CHUNK, pair_weight.shape[0])
    return pl.pallas_call(
        rows_remote_kernel,
        in_specs=[VM] * 2,
        out_specs=(VM,) * 2,
        out_shape=(shape(dims), shape(dims)),
        compiler_params=ROOM,
        cost_estimate=pl.CostEstimate(
            flops=4 * dims[0] * pair_weight.size, bytes_accessed=6 * 10**6, transcendentals=0
        ),
        name="rows_remote",
    )(grad_pairs, pair_weight)


def qkv_grad_kernel(places, grad_query, *rest):
    pairs, rows, out = rest[:places], rest[places:-1], rest[-1]
    width, local_rows = grad_query.shape
    total_query = total_pair = None
    spots = [(pair, at) for pair in pairs for at in range(0, pair.shape[0] * CHUNK, CHUNK)]
    first = 0
    for one in rows:
        value = one[...]
        count = value.shape[0]
        pair, at = spots[first // CHUNK]
        chunks = slice(at // CHUNK, (at + count) // CHUNK)
        part = dot_plain(pair[chunks].reshape(count, 2 * width).T, value)
        total_pair = part if total_pair is None else total_pair + part
        if first < local_rows:
            part = dot_plain(grad_query[:, first : first + count], value)
            total_query = part if total_query is None else total_query + part
        first += count
    out[...] = low(jnp.concatenate([total_query, total_pair], axis=0).T)


def qkv_grad(grad_query, pairs, rows):
    width = rows[0].shape[1]
    count = sum(one.shape[0] for one in rows)
    return pl.pallas_call(
        functools.partial(qkv_grad_kernel, len(pairs)),
        out_shape=shape((width, 3 * grad_query.shape[0])),
        in_specs=[VM] * (1 + len(pairs) + len(rows)),
        out_specs=VM,
        compiler_params=ROOM,
        cost_estimate=pl.CostEstimate(
            flops=6 * count * width * grad_query.shape[0],
            bytes_accessed=2 * 10**7,
            transcendentals=0,
        ),
        name="qkv_grad",
    )(grad_query, *pairs, *rows)


def final_kernel(first, tokens, gains, grad_middle, kept, beside, across, own, far, out):
    unit, factor = rms_unit(tokens[...].astype(F32))
    rows = kept[0].astype(F32) + beside[0].astype(F32) + across[...].astype(F32)
    ring = jnp.concatenate([own[...], far[...]], axis=0).astype(F32)
    rows = plain_order(rows + jnp.where(first[0] == 0, ring, 0.0))
    out[...] = rms_backward(rows, unit, factor, gains[0:1, :]) + grad_middle[...]


def final_rows(side, tokens, gains, grad_middle, kept, beside, across, own, far):
    rows, width = tokens.shape
    last = pl.BlockSpec((1, rows, width), lambda at: (1, 0, 0))
    half = pl.BlockSpec((rows // 2, width), lambda at: (0, 0))
    whole = pl.BlockSpec((rows, width), lambda at: (0, 0))
    return pl.pallas_call(
        final_kernel,
        grid=(1,),
        in_specs=[
            SM,
            whole,
            pl.BlockSpec(gains.shape, lambda at: (0, 0)),
            whole,
            last,
            last,
            whole,
            half,
            half,
        ],
        out_specs=whole,
        out_shape=shape((rows, width), F32),
        compiler_params=ROOM,
        name="final_rows",
    )(side, tokens, gains, grad_middle, kept, beside, across, own, far)


def slot_places(chosen, priority, first, expert_count, capacity):
    tokens = chosen.shape[0]
    expert_range = jnp.arange(expert_count)
    chosen_hot = low(chosen[:, None] == expert_range[None, :])
    order_hot = low(priority[:, None] == jnp.arange(tokens)[None, :])
    sorted_hot = jnp.dot(order_hot, chosen_hot, preferred_element_type=F32)
    places = jnp.arange(tokens)
    before = low(places[:, None] > places[None, :])
    earlier = jnp.dot(before, low(sorted_hot), preferred_element_type=F32)
    sorted_rank = jnp.minimum(jnp.sum(earlier * sorted_hot, axis=1), capacity)
    rank = jnp.einsum("it,i->t", order_hot, low(sorted_rank), preferred_element_type=F32)
    rank = rank.astype(jnp.int32)
    near = chosen ^ first
    block = (near >> 1) + (near & 1) * (expert_count // 2)
    return jnp.where(rank < capacity, block * capacity + rank, -1)


def softmax_rows(logits):
    shifted = jnp.exp(logits - jnp.max(logits, axis=-1, keepdims=True))
    return shifted / jnp.sum(shifted, axis=-1, keepdims=True)


def one_hot_experts(ids, expert_count):
    return ids == lax.broadcasted_iota(jnp.int32, (ids.shape[0], expert_count), 1)


def middle_kernel(
    parts, tokens, cotangent, gains, router, ids, place_row, *rest
):
    attended, proj = rest[:parts], rest[parts : 2 * parts]
    even_rows, odd_rows, even_grads, odd_grads, middle, normed, probs = rest[2 * parts :]
    mixed = plain_order(jnp.concatenate([one[...] for one in attended], axis=0), 1)
    branch = dot_plain(mixed.T, jnp.concatenate([one[...] for one in proj], axis=0))
    total = tokens[...].astype(F32) + branch
    middle[...] = total
    unit, _ = rms_unit(total)
    normed_rows = low(gains[1:2, :] * unit)
    normed[...] = normed_rows
    chances = softmax_rows(dot_plain(normed_rows, router[...]))
    probs[...] = chances
    hot = one_hot_experts(ids[...], chances.shape[1])
    gate = jnp.sum(jnp.where(hot, chances, 0.0), axis=1, keepdims=True)
    weighted = low(gate * cotangent[...].astype(F32))
    half = even_rows.shape[0]
    for at, (row_slots, grad_slots) in enumerate(((even_rows, even_grads), (odd_rows, odd_grads))):
        slots = at * half + lax.broadcasted_iota(jnp.int32, (half, tokens.shape[0]), 0)
        dispatch = low(slots == place_row[...])
        row_slots[...] = low(dot_plain(dispatch, normed_rows))
        grad_slots[...] = low(dot_plain(dispatch, weighted))


def middle_rows(tokens, cotangent, gains, router, ids, place, slots, attended, proj):
    rows, width = tokens.shape
    half = shape((slots // 2, width))
    return pl.pallas_call(
        functools.partial(middle_kernel, len(attended)),
        out_shape=(
            half,
            half,
            half,
            half,
            shape((rows, width), F32),
            shape((rows, width)),
            shape((rows, router.shape[1]), F32),
        ),
        in_specs=[VM] * (6 + 2 * len(attended)),
        out_specs=(VM,) * 7,
        compiler_params=ROOM,
        name="middle_rows",
    )(tokens, cotangent, gains, router, ids, place[None, :], *attended, *proj)


def gather_slots(refs, capacity):
    own, beside, *pairs = refs
    even = [own[0:capacity, :]] + [pair[0:capacity, :] for pair in pairs]
    odd = [beside[0:capacity, :]] + [pair[capacity:, :] for pair in pairs]
    return jnp.concatenate(even + odd, axis=0)


def made_kernel(
    capacity, cotangent, ids, place_column, middle, normed, probs, *rest
):
    *row_refs, output, grad_logits, grad_router = rest
    rows, expert_count = probs.shape
    slots = 2 * row_refs[1].shape[0]
    slot_range = lax.broadcasted_iota(jnp.int32, (rows, slots), 1)
    dispatch = low(slot_range == place_column[...])
    routed = dot_plain(dispatch, gather_slots(row_refs, capacity))
    chances = probs[...]
    hot = one_hot_experts(ids[...], expert_count)
    gate = jnp.sum(jnp.where(hot, chances, 0.0), axis=1, keepdims=True)
    output[...] = low(middle[...] + gate * routed)
    grad_gate = jnp.sum(cotangent[...].astype(F32) * routed, axis=1, keepdims=True)
    logits = low((grad_gate * gate) * (hot.astype(F32) - chances))
    grad_logits[...] = logits
    grad_router[...] = dot_plain(logits.T, normed[...])


def made_rows(cotangent, ids, place, middle, normed, probs, row_slots):
    rows, width = middle.shape
    expert_count = probs.shape[1]
    capacity = row_slots[1].shape[0] // (len(row_slots) - 1)
    inputs = [cotangent, ids, place[:, None], middle, normed, probs, *row_slots]
    return pl.pallas_call(
        functools.partial(made_kernel, capacity),
        out_shape=(
            shape((rows, width)),
            shape((rows, expert_count)),
            shape((expert_count, width), F32),
        ),
        in_specs=[VM] * len(inputs),
        out_specs=(VM,) * 3,
        compiler_params=ROOM,
        name="made_rows",
    )(*inputs)


def back_kernel(
    parts, capacity, cotangent, gains, router, place_column, middle, grad_logits, *rest
):
    proj, rest = rest[:parts], rest[parts:]
    *grad_refs, grad_middle, grad_split, gain_two = rest[: -parts]
    near = rest[-parts:]
    rows = middle.shape[0]
    slots = 2 * grad_refs[1].shape[0]
    slot_range = lax.broadcasted_iota(jnp.int32, (rows, slots), 1)
    dispatch = low(slot_range == place_column[...])
    grad_second = dot_plain(dispatch, gather_slots(grad_refs, capacity))
    grad_second = grad_second + dot_last(grad_logits[...], router[...])
    unit, factor = rms_unit(middle[...])
    total = cotangent[...].astype(F32) + rms_backward(grad_second, unit, factor, gains[1:2, :])
    grad_low = split_order(low(total))
    for place in range(parts):
        near[place][...] = low(dot_last(proj[place][...], grad_low))
    grad_middle[...] = total
    grad_split[...] = grad_low
    summed = jnp.sum(grad_second * unit, axis=0, keepdims=True)
    gain_two[...] = jnp.broadcast_to(summed, gain_two.shape)


def back_rows(cotangent, gains, router, place, middle, grad_logits, proj, grad_slots):
    rows, width = middle.shape
    parts = len(proj)
    capacity = grad_slots[1].shape[0] // (len(grad_slots) - 1)
    inputs = [cotangent, gains, router, place[:, None], middle, grad_logits, *proj, *grad_slots]
    return pl.pallas_call(
        functools.partial(back_kernel, parts, capacity),
        out_shape=(
            shape((rows, width), F32),
            shape((rows, width)),
            shape((8, width), F32),
            *([shape((proj[0].shape[0], rows))] * parts),
        ),
        in_specs=[VM] * len(inputs),
        out_specs=(VM,) * (3 + parts),
        compiler_params=ROOM,
        name="back_rows",
    )(*inputs)


def proj_grad_kernel(grad_rows, *rest):
    *attended, keep, send = rest
    for place, one in enumerate(attended):
        part = dot_plain(one[...], grad_rows[...])
        if place % 2:
            send[place // 2] = low(part)
        else:
            keep[place // 2] = part


def proj_grad(grad_rows, attended):
    dims = (len(attended) // 2, attended[0].shape[0], grad_rows.shape[1])
    return pl.pallas_call(
        proj_grad_kernel,
        out_shape=(shape(dims, F32), shape(dims)),
        in_specs=[VM] * (1 + len(attended)),
        out_specs=(VM,) * 2,
        compiler_params=ROOM,
        name="proj_grad",
    )(grad_rows, *attended)


def expert_up_kernel(capacity, *refs):
    *parts, up, hidden, slope, rows_flip, rows = refs

    @pl.when(pl.program_id(0) == 0)
    def _():
        arrived = gather_slots(parts, capacity)
        rows[...] = arrived
        rows_flip[...] = arrived.T

    pre = dot_plain(rows[...], up[...])
    square = pre * pre
    bend = jnp.tanh(ROOT * (pre + CUBE * (square * pre)))
    half = 0.5 * (1.0 + bend)
    hidden[...] = low(pre * half)
    bent = (0.5 * ROOT) * pre * (1.0 - bend * bend) * (1.0 + (3.0 * CUBE) * square)
    slope[...] = low(half + bent)


def expert_out_kernel(hidden, down, even, odd, total):
    step = pl.program_id(0)
    part = dot_plain(hidden[...], down[...])

    @pl.when(step == 0)
    def _():
        total[...] = part

    @pl.when(step > 0)
    def _():
        total[...] += part

    @pl.when(step == pl.num_programs(0) - 1)
    def _():
        half = even.shape[0]
        even[...] = low(total[:half])
        odd[...] = low(total[half:])


def expert_down_kernel(capacity, *refs):
    *parts, hidden, grad_down, grads, grads_flip = refs

    @pl.when(pl.program_id(0) == 0)
    def _():
        arrived = gather_slots(parts, capacity)
        grads[...] = arrived
        grads_flip[...] = arrived.T

    grad_down[...] = low(dot_plain(grads_flip[...], hidden[...]))


def expert_back_kernel(grads, slope, rows_flip, up, down, even, odd, grad_up, total):
    step = pl.program_id(0)
    grad_pre = low(dot_last(grads[...], down[...]) * slope[...].astype(F32))
    grad_up[...] = low(dot_plain(rows_flip[...], grad_pre))
    part = dot_last(grad_pre, up[...])

    @pl.when(step == 0)
    def _():
        total[...] = part

    @pl.when(step > 0)
    def _():
        total[...] += part

    @pl.when(step == pl.num_programs(0) - 1)
    def _():
        half = even.shape[0]
        even[...] = low(total[:half])
        odd[...] = low(total[half:])


def whole_spec(dims):
    return pl.BlockSpec(dims, lambda at: (0, 0))


def column_spec(rows):
    return pl.BlockSpec((rows, UNITS), lambda at: (0, at))


def row_spec(width):
    return pl.BlockSpec((UNITS, width), lambda at: (at, 0))


def expert_cost(products, slots, width, units):
    return pl.CostEstimate(
        flops=2 * products * slots * width * units,
        bytes_accessed=4 * slots * units + 2 * products * width * units,
        transcendentals=slots * units,
    )


def expert_hidden(parts, up):
    width, units = up.shape
    half = parts[1].shape[0]
    slots = 2 * half
    return pl.pallas_call(
        functools.partial(expert_up_kernel, half // (len(parts) - 1)),
        grid=(units // UNITS,),
        in_specs=[whole_spec(one.shape) for one in parts] + [column_spec(width)],
        out_specs=(column_spec(slots), column_spec(slots), whole_spec((width, slots))),
        out_shape=(shape((slots, units)), shape((slots, units)), shape((width, slots))),
        scratch_shapes=[pltpu.VMEM((slots, width), BF16)],
        compiler_params=ROOM,
        cost_estimate=expert_cost(1, slots, width, units),
        name="expert_hidden",
    )(*parts, up)


def expert_out(hidden, down):
    slots, units = hidden.shape
    width = down.shape[1]
    block = whole_spec((slots // 2, width))
    return pl.pallas_call(
        expert_out_kernel,
        grid=(units // UNITS,),
        in_specs=[column_spec(slots), row_spec(width)],
        out_specs=(block, block),
        out_shape=(shape((slots // 2, width)), shape((slots // 2, width))),
        scratch_shapes=[pltpu.VMEM((slots, width), F32)],
        compiler_params=ROOM,
        cost_estimate=expert_cost(1, slots, width, units),
        name="expert_out",
    )(hidden, down)


def expert_down_grad(parts, hidden):
    slots, units = hidden.shape
    half, width = parts[1].shape
    return pl.pallas_call(
        functools.partial(expert_down_kernel, half // (len(parts) - 1)),
        grid=(units // UNITS,),
        in_specs=[whole_spec(one.shape) for one in parts] + [column_spec(slots)],
        out_specs=(column_spec(width), whole_spec((slots, width))),
        out_shape=(shape((width, units)), shape((slots, width))),
        scratch_shapes=[pltpu.VMEM((width, slots), BF16)],
        compiler_params=ROOM,
        cost_estimate=expert_cost(1, slots, width, units),
        name="expert_down_grad",
    )(*parts, hidden)


def expert_back(grads, slope, rows_flip, up, down):
    slots, units = slope.shape
    width = grads.shape[1]
    block = whole_spec((slots // 2, width))
    return pl.pallas_call(
        expert_back_kernel,
        grid=(units // UNITS,),
        in_specs=[
            whole_spec(grads.shape),
            column_spec(slots),
            whole_spec(rows_flip.shape),
            column_spec(width),
            row_spec(width),
        ],
        out_specs=(block, block, column_spec(width)),
        out_shape=(
            shape((slots // 2, width)),
            shape((slots // 2, width)),
            shape((width, units)),
        ),
        scratch_shapes=[pltpu.VMEM((slots, width), F32)],
        compiler_params=ROOM,
        cost_estimate=expert_cost(3, slots, width, units),
        name="expert_back",
    )(grads, slope, rows_flip, up, down)


def shards(
    tokens,
    cotangent,
    gains,
    qkv_weight,
    proj_weight,
    router_weight,
    expert_up,
    expert_down,
    expert_ids,
    slot_order,
    segment_ids,
):
    dp_count, ctx_count, tp_count = (lax.axis_size(name) for name in ("dp", "ctx", "tp"))
    dp_index, ctx_index, tp_index = (lax.axis_index(name) for name in ("dp", "ctx", "tp"))
    group = dp_count * tp_count
    group_index = dp_index * tp_count + tp_index
    tok_dev, width = tokens.shape
    half_rows = tok_dev // 2
    expert_count = router_weight.shape[1]
    capacity = 5 * tok_dev // (4 * expert_count)
    slots = expert_count * capacity
    per = PLEN // ctx_count // CHUNK
    conts_here = segment_ids.shape[0]
    prompts_here = conts_here * ctx_count // CONTS
    local_width = qkv_weight.shape[2]
    shard_rows = qkv_weight.shape[1]
    side, core = tp_index >> 1, tp_index & 1

    def across(value):
        return xor_swap(value, "tp", tp_count, 2)

    def beside(value):
        return xor_swap(value, "tp", tp_count, 1)

    packed = jnp.concatenate(
        [
            qkv_weight.transpose(1, 0, 2).reshape(shard_rows, 3 * local_width),
            proj_weight.T,
            router_weight,
        ],
        axis=1,
    )
    by_ctx = xor_exchange([packed] * ctx_count, "ctx", ctx_count)
    own, own_second = normalize(tokens, gains)
    far_second = across(own_second)
    carried = jnp.where(side == 0, own[:half_rows], far_second)
    by_ctx, carried = lax.optimization_barrier((by_ctx, carried))
    by_dp = xor_gather(jnp.stack(by_ctx), "dp", dp_count)
    far_first = across(own[:half_rows])
    arrived = ring_step(carried, "ctx", ctx_count, 1)
    arrived, far_first, by_dp = lax.optimization_barrier((arrived, far_first, by_dp))
    rows = [own, beside(own), far_first, far_second, beside(far_first), beside(far_second)]
    local_count = len(rows)

    by_dp = jnp.stack(by_dp).reshape((-1,) + packed.shape)
    shard_index = dp_index * ctx_count + ctx_index
    weights = jnp.concatenate(
        [pick(by_dp, shard_index ^ place) for place in range(dp_count * ctx_count)], axis=0
    )
    query_weight = weights[:, :local_width]
    pair_weight = weights[:, local_width : 3 * local_width]
    router = weights[:, 4 * local_width :]

    query, local = project_local(query_weight, pair_weight, rows)
    remote = []
    blocks = []
    for place in range(1, ctx_count):
        other = across(arrived)
        if place < ctx_count - 1:
            following = ring_step(arrived, "ctx", ctx_count, 1)
            if place == 1:
                expert_up, expert_down, following = lax.optimization_barrier(
                    (expert_up, expert_down, following)
                )
                full_up = lax.all_gather(expert_up, "ctx", axis=2, tiled=True)[0]
                full_down = lax.all_gather(expert_down, "ctx", axis=1, tiled=True)[0]
            if place == ctx_count - 2:
                following, query, local = lax.optimization_barrier((following, query, local))
            following, other = lax.optimization_barrier((following, other))
        blocks.append([arrived, other, beside(arrived), beside(other)])
        arrived = following
    rows += [one for block in blocks for one in block]
    remote = [project_remote(pair_weight, block) for block in blocks]
    proj_part, _ = lax.optimization_barrier(
        (weights[:, 3 * local_width : 4 * local_width].T, blocks[-1][1])
    )
    proj = xor_gather(proj_part, "tp", tp_count, [2, 1])

    device_chunks = tok_dev // CHUNK

    def split_place(at):
        return (at % 2) * (device_chunks // 2) + at // 2

    at = jnp.arange(prompts_here * per)
    owner, inside = at // device_chunks, at % device_chunks
    local_at = (owner ^ tp_index) * device_chunks + split_place(inside)
    remote_at = ((owner ^ core) * 2 + ((inside % 2) ^ side)) * (device_chunks // 2) + inside // 2
    prompt_at = jnp.concatenate(
        [local_at.reshape(prompts_here, per), remote_at.reshape(prompts_here, per)], axis=1
    )
    at = jnp.arange(conts_here)
    cont_at = ((2 + at // device_chunks) ^ tp_index) * device_chunks + split_place(
        at % device_chunks
    )
    info = jnp.concatenate([ctx_index[None], prompt_at.reshape(-1), cont_at, segment_ids])
    info = info.astype(jnp.int32)
    sizes = (prompts_here, conts_here, ctx_count, per)

    *attended, lse_prompt, lse_cont = attend_forward(sizes, info, query, local, remote)
    attended = xor_exchange(attended, "tp", tp_count)
    place = slot_places(expert_ids[:, 0], slot_order[0], group_index, expert_count, capacity)

    def start_exchange(odd):
        return xor_swap(odd, ("dp", "tp"), group, 1)

    def finish_exchange(even, other):
        moved = [even, other]
        for at in range(1, group // 2):
            block = slice(at * capacity, (at + 1) * capacity)
            pair = jnp.concatenate([even[block], other[block]], axis=0)
            moved.append(xor_swap(pair, ("dp", "tp"), group, 2 * at))
        return moved

    even_rows, odd_rows, even_grads, odd_grads, middle, normed_two, probs = middle_rows(
        tokens, cotangent, gains, router, expert_ids, place, slots, attended, proj
    )
    row_slots = finish_exchange(even_rows, start_exchange(odd_rows))
    other_grads = start_exchange(odd_grads)
    row_slots, even_grads, other_grads = lax.optimization_barrier(
        (row_slots, even_grads, other_grads)
    )
    grad_slots = finish_exchange(even_grads, other_grads)
    hidden, slope, rows_flip = expert_hidden(row_slots, full_up)
    grad_down, arrived_grads = expert_down_grad(grad_slots, hidden)
    hidden, arrived_grads = lax.optimization_barrier((hidden, arrived_grads))
    even, odd = expert_out(hidden, full_down)
    even, other, slope = lax.optimization_barrier((even, start_exchange(odd), slope))
    made_slots = finish_exchange(even, other)
    even, odd, grad_up = expert_back(arrived_grads, slope, rows_flip, full_up, full_down)
    even, odd, made_slots, grad_up = lax.optimization_barrier((even, odd, made_slots, grad_up))
    back_slots = finish_exchange(even, start_exchange(odd))
    grad_down = lax.psum_scatter(grad_down, "ctx", scatter_dimension=1, tiled=True)
    grad_down = grad_down.T.astype(F32)[None]
    grad_up = lax.psum_scatter(grad_up, "ctx", scatter_dimension=1, tiled=True).astype(F32)[None]

    output, grad_logits, router_part = made_rows(
        cotangent, expert_ids, place, middle, normed_two, probs, made_slots
    )
    grad_middle, grad_split, gain_two, *grad_near = back_rows(
        cotangent, gains, router, place, middle, grad_logits, proj, back_slots
    )
    grad_near = xor_exchange(grad_near, "tp", tp_count)
    proj_keep, proj_send = proj_grad(grad_split, attended)
    proj_chip = proj_keep + beside(proj_send).astype(F32)
    proj_message = low(proj_chip[1])
    grad_near, proj_message = lax.optimization_barrier((grad_near, proj_message))
    grad_query, grad_local, *grads = attend_backward(
        sizes,
        info,
        query,
        lse_prompt,
        lse_cont,
        local,
        remote,
        query_weight,
        pair_weight,
        grad_near,
    )
    count = ctx_count - 1
    grad_remote, (*remote_rows, local_keep, local_send) = grads[:count], grads[count:]
    if remote_rows:
        remote_rows = list(zip(remote_rows[:count], remote_rows[count:]))
    else:
        remote_rows = [rows_remote(one, pair_weight) for one in grad_remote]

    pieces = []
    messages = []
    for keep, send in remote_rows[::-1]:
        chip = keep.astype(F32) + beside(send).astype(F32)
        messages.append(low(chip[half_rows:]))
        pieces.append(chip[:half_rows])
    local_send, proj_message, messages = lax.optimization_barrier(
        (local_send, proj_message, messages)
    )
    pieces = [piece + across(message).astype(F32) for piece, message in zip(pieces, messages)]
    running = low(pieces[0])
    local_send = beside(local_send)
    far_message = low(local_keep[0].astype(F32) + local_send[0].astype(F32))
    far_rows = across(far_message)
    proj_far = across(proj_message)
    grad_pairs, running, far_message = lax.optimization_barrier(
        ([grad_local, *grad_remote], running, far_message)
    )
    qkv_part = qkv_grad(grad_query, grad_pairs, rows)
    moved = ring_step(running, "ctx", ctx_count, -1)
    moved, proj_far, qkv_part = lax.optimization_barrier((moved, proj_far, qkv_part))

    proj_sum = proj_chip[0] + proj_far.astype(F32)
    early = jnp.concatenate([low(proj_sum), low(router_part), low(gain_two[:1])], axis=0).T
    packed = jnp.concatenate([qkv_part, early], axis=1)
    packed = packed.reshape(dp_count, ctx_count, shard_rows, -1)

    def scatter_sum(values, axis, size, me):
        parts = xor_exchange([pick(values, me ^ k) for k in range(size)], axis, size)
        return add_all([piece.astype(F32) for piece in parts])

    for piece in pieces[1:-1]:
        moved = ring_step(low(piece + moved.astype(F32)), "ctx", ctx_count, -1)
    summed = low(scatter_sum(packed, "dp", dp_count, dp_index))
    moved, summed, far_rows = lax.optimization_barrier((moved, summed, far_rows))
    running = low(pieces[-1] + moved.astype(F32))
    hops = [[], []]
    for ctx_from in range(ctx_count):
        for tp_from in range(tp_count):
            target = (ctx_from - 1) % ctx_count * tp_count + (tp_from & 1)
            hops[tp_from >> 1].append((ctx_from * tp_count + tp_from, target))
    own_rows, other_rows = (lax.ppermute(running, ("ctx", "tp"), hop) for hop in hops)
    summed = scatter_sum(summed, "ctx", ctx_count, ctx_index)
    other_rows, grad_up, grad_down = lax.optimization_barrier((other_rows, grad_up, grad_down))
    grad_tokens = final_rows(
        side.astype(jnp.int32).reshape(1),
        tokens,
        gains,
        grad_middle,
        local_keep,
        local_send,
        far_rows,
        own_rows,
        other_rows,
    )

    def sum_tp(values):
        moved = xor_exchange([low(values)] * tp_count, "tp", tp_count)
        return values + add_all([piece.astype(F32) for piece in moved[1:]])

    qkv_width = 3 * local_width
    grad_qkv = summed[:, :qkv_width].reshape(shard_rows, 3, local_width).transpose(1, 0, 2)
    grad_proj = summed[:, qkv_width : qkv_width + local_width].T
    gain_range = lax.dynamic_slice_in_dim(gains[0], shard_index * shard_rows, shard_rows)
    gain_one = jnp.sum(qkv_weight.astype(F32) * grad_qkv, axis=(0, 2))
    small = sum_tp(jnp.concatenate([summed[:, qkv_width + local_width :], gain_one[:, None]], axis=1))
    grad_router = small[:, :expert_count]
    grad_gains = jnp.stack([small[:, expert_count + 1] / gain_range, small[:, expert_count]])
    return (output, grad_tokens, grad_gains, grad_qkv, grad_proj, grad_router, grad_up, grad_down)


def solution(mesh):
    in_specs = (
        P(("dp", "ctx", "tp"), None),
        P(("dp", "ctx", "tp"), None),
        P(),
        P(None, ("dp", "ctx"), "tp"),
        P("tp", ("dp", "ctx")),
        P(("dp", "ctx"), None),
        P(("dp", "tp"), None, "ctx"),
        P(("dp", "tp"), "ctx", None),
        P(("dp", "ctx", "tp"), None),
        P(("dp", "ctx", "tp"), None),
        P(("dp", "ctx")),
    )
    out_specs = (
        P(("dp", "ctx", "tp"), None),
        P(("dp", "ctx", "tp"), None),
        P(None, ("dp", "ctx")),
        P(None, ("dp", "ctx"), "tp"),
        P("tp", ("dp", "ctx")),
        P(("dp", "ctx"), None),
        P(("dp", "tp"), None, "ctx"),
        P(("dp", "tp"), "ctx", None),
    )
    return jax.shard_map(shards, mesh=mesh, in_specs=in_specs, out_specs=out_specs, check_vma=False)
```

```python
import functools

import jax
import jax.numpy as jnp
from jax import lax
from jax.experimental import pallas as pl
from jax.experimental.pallas import tpu as pltpu
from jax.sharding import PartitionSpec as P

HD = 64
PLEN = 1024
CLEN = 128
CONTS = 8
CHUNK = 128
UNITS = 768

EPSILON = 1e-06
NEGATIVE = -1e30
ROOT = 0.7978845608028654
CUBE = 0.044715
F32 = jnp.float32
BF16 = jnp.bfloat16
VM = pl.BlockSpec(memory_space=pltpu.VMEM)
SM = pl.BlockSpec(memory_space=pltpu.SMEM)
ROOM = pltpu.CompilerParams(vmem_limit_bytes=60 * 2**20)


def shape(dims, dtype=BF16):
    return jax.ShapeDtypeStruct(dims, dtype)


def low(value):
    return value.astype(BF16)


def dot_last(left, right):
    return lax.dot_general(left, right, (((1,), (1,)), ((), ())), preferred_element_type=F32)


def dot_plain(left, right):
    return lax.dot_general(left, right, (((1,), (0,)), ((), ())), preferred_element_type=F32)


def add_all(parts):
    return functools.reduce(jnp.add, parts)


def xor_swap(value, axis, size, mask):
    return lax.ppermute(value, axis, [(place, place ^ mask) for place in range(size)])


def ring_step(value, axis, size, shift):
    return lax.ppermute(value, axis, [(place, (place + shift) % size) for place in range(size)])


def pick(stacked, index):
    return lax.dynamic_index_in_dim(stacked, index, 0, keepdims=False)


def xor_gather(value, axis, size, order=None):
    if order is None:
        order = [1 << bit for bit in range(size.bit_length() - 1)]
    have = {0: value}
    for mask in order:
        keys = sorted(have)
        moved = xor_swap(jnp.stack([have[key] for key in keys]), axis, size, mask)
        for place, key in enumerate(keys):
            have[key ^ mask] = moved[place]
    return [have[key] for key in range(size)]


def xor_exchange(pieces, axis, size):
    return [pieces[0]] + [xor_swap(pieces[mask], axis, size, mask) for mask in range(1, size)]


def chunk_list(value, axis):
    return [
        lax.slice_in_dim(value, first, first + CHUNK, axis=axis)
        for first in range(0, value.shape[axis], CHUNK)
    ]


def split_order(value, axis=0):
    parts = chunk_list(value, axis)
    return jnp.concatenate(parts[0::2] + parts[1::2], axis=axis)


def plain_order(value, axis=0):
    parts = chunk_list(value, axis)
    half = len(parts) // 2
    return jnp.concatenate([parts[(at % 2) * half + at // 2] for at in range(2 * half)], axis=axis)


def rms_unit(values):
    factor = lax.rsqrt(jnp.mean(values * values, axis=-1, keepdims=True) + EPSILON)
    return (values * factor, factor)


def rms_backward(grad_normed, unit_part, factor, gain):
    scaled = grad_normed * gain
    inner = jnp.mean(scaled * unit_part, axis=-1, keepdims=True)
    return factor * (scaled - unit_part * inner)


def normalize_kernel(tokens, gains, own, second):
    unit, _ = rms_unit(tokens[...].astype(F32))
    own[...] = split_order(low(gains[0:1, :] * unit))
    second[...] = own[own.shape[0] // 2 :, :]


def normalize(tokens, gains):
    rows, width = tokens.shape
    return pl.pallas_call(
        normalize_kernel,
        out_shape=(shape((rows, width)), shape((rows // 2, width))),
        in_specs=[VM] * 2,
        out_specs=(VM,) * 2,
        compiler_params=ROOM,
        name="normalize",
    )(tokens, gains)


def key_lanes(rows, width):
    return rows[:, : width + (-width) % 128]


def value_lanes(rows, width):
    return rows[:, width - (-width) % 128 :]


def spread_heads(columns, ahead, behind):
    width, count = columns.shape
    groups = []
    for first in range(0, width, HD):
        pieces = [columns[first : first + HD]]
        above, below = ahead + first, width - first - HD + behind
        if above:
            pieces.insert(0, jnp.zeros((above, count), columns.dtype))
        if below:
            pieces.append(jnp.zeros((below, count), columns.dtype))
        groups.append(jnp.concatenate(pieces, axis=0))
    return jnp.concatenate(groups, axis=1)


def causal(scores, count):
    key_row = lax.broadcasted_iota(jnp.int32, scores.shape, 0)
    query_row = lax.broadcasted_iota(jnp.int32, scores.shape, 1) % count
    return jnp.where(key_row <= query_row, scores, NEGATIVE)


def work_items(info, sizes, attend):
    prompts, conts, places, per = sizes
    ctx_index = info[0]

    def prompt_chunks(prompt):
        first = 1 + prompt * 2 * per
        return [info[first + at] for at in range(per)], [info[first + per + at] for at in range(per)]

    def prompt_mask(scores):
        count = per * CHUNK
        parts = [causal(scores[:count], count)]
        for place in range(1, places):
            part = scores[place * count : (place + 1) * count]
            parts.append(jnp.where(place <= ctx_index, part, NEGATIVE))
        return jnp.concatenate(parts, axis=0)

    def cont_mask(scores):
        return jnp.concatenate([causal(scores[:CLEN], CLEN), scores[CLEN:]], axis=0)

    @pl.loop(0, prompts, unroll=2)
    def _(prompt):
        own, far = prompt_chunks(prompt)
        attend(0, prompt, own, own, far, prompt_mask)

    first = 1 + prompts * 2 * per

    @pl.loop(0, conts, unroll=2)
    def _(cont):
        own = [info[first + cont]]
        near, far = prompt_chunks(info[first + conts + cont])
        attend(1, cont, own, own + near, far, cont_mask)


def chunk_lanes(chunk):
    return pl.ds(pl.multiple_of(chunk * CHUNK, CHUNK), CHUNK)


def load_lanes(ref, chunks):
    return jnp.concatenate([ref[:, chunk_lanes(chunk)] for chunk in chunks], axis=1)


def project_local_kernel(query_weight, pair_weight, *rest):
    *rows, query, pairs = rest
    width = query.shape[0]
    query_flip = query_weight[...].T
    at = 0
    for one in rows:
        value = one[...]
        count = value.shape[0]
        pair = low(dot_plain(value, pair_weight[...]))
        pairs[at // CHUNK : (at + count) // CHUNK] = pair.reshape(-1, CHUNK, 2 * width)
        query[:, at : at + count] = low(dot_last(query_flip, value) * 0.125)
        at += count


def project_remote_kernel(pair_weight, *rest):
    *rows, pairs = rest
    at = 0
    for one in rows:
        count = one.shape[0]
        pair = low(dot_plain(one[...], pair_weight[...]))
        pairs[at // CHUNK : (at + count) // CHUNK] = pair.reshape(-1, CHUNK, pairs.shape[2])
        at += count


def project_local(query_weight, pair_weight, rows):
    count = sum(one.shape[0] for one in rows)
    wide = pair_weight.shape[1]
    return pl.pallas_call(
        project_local_kernel,
        out_shape=(shape((query_weight.shape[1], count)), shape((count // CHUNK, CHUNK, wide))),
        in_specs=[VM] * (2 + len(rows)),
        out_specs=(VM,) * 2,
        compiler_params=ROOM,
        cost_estimate=pl.CostEstimate(
            flops=3 * count * pair_weight.size, bytes_accessed=10**7, transcendentals=0
        ),
        name="project_local",
    )(query_weight, pair_weight, *rows)


def project_remote(pair_weight, rows):
    count = sum(one.shape[0] for one in rows)
    return pl.pallas_call(
        project_remote_kernel,
        out_shape=shape((count // CHUNK, CHUNK, pair_weight.shape[1])),
        in_specs=[VM] * (1 + len(rows)),
        out_specs=VM,
        compiler_params=ROOM,
        cost_estimate=pl.CostEstimate(
            flops=2 * count * pair_weight.size, bytes_accessed=4 * 10**6, transcendentals=0
        ),
        name="project_remote",
    )(pair_weight, *rows)


def load_block(local, remote, near, far):
    blocks = [local[chunk] for chunk in near]
    blocks += [one[chunk] for one in remote for chunk in far]
    return jnp.concatenate(blocks, axis=0)


def attend_forward_kernel(sizes, info, query, local, *rest):
    remote, (*outs, lse_prompt, lse_cont, mixed) = rest[: sizes[2] - 1], rest[sizes[2] - 1 :]
    lse = (lse_prompt, lse_cont)
    width = query.shape[0]
    pad = (-width) % 128

    def attend(kind, index, own, near, far, mask):
        count = len(own) * CHUNK
        block = load_block(local, remote, near, far)
        spread = spread_heads(load_lanes(query, own), 0, pad)
        scores = mask(dot_plain(key_lanes(block, width), spread))
        peak = jnp.max(scores, axis=0, keepdims=True)
        shifted = jnp.exp(scores - peak)
        total = jnp.sum(shifted, axis=0, keepdims=True)
        weights = low(shifted)
        flip = value_lanes(block, width).T
        for head in range(width // HD):
            group = slice(head * count, (head + 1) * count)
            part = slice(pad + head * HD, pad + (head + 1) * HD)
            result = low(dot_plain(flip[part], weights[:, group]) / total[:, group])
            for place, chunk in enumerate(own):
                mixed[head * HD : (head + 1) * HD, chunk_lanes(chunk)] = result[
                    :, place * CHUNK : (place + 1) * CHUNK
                ]
        lse[kind][index] = peak + jnp.log(total)

    work_items(info, sizes, attend)
    each = outs[0].shape[1]
    for place, out in enumerate(outs):
        out[...] = mixed[:, place * each : (place + 1) * each]


def attend_backward_kernel(sizes, info, query, lse_prompt, lse_cont, local, *rest):
    count_remote = sizes[2] - 1
    remote, rest = rest[:count_remote], rest[count_remote:]
    query_weight, pair_weight, *rest = rest
    grads, mixed, rest = rest[:4], rest[4:8], rest[8:]
    grad_query, grad_local, *rest, grad, centre, sum_local, sum_remote = rest
    grad_remote, rest = rest[:count_remote], rest[count_remote:]
    *rest, keep_local, send_local = rest
    keep_remote, send_remote = rest[: len(rest) // 2], rest[len(rest) // 2 :]
    lse = (lse_prompt, lse_cont)
    width = query.shape[0]
    pad = (-width) % 128
    each = grads[0].shape[1]
    for place, (one, result) in enumerate(zip(grads, mixed)):
        columns = slice(place * each, (place + 1) * each)
        grad[:, columns] = one[...]
        product = one[...].astype(F32) * result[...].astype(F32)
        for head in range(width // HD):
            centre[head : head + 1, columns] = jnp.sum(
                product[head * HD : (head + 1) * HD], axis=0, keepdims=True
            )

    def attend(kind, index, own, near, far, mask):
        count = len(own) * CHUNK
        block = load_block(local, remote, near, far)
        query_spread = spread_heads(load_lanes(query, own), 0, pad)
        grad_spread = spread_heads(load_lanes(grad, own), pad, 0)
        keys = key_lanes(block, width)
        weights = jnp.exp(mask(dot_plain(keys, query_spread)) - lse[kind][index])
        slopes = dot_plain(value_lanes(block, width), grad_spread)
        middle = load_lanes(centre, own)
        middle = jnp.concatenate([middle[head : head + 1] for head in range(width // HD)], axis=1)
        grad_scores = low(weights * (slopes - middle))
        flip = keys.T
        for head in range(width // HD):
            group = slice(head * count, (head + 1) * count)
            part = slice(head * HD, (head + 1) * HD)
            result = low(dot_plain(flip[part], grad_scores[:, group]) * 0.125)
            for place, chunk in enumerate(own):
                grad_query[part, chunk_lanes(chunk)] = result[
                    :, place * CHUNK : (place + 1) * CHUNK
                ]
        key_part = dot_last(grad_scores, query_spread)
        value_part = dot_last(low(weights), grad_spread)
        if pad:
            edge = width - pad
            shared = key_part[:, edge:] + value_part[:, : 2 * pad]
            joined = [key_part[:, :edge], shared, value_part[:, 2 * pad :]]
        else:
            joined = [key_part, value_part]
        result = jnp.concatenate(joined, axis=1)
        spots = [(sum_local, chunk) for chunk in near]
        spots += [(sum_remote.at[place], chunk) for place in range(count_remote) for chunk in far]
        for at, (sums, chunk) in enumerate(spots):
            part = result[at * CHUNK : (at + 1) * CHUNK]
            if kind == 0 or at == 0:
                sums[chunk] = part
            else:
                sums[chunk] += part

    work_items(info, sizes, attend)

    half = remote[0].shape[0] // 2
    for place in range(count_remote):
        for side, outs in enumerate((keep_remote, send_remote)):
            chunks = slice(side * half, (side + 1) * half)
            part = low(sum_remote[place, chunks])
            grad_remote[place][chunks] = part
            if outs:
                flat = part.reshape(half * CHUNK, 2 * width)
                outs[place][...] = low(dot_last(flat, pair_weight[...]))
    for at, out in enumerate((keep_local.at[1], send_local.at[1], keep_local.at[0], send_local.at[0])):
        chunks = slice(at * half, (at + 1) * half)
        part = low(sum_local[chunks])
        grad_local[chunks] = part
        flat = part.reshape(half * CHUNK, 2 * width)
        part = grad_query[:, at * each : (at + 1) * each].T
        out[...] = low(dot_last(flat, pair_weight[...]) + dot_last(part, query_weight[...]))


def attend_cost(factor, sizes, heads):
    prompts, conts, places, per = sizes
    scores = heads * places * per * CHUNK * CHUNK * (prompts * per + conts)
    return pl.CostEstimate(flops=factor * HD * scores, bytes_accessed=10**7, transcendentals=scores)


def attend_forward(sizes, info, query, local, remote):
    prompts, conts, places, per = sizes
    width, local_rows = query.shape
    heads = width // HD
    return pl.pallas_call(
        functools.partial(attend_forward_kernel, sizes),
        out_shape=(
            *([shape((width, local_rows // 4))] * 4),
            shape((prompts, 1, heads * per * CHUNK), F32),
            shape((conts, 1, heads * CLEN), F32),
        ),
        in_specs=[SM] + [VM] * (2 + len(remote)),
        out_specs=(VM,) * 6,
        scratch_shapes=[pltpu.VMEM((width, local_rows), BF16)],
        compiler_params=ROOM,
        cost_estimate=attend_cost(16, sizes, heads),
        name="attend_forward",
    )(info, query, local, *remote)


def attend_backward(
    sizes, info, query, lse_prompt, lse_cont, local, remote, query_weight, pair_weight, grads, mixed
):
    pairs = [local] + list(remote)
    remote_rows = 2 * len(remote) if len(remote) <= 4 else 0
    each = shape((grads[0].shape[1], query_weight.shape[0]))
    both = shape((2,) + each.shape)
    count = len(remote)
    return pl.pallas_call(
        functools.partial(attend_backward_kernel, sizes),
        out_shape=(
            shape(query.shape),
            *(shape(one.shape) for one in pairs),
            *([each] * remote_rows),
            both,
            both,
        ),
        in_specs=[SM] + [VM] * (5 + len(pairs) + 2 * len(grads)),
        out_specs=(VM,) * (3 + len(pairs) + remote_rows),
        scratch_shapes=[
            pltpu.VMEM(query.shape, BF16),
            pltpu.VMEM((8, query.shape[1]), F32),
            pltpu.VMEM(local.shape, F32),
            pltpu.VMEM((count,) + remote[0].shape, F32),
        ],
        compiler_params=ROOM,
        cost_estimate=attend_cost(40, sizes, query.shape[0] // HD),
        name="attend_backward",
    )(info, query, lse_prompt, lse_cont, *pairs, query_weight, pair_weight, *grads, *mixed)


def rows_remote_kernel(grad_pairs, pair_weight, keep, send):
    half = grad_pairs.shape[0] // 2
    wide = grad_pairs.shape[2]
    send[...] = low(dot_last(grad_pairs[half:].reshape(half * CHUNK, wide), pair_weight[...]))
    keep[...] = low(dot_last(grad_pairs[:half].reshape(half * CHUNK, wide), pair_weight[...]))


def rows_remote(grad_pairs, pair_weight):
    dims = (grad_pairs.shape[0] // 2 * CHUNK, pair_weight.shape[0])
    return pl.pallas_call(
        rows_remote_kernel,
        in_specs=[VM] * 2,
        out_specs=(VM,) * 2,
        out_shape=(shape(dims), shape(dims)),
        compiler_params=ROOM,
        cost_estimate=pl.CostEstimate(
            flops=4 * dims[0] * pair_weight.size, bytes_accessed=6 * 10**6, transcendentals=0
        ),
        name="rows_remote",
    )(grad_pairs, pair_weight)


def qkv_grad_kernel(places, grad_query, *rest):
    pairs, rows, out = rest[:places], rest[places:-1], rest[-1]
    width, local_rows = grad_query.shape
    total_query = total_pair = None
    spots = [(pair, at) for pair in pairs for at in range(0, pair.shape[0] * CHUNK, CHUNK)]
    first = 0
    for one in rows:
        value = one[...]
        count = value.shape[0]
        pair, at = spots[first // CHUNK]
        chunks = slice(at // CHUNK, (at + count) // CHUNK)
        part = dot_plain(pair[chunks].reshape(count, 2 * width).T, value)
        total_pair = part if total_pair is None else total_pair + part
        if first < local_rows:
            part = dot_plain(grad_query[:, first : first + count], value)
            total_query = part if total_query is None else total_query + part
        first += count
    out[...] = low(jnp.concatenate([total_query, total_pair], axis=0).T)


def qkv_grad(grad_query, pairs, rows):
    width = rows[0].shape[1]
    count = sum(one.shape[0] for one in rows)
    return pl.pallas_call(
        functools.partial(qkv_grad_kernel, len(pairs)),
        out_shape=shape((width, 3 * grad_query.shape[0])),
        in_specs=[VM] * (1 + len(pairs) + len(rows)),
        out_specs=VM,
        compiler_params=ROOM,
        cost_estimate=pl.CostEstimate(
            flops=6 * count * width * grad_query.shape[0],
            bytes_accessed=2 * 10**7,
            transcendentals=0,
        ),
        name="qkv_grad",
    )(grad_query, *pairs, *rows)


def final_kernel(first, tokens, gains, grad_middle, kept, beside, one, two, own, far, out):
    unit, factor = rms_unit(tokens[...].astype(F32))
    across = jnp.concatenate([one[one.shape[0] + two.shape[0] - kept.shape[1] :, :], two[...]], axis=0)
    rows = kept[0].astype(F32) + beside[0].astype(F32) + across.astype(F32)
    ring = jnp.concatenate([own[...], far[...]], axis=0).astype(F32)
    rows = plain_order(rows + jnp.where(first[0] == 0, ring, 0.0))
    out[...] = rms_backward(rows, unit, factor, gains[0:1, :]) + grad_middle[...]


def final_rows(side, tokens, gains, grad_middle, kept, beside, one, two, own, far):
    rows, width = tokens.shape
    last = pl.BlockSpec((1, rows, width), lambda at: (1, 0, 0))
    half = pl.BlockSpec((rows // 2, width), lambda at: (0, 0))
    whole = pl.BlockSpec((rows, width), lambda at: (0, 0))
    return pl.pallas_call(
        final_kernel,
        grid=(1,),
        in_specs=[
            SM,
            whole,
            pl.BlockSpec(gains.shape, lambda at: (0, 0)),
            whole,
            last,
            last,
            pl.BlockSpec(one.shape, lambda at: (0, 0)),
            pl.BlockSpec(two.shape, lambda at: (0, 0)),
            half,
            half,
        ],
        out_specs=whole,
        out_shape=shape((rows, width), F32),
        compiler_params=ROOM,
        name="final_rows",
    )(side, tokens, gains, grad_middle, kept, beside, one, two, own, far)


def slot_places(chosen, priority, first, expert_count, capacity):
    tokens = chosen.shape[0]
    expert_range = jnp.arange(expert_count)
    chosen_hot = low(chosen[:, None] == expert_range[None, :])
    order_hot = low(priority[:, None] == jnp.arange(tokens)[None, :])
    sorted_hot = jnp.dot(order_hot, chosen_hot, preferred_element_type=F32)
    places = jnp.arange(tokens)
    before = low(places[:, None] > places[None, :])
    earlier = jnp.dot(before, low(sorted_hot), preferred_element_type=F32)
    sorted_rank = jnp.minimum(jnp.sum(earlier * sorted_hot, axis=1), capacity)
    rank = jnp.einsum("it,i->t", order_hot, low(sorted_rank), preferred_element_type=F32)
    rank = rank.astype(jnp.int32)
    near = chosen ^ first
    block = (near >> 1) + (near & 1) * (expert_count // 2)
    return jnp.where(rank < capacity, block * capacity + rank, -1)


def softmax_rows(logits):
    shifted = jnp.exp(logits - jnp.max(logits, axis=-1, keepdims=True))
    return shifted / jnp.sum(shifted, axis=-1, keepdims=True)


def one_hot_experts(ids, expert_count):
    return ids == lax.broadcasted_iota(jnp.int32, (ids.shape[0], expert_count), 1)


def middle_kernel(
    parts, tokens, cotangent, gains, router, ids, place_row, *rest
):
    attended, proj = rest[:parts], rest[parts : 2 * parts]
    even_rows, odd_rows, even_grads, odd_grads, middle, normed, probs = rest[2 * parts :]
    mixed = plain_order(jnp.concatenate([one[...] for one in attended], axis=0), 1)
    branch = dot_plain(mixed.T, jnp.concatenate([one[...] for one in proj], axis=0))
    total = tokens[...].astype(F32) + branch
    middle[...] = total
    unit, _ = rms_unit(total)
    normed_rows = low(gains[1:2, :] * unit)
    normed[...] = normed_rows
    chances = softmax_rows(dot_plain(normed_rows, router[...]))
    probs[...] = chances
    hot = one_hot_experts(ids[...], chances.shape[1])
    gate = jnp.sum(jnp.where(hot, chances, 0.0), axis=1, keepdims=True)
    weighted = low(gate * cotangent[...].astype(F32))
    half = even_rows.shape[0]
    for at, (row_slots, grad_slots) in enumerate(((even_rows, even_grads), (odd_rows, odd_grads))):
        slots = at * half + lax.broadcasted_iota(jnp.int32, (half, tokens.shape[0]), 0)
        dispatch = low(slots == place_row[...])
        row_slots[...] = low(dot_plain(dispatch, normed_rows))
        grad_slots[...] = low(dot_plain(dispatch, weighted))


def middle_rows(tokens, cotangent, gains, router, ids, place, slots, attended, proj):
    rows, width = tokens.shape
    half = shape((slots // 2, width))
    return pl.pallas_call(
        functools.partial(middle_kernel, len(attended)),
        out_shape=(
            half,
            half,
            half,
            half,
            shape((rows, width), F32),
            shape((rows, width)),
            shape((rows, router.shape[1]), F32),
        ),
        in_specs=[VM] * (6 + 2 * len(attended)),
        out_specs=(VM,) * 7,
        compiler_params=ROOM,
        name="middle_rows",
    )(tokens, cotangent, gains, router, ids, place[None, :], *attended, *proj)


def gather_slots(refs, capacity):
    own, beside, *pairs = refs
    even = [own[0:capacity, :]] + [pair[0:capacity, :] for pair in pairs]
    odd = [beside[0:capacity, :]] + [pair[capacity:, :] for pair in pairs]
    return jnp.concatenate(even + odd, axis=0)


def made_kernel(
    capacity, cotangent, ids, place_column, middle, normed, probs, *rest
):
    *row_refs, output, grad_logits, grad_router = rest
    rows, expert_count = probs.shape
    slots = 2 * row_refs[1].shape[0]
    slot_range = lax.broadcasted_iota(jnp.int32, (rows, slots), 1)
    dispatch = low(slot_range == place_column[...])
    routed = dot_plain(dispatch, gather_slots(row_refs, capacity))
    chances = probs[...]
    hot = one_hot_experts(ids[...], expert_count)
    gate = jnp.sum(jnp.where(hot, chances, 0.0), axis=1, keepdims=True)
    output[...] = low(middle[...] + gate * routed)
    grad_gate = jnp.sum(cotangent[...].astype(F32) * routed, axis=1, keepdims=True)
    logits = low((grad_gate * gate) * (hot.astype(F32) - chances))
    grad_logits[...] = logits
    grad_router[...] = dot_plain(logits.T, normed[...])


def made_rows(cotangent, ids, place, middle, normed, probs, row_slots):
    rows, width = middle.shape
    expert_count = probs.shape[1]
    capacity = row_slots[1].shape[0] // (len(row_slots) - 1)
    inputs = [cotangent, ids, place[:, None], middle, normed, probs, *row_slots]
    return pl.pallas_call(
        functools.partial(made_kernel, capacity),
        out_shape=(
            shape((rows, width)),
            shape((rows, expert_count)),
            shape((expert_count, width), F32),
        ),
        in_specs=[VM] * len(inputs),
        out_specs=(VM,) * 3,
        compiler_params=ROOM,
        name="made_rows",
    )(*inputs)


def back_kernel(
    parts, capacity, cotangent, gains, router, place_column, middle, grad_logits, *rest
):
    proj, rest = rest[:parts], rest[parts:]
    *grad_refs, grad_middle, grad_split, gain_two = rest[: -parts]
    near = rest[-parts:]
    rows = middle.shape[0]
    slots = 2 * grad_refs[1].shape[0]
    slot_range = lax.broadcasted_iota(jnp.int32, (rows, slots), 1)
    dispatch = low(slot_range == place_column[...])
    grad_second = dot_plain(dispatch, gather_slots(grad_refs, capacity))
    grad_second = grad_second + dot_last(grad_logits[...], router[...])
    unit, factor = rms_unit(middle[...])
    total = cotangent[...].astype(F32) + rms_backward(grad_second, unit, factor, gains[1:2, :])
    grad_low = split_order(low(total))
    for place in range(parts):
        near[place][...] = low(dot_last(proj[place][...], grad_low))
    grad_middle[...] = total
    grad_split[...] = grad_low
    summed = jnp.sum(grad_second * unit, axis=0, keepdims=True)
    gain_two[...] = jnp.broadcast_to(summed, gain_two.shape)


def back_rows(cotangent, gains, router, place, middle, grad_logits, proj, grad_slots):
    rows, width = middle.shape
    parts = len(proj)
    capacity = grad_slots[1].shape[0] // (len(grad_slots) - 1)
    inputs = [cotangent, gains, router, place[:, None], middle, grad_logits, *proj, *grad_slots]
    return pl.pallas_call(
        functools.partial(back_kernel, parts, capacity),
        out_shape=(
            shape((rows, width), F32),
            shape((rows, width)),
            shape((8, width), F32),
            *([shape((proj[0].shape[0], rows))] * parts),
        ),
        in_specs=[VM] * len(inputs),
        out_specs=(VM,) * (3 + parts),
        compiler_params=ROOM,
        name="back_rows",
    )(*inputs)


def proj_grad_kernel(grad_rows, *rest):
    *attended, keep, send = rest
    for place, one in enumerate(attended):
        part = dot_plain(one[...], grad_rows[...])
        if place % 2:
            send[place // 2] = low(part)
        else:
            keep[place // 2] = part


def proj_grad(grad_rows, attended):
    dims = (len(attended) // 2, attended[0].shape[0], grad_rows.shape[1])
    return pl.pallas_call(
        proj_grad_kernel,
        out_shape=(shape(dims, F32), shape(dims)),
        in_specs=[VM] * (1 + len(attended)),
        out_specs=(VM,) * 2,
        compiler_params=ROOM,
        name="proj_grad",
    )(grad_rows, *attended)


def expert_up_kernel(capacity, *refs):
    *parts, up, hidden, slope, rows_flip, rows = refs

    @pl.when(pl.program_id(0) == 0)
    def _():
        arrived = gather_slots(parts, capacity)
        rows[...] = arrived
        rows_flip[...] = arrived.T

    pre = dot_plain(rows[...], up[...])
    square = pre * pre
    bend = jnp.tanh(ROOT * (pre + CUBE * (square * pre)))
    half = 0.5 * (1.0 + bend)
    hidden[...] = low(pre * half)
    bent = (0.5 * ROOT) * pre * (1.0 - bend * bend) * (1.0 + (3.0 * CUBE) * square)
    slope[...] = low(half + bent)


def expert_out_kernel(hidden, down, even, odd):
    part = low(dot_plain(hidden[...], down[...]))

    @pl.when(pl.program_id(0) < 2)
    def _():
        even[...] = part

    @pl.when(pl.program_id(0) >= 2)
    def _():
        odd[...] = part


def expert_down_kernel(capacity, *refs):
    *parts, hidden, grad_down, grads, grads_flip = refs

    @pl.when(pl.program_id(0) == 0)
    def _():
        arrived = gather_slots(parts, capacity)
        grads[...] = arrived
        grads_flip[...] = arrived.T

    grad_down[...] = low(dot_plain(grads_flip[...], hidden[...]))


def expert_back_kernel(grads, slope, rows_flip, up, down, even, odd, grad_up, total):
    step = pl.program_id(0)
    grad_pre = low(dot_last(grads[...], down[...]) * slope[...].astype(F32))
    grad_up[...] = low(dot_plain(rows_flip[...], grad_pre))
    part = dot_last(grad_pre, up[...])

    @pl.when(step == 0)
    def _():
        total[...] = part

    @pl.when(step > 0)
    def _():
        total[...] += part

    @pl.when(step == pl.num_programs(0) - 1)
    def _():
        half = even.shape[0]
        even[...] = low(total[:half])
        odd[...] = low(total[half:])


def whole_spec(dims):
    return pl.BlockSpec(dims, lambda at: (0, 0))


def column_spec(rows):
    return pl.BlockSpec((rows, UNITS), lambda at: (0, at))


def row_spec(width):
    return pl.BlockSpec((UNITS, width), lambda at: (at, 0))


def expert_cost(products, slots, width, units):
    return pl.CostEstimate(
        flops=2 * products * slots * width * units,
        bytes_accessed=4 * slots * units + 2 * products * width * units,
        transcendentals=slots * units,
    )


def expert_hidden(parts, up):
    width, units = up.shape
    half = parts[1].shape[0]
    slots = 2 * half
    return pl.pallas_call(
        functools.partial(expert_up_kernel, half // (len(parts) - 1)),
        grid=(units // UNITS,),
        in_specs=[whole_spec(one.shape) for one in parts] + [column_spec(width)],
        out_specs=(column_spec(slots), column_spec(slots), whole_spec((width, slots))),
        out_shape=(shape((slots, units)), shape((slots, units)), shape((width, slots))),
        scratch_shapes=[pltpu.VMEM((slots, width), BF16)],
        compiler_params=ROOM,
        cost_estimate=expert_cost(1, slots, width, units),
        name="expert_hidden",
    )(*parts, up)


def expert_out(hidden, down):
    slots, units = hidden.shape
    width = down.shape[1]
    return pl.pallas_call(
        expert_out_kernel,
        grid=(4,),
        in_specs=[
            pl.BlockSpec((slots // 4, units), lambda at: (at, 0)),
            pl.BlockSpec((units, width), lambda at: (0, 0), pipeline_mode=pl.Buffered(1)),
        ],
        out_specs=(
            pl.BlockSpec((slots // 4, width), lambda at: (jnp.minimum(at, 1), 0)),
            pl.BlockSpec((slots // 4, width), lambda at: (jnp.maximum(at - 2, 0), 0)),
        ),
        out_shape=(shape((slots // 2, width)), shape((slots // 2, width))),
        compiler_params=ROOM,
        cost_estimate=expert_cost(1, slots, width, units),
        name="expert_out",
    )(hidden, down)


def expert_down_grad(parts, hidden):
    slots, units = hidden.shape
    half, width = parts[1].shape
    return pl.pallas_call(
        functools.partial(expert_down_kernel, half // (len(parts) - 1)),
        grid=(units // UNITS,),
        in_specs=[whole_spec(one.shape) for one in parts] + [column_spec(slots)],
        out_specs=(column_spec(width), whole_spec((slots, width))),
        out_shape=(shape((width, units)), shape((slots, width))),
        scratch_shapes=[pltpu.VMEM((width, slots), BF16)],
        compiler_params=ROOM,
        cost_estimate=expert_cost(1, slots, width, units),
        name="expert_down_grad",
    )(*parts, hidden)


def expert_back(grads, slope, rows_flip, up, down):
    slots, units = slope.shape
    width = grads.shape[1]
    block = whole_spec((slots // 2, width))
    return pl.pallas_call(
        expert_back_kernel,
        grid=(units // UNITS,),
        in_specs=[
            whole_spec(grads.shape),
            column_spec(slots),
            whole_spec(rows_flip.shape),
            column_spec(width),
            row_spec(width),
        ],
        out_specs=(block, block, column_spec(width)),
        out_shape=(
            shape((slots // 2, width)),
            shape((slots // 2, width)),
            shape((width, units)),
        ),
        scratch_shapes=[pltpu.VMEM((slots, width), F32)],
        compiler_params=ROOM,
        cost_estimate=expert_cost(3, slots, width, units),
        name="expert_back",
    )(grads, slope, rows_flip, up, down)


def shards(
    tokens,
    cotangent,
    gains,
    qkv_weight,
    proj_weight,
    router_weight,
    expert_up,
    expert_down,
    expert_ids,
    slot_order,
    segment_ids,
):
    dp_count, ctx_count, tp_count = (lax.axis_size(name) for name in ("dp", "ctx", "tp"))
    dp_index, ctx_index, tp_index = (lax.axis_index(name) for name in ("dp", "ctx", "tp"))
    group = dp_count * tp_count
    group_index = dp_index * tp_count + tp_index
    tok_dev, width = tokens.shape
    half_rows = tok_dev // 2
    expert_count = router_weight.shape[1]
    capacity = 5 * tok_dev // (4 * expert_count)
    slots = expert_count * capacity
    per = PLEN // ctx_count // CHUNK
    conts_here = segment_ids.shape[0]
    prompts_here = conts_here * ctx_count // CONTS
    local_width = qkv_weight.shape[2]
    shard_rows = qkv_weight.shape[1]
    side, core = tp_index >> 1, tp_index & 1

    def across(value):
        return xor_swap(value, "tp", tp_count, 2)

    def beside(value):
        return xor_swap(value, "tp", tp_count, 1)

    packed = jnp.concatenate(
        [
            qkv_weight.transpose(1, 0, 2).reshape(shard_rows, 3 * local_width),
            proj_weight.T,
            router_weight,
        ],
        axis=1,
    )
    by_ctx = xor_exchange([packed] * ctx_count, "ctx", ctx_count)
    own, own_second = normalize(tokens, gains)
    far_second = across(own_second)
    carried = jnp.where(side == 0, own[:half_rows], far_second)
    by_ctx, carried = lax.optimization_barrier((by_ctx, carried))
    by_dp = xor_gather(jnp.stack(by_ctx), "dp", dp_count)
    far_first = across(own[:half_rows])
    arrived = ring_step(carried, "ctx", ctx_count, 1)
    arrived, far_first, by_dp = lax.optimization_barrier((arrived, far_first, by_dp))
    rows = [own, beside(own), far_first, far_second, beside(far_first), beside(far_second)]
    local_count = len(rows)

    by_dp = jnp.stack(by_dp).reshape((-1,) + packed.shape)
    shard_index = dp_index * ctx_count + ctx_index
    weights = jnp.concatenate(
        [pick(by_dp, shard_index ^ place) for place in range(dp_count * ctx_count)], axis=0
    )
    query_weight = weights[:, :local_width]
    pair_weight = weights[:, local_width : 3 * local_width]
    router = weights[:, 4 * local_width :]

    query, local = project_local(query_weight, pair_weight, rows)
    remote = []
    blocks = []
    for place in range(1, ctx_count):
        other = across(arrived)
        if place < ctx_count - 1:
            following = ring_step(arrived, "ctx", ctx_count, 1)
            if place == 1:
                expert_up, expert_down, following = lax.optimization_barrier(
                    (expert_up, expert_down, following)
                )
                full_up = lax.all_gather(expert_up, "ctx", axis=2, tiled=True)[0]
                full_down = lax.all_gather(expert_down, "ctx", axis=1, tiled=True)[0]
            if place == ctx_count - 2:
                following, query, local = lax.optimization_barrier((following, query, local))
            following, other = lax.optimization_barrier((following, other))
        blocks.append([arrived, other, beside(arrived), beside(other)])
        arrived = following
    rows += [one for block in blocks for one in block]
    remote = [project_remote(pair_weight, block) for block in blocks]
    proj_part, _ = lax.optimization_barrier(
        (weights[:, 3 * local_width : 4 * local_width].T, blocks[-1][1])
    )
    proj = xor_gather(proj_part, "tp", tp_count, [2, 1])

    device_chunks = tok_dev // CHUNK

    def split_place(at):
        return (at % 2) * (device_chunks // 2) + at // 2

    at = jnp.arange(prompts_here * per)
    owner, inside = at // device_chunks, at % device_chunks
    local_at = (owner ^ tp_index) * device_chunks + split_place(inside)
    remote_at = ((owner ^ core) * 2 + ((inside % 2) ^ side)) * (device_chunks // 2) + inside // 2
    prompt_at = jnp.concatenate(
        [local_at.reshape(prompts_here, per), remote_at.reshape(prompts_here, per)], axis=1
    )
    at = jnp.arange(conts_here)
    cont_at = ((2 + at // device_chunks) ^ tp_index) * device_chunks + split_place(
        at % device_chunks
    )
    info = jnp.concatenate([ctx_index[None], prompt_at.reshape(-1), cont_at, segment_ids])
    info = info.astype(jnp.int32)
    sizes = (prompts_here, conts_here, ctx_count, per)

    *attended, lse_prompt, lse_cont = attend_forward(sizes, info, query, local, remote)
    mixed = attended
    attended = xor_exchange(attended, "tp", tp_count)
    place = slot_places(expert_ids[:, 0], slot_order[0], group_index, expert_count, capacity)

    def start_exchange(odd):
        return xor_swap(odd, ("dp", "tp"), group, 1)

    def finish_exchange(even, other):
        moved = [even, other]
        for at in range(1, group // 2):
            block = slice(at * capacity, (at + 1) * capacity)
            pair = jnp.concatenate([even[block], other[block]], axis=0)
            moved.append(xor_swap(pair, ("dp", "tp"), group, 2 * at))
        return moved

    even_rows, odd_rows, even_grads, odd_grads, middle, normed_two, probs = middle_rows(
        tokens, cotangent, gains, router, expert_ids, place, slots, attended, proj
    )
    row_slots = finish_exchange(even_rows, start_exchange(odd_rows))
    other_grads = start_exchange(odd_grads)
    row_slots, even_grads, other_grads = lax.optimization_barrier(
        (row_slots, even_grads, other_grads)
    )
    grad_slots = finish_exchange(even_grads, other_grads)
    hidden, slope, rows_flip = expert_hidden(row_slots, full_up)
    grad_down, arrived_grads = expert_down_grad(grad_slots, hidden)
    hidden, arrived_grads = lax.optimization_barrier((hidden, arrived_grads))
    even, odd = expert_out(hidden, full_down)
    even, other, slope = lax.optimization_barrier((even, start_exchange(odd), slope))
    made_slots = finish_exchange(even, other)
    even, odd, grad_up = expert_back(arrived_grads, slope, rows_flip, full_up, full_down)
    even, odd, made_slots, grad_up = lax.optimization_barrier((even, odd, made_slots, grad_up))
    back_slots = finish_exchange(even, start_exchange(odd))
    grad_down = lax.psum_scatter(grad_down, "ctx", scatter_dimension=1, tiled=True)
    grad_down = grad_down.T.astype(F32)[None]
    grad_up = lax.psum_scatter(grad_up, "ctx", scatter_dimension=1, tiled=True).astype(F32)[None]

    output, grad_logits, router_part = made_rows(
        cotangent, expert_ids, place, middle, normed_two, probs, made_slots
    )
    grad_middle, grad_split, gain_two, *grad_near = back_rows(
        cotangent, gains, router, place, middle, grad_logits, proj, back_slots
    )
    grad_near = xor_exchange(grad_near, "tp", tp_count)
    proj_keep, proj_send = proj_grad(grad_split, attended)
    grad_near, proj_keep, proj_send = lax.optimization_barrier((grad_near, proj_keep, proj_send))
    grad_query, grad_local, *grads = attend_backward(
        sizes,
        info,
        query,
        lse_prompt,
        lse_cont,
        local,
        remote,
        query_weight,
        pair_weight,
        grad_near,
        mixed,
    )
    count = ctx_count - 1
    grad_remote, (*remote_rows, local_keep, local_send) = grads[:count], grads[count:]
    if remote_rows:
        remote_rows = list(zip(remote_rows[:count], remote_rows[count:]))
    else:
        remote_rows = [rows_remote(one, pair_weight) for one in grad_remote]

    remote_rows = remote_rows[::-1]

    def chip_rows(keep, send):
        chip = keep.astype(F32) + beside(send).astype(F32)
        return chip[:half_rows], low(chip[half_rows:])

    def scatter_sum(values, axis, size, me):
        parts = xor_exchange([pick(values, me ^ k) for k in range(size)], axis, size)
        return add_all([piece.astype(F32) for piece in parts])

    piece, message = chip_rows(*remote_rows[0])
    following = chip_rows(*remote_rows[1])
    near = across(message)
    grad_pairs, message = lax.optimization_barrier(([grad_local, *grad_remote], message))
    qkv_part = qkv_grad(grad_query, grad_pairs, rows)
    near, qkv_part, following, local_send, proj_send, remote_rows[2:] = lax.optimization_barrier(
        (near, qkv_part, following, local_send, proj_send, remote_rows[2:])
    )
    running = low(piece + near.astype(F32))
    for place in range(1, count):
        piece, message = following
        message, running = lax.optimization_barrier((message, running))
        moved = ring_step(running, "ctx", ctx_count, -1)
        near = across(message)
        if place < count - 1:
            following = chip_rows(*remote_rows[place + 1])
        if place == 1:
            local_send = beside(local_send)
            far_message = low(local_keep[0].astype(F32) + local_send[0].astype(F32))
            first_rows = (tok_dev - local_width) // 2
            proj_chip = proj_keep + beside(proj_send).astype(F32)
            far_first = jnp.concatenate([low(proj_chip[1]), far_message[:first_rows]], axis=0)
            near, far_first = lax.optimization_barrier((near, far_first))
            far_first = across(far_first)
            moved, near, far_first, following = lax.optimization_barrier(
                (moved, near, far_first, following)
            )
            proj_sum = proj_chip[0] + far_first[:local_width].astype(F32)
            early = jnp.concatenate([low(proj_sum), low(router_part), low(gain_two[:1])], axis=0)
            packed = jnp.concatenate([qkv_part, early.T], axis=1)
            packed = packed.reshape(dp_count, ctx_count, shard_rows, -1)
        if place == count - 1:
            summed = low(scatter_sum(packed, "dp", dp_count, dp_index))
            near, far_second = lax.optimization_barrier((near, far_message[first_rows:]))
            far_second = across(far_second)
            moved, near, summed, grad_up, grad_down = lax.optimization_barrier(
                (moved, near, summed, grad_up, grad_down)
            )
        running = low(piece + near.astype(F32) + moved.astype(F32))
    running, summed = lax.optimization_barrier((running, summed))
    hops = [[], []]
    for ctx_from in range(ctx_count):
        for tp_from in range(tp_count):
            target = (ctx_from - 1) % ctx_count * tp_count + (tp_from & 1)
            hops[tp_from >> 1].append((ctx_from * tp_count + tp_from, target))
    own_rows, other_rows = (lax.ppermute(running, ("ctx", "tp"), hop) for hop in hops)
    summed = scatter_sum(summed, "ctx", ctx_count, ctx_index)
    grad_tokens = final_rows(
        side.astype(jnp.int32).reshape(1),
        tokens,
        gains,
        grad_middle,
        local_keep,
        local_send,
        far_first,
        far_second,
        own_rows,
        other_rows,
    )

    qkv_width = 3 * local_width
    grad_qkv = summed[:, :qkv_width].reshape(shard_rows, 3, local_width).transpose(1, 0, 2)
    grad_proj = summed[:, qkv_width : qkv_width + local_width].T
    gain_range = lax.dynamic_slice_in_dim(gains[0], shard_index * shard_rows, shard_rows)
    gain_one = jnp.sum(qkv_weight.astype(F32) * grad_qkv, axis=(0, 2))
    small = jnp.concatenate([summed[:, qkv_width + local_width :], gain_one[:, None]], axis=1)
    parts = xor_exchange([low(small)] * tp_count, "tp", tp_count)
    parts, grad_tokens = lax.optimization_barrier((parts, grad_tokens))
    small = small + add_all([part.astype(F32) for part in parts[1:]])
    grad_router = small[:, :expert_count]
    grad_gains = jnp.stack([small[:, expert_count + 1] / gain_range, small[:, expert_count]])
    return (output, grad_tokens, grad_gains, grad_qkv, grad_proj, grad_router, grad_up, grad_down)


def solution(mesh):
    in_specs = (
        P(("dp", "ctx", "tp"), None),
        P(("dp", "ctx", "tp"), None),
        P(),
        P(None, ("dp", "ctx"), "tp"),
        P("tp", ("dp", "ctx")),
        P(("dp", "ctx"), None),
        P(("dp", "tp"), None, "ctx"),
        P(("dp", "tp"), "ctx", None),
        P(("dp", "ctx", "tp"), None),
        P(("dp", "ctx", "tp"), None),
        P(("dp", "ctx")),
    )
    out_specs = (
        P(("dp", "ctx", "tp"), None),
        P(("dp", "ctx", "tp"), None),
        P(None, ("dp", "ctx")),
        P(None, ("dp", "ctx"), "tp"),
        P("tp", ("dp", "ctx")),
        P(("dp", "ctx"), None),
        P(("dp", "tp"), None, "ctx"),
        P(("dp", "tp"), "ctx", None),
    )
    return jax.shard_map(shards, mesh=mesh, in_specs=in_specs, out_specs=out_specs, check_vma=False)
```

```python
import functools

import jax
import jax.numpy as jnp
from jax import lax
from jax.experimental import pallas as pl
from jax.experimental.pallas import tpu as pltpu
from jax.sharding import PartitionSpec as P

HD = 64
PLEN = 1024
CLEN = 128
CONTS = 8
CHUNK = 128
UNITS = 768

EPSILON = 1e-06
NEGATIVE = -1e30
ROOT = 0.7978845608028654
CUBE = 0.044715
F32 = jnp.float32
BF16 = jnp.bfloat16
VM = pl.BlockSpec(memory_space=pltpu.VMEM)
SM = pl.BlockSpec(memory_space=pltpu.SMEM)
ROOM = pltpu.CompilerParams(vmem_limit_bytes=60 * 2**20)


def shape(dims, dtype=BF16):
    return jax.ShapeDtypeStruct(dims, dtype)


def low(value):
    return value.astype(BF16)


def dot_last(left, right):
    return lax.dot_general(left, right, (((1,), (1,)), ((), ())), preferred_element_type=F32)


def dot_plain(left, right):
    return lax.dot_general(left, right, (((1,), (0,)), ((), ())), preferred_element_type=F32)


def add_all(parts):
    return functools.reduce(jnp.add, parts)


def xor_swap(value, axis, size, mask):
    return lax.ppermute(value, axis, [(place, place ^ mask) for place in range(size)])


def ring_step(value, axis, size, shift):
    return lax.ppermute(value, axis, [(place, (place + shift) % size) for place in range(size)])


def pick(stacked, index):
    return lax.dynamic_index_in_dim(stacked, index, 0, keepdims=False)


def xor_gather(value, axis, size, order=None):
    if order is None:
        order = [1 << bit for bit in range(size.bit_length() - 1)]
    have = {0: value}
    for mask in order:
        keys = sorted(have)
        moved = xor_swap(jnp.stack([have[key] for key in keys]), axis, size, mask)
        for place, key in enumerate(keys):
            have[key ^ mask] = moved[place]
    return [have[key] for key in range(size)]


def xor_exchange(pieces, axis, size):
    return [pieces[0]] + [xor_swap(pieces[mask], axis, size, mask) for mask in range(1, size)]


def chunk_list(value, axis):
    return [
        lax.slice_in_dim(value, first, first + CHUNK, axis=axis)
        for first in range(0, value.shape[axis], CHUNK)
    ]


def split_order(value, axis=0):
    parts = chunk_list(value, axis)
    return jnp.concatenate(parts[0::2] + parts[1::2], axis=axis)


def plain_order(value, axis=0):
    parts = chunk_list(value, axis)
    half = len(parts) // 2
    return jnp.concatenate([parts[(at % 2) * half + at // 2] for at in range(2 * half)], axis=axis)


def rms_unit(values):
    factor = lax.rsqrt(jnp.mean(values * values, axis=-1, keepdims=True) + EPSILON)
    return (values * factor, factor)


def rms_backward(grad_normed, unit_part, factor, gain):
    scaled = grad_normed * gain
    inner = jnp.mean(scaled * unit_part, axis=-1, keepdims=True)
    return factor * (scaled - unit_part * inner)


def normalize_kernel(tokens, gains, own, second):
    unit, _ = rms_unit(tokens[...].astype(F32))
    own[...] = split_order(low(gains[0:1, :] * unit))
    second[...] = own[own.shape[0] // 2 :, :]


def normalize(tokens, gains):
    rows, width = tokens.shape
    return pl.pallas_call(
        normalize_kernel,
        out_shape=(shape((rows, width)), shape((rows // 2, width))),
        in_specs=[VM] * 2,
        out_specs=(VM,) * 2,
        compiler_params=ROOM,
        name="normalize",
    )(tokens, gains)


def key_lanes(rows, width):
    return rows[:, : width + (-width) % 128]


def value_lanes(rows, width):
    return rows[:, width - (-width) % 128 :]


def spread_heads(columns, ahead, behind):
    width, count = columns.shape
    groups = []
    for first in range(0, width, HD):
        pieces = [columns[first : first + HD]]
        above, below = ahead + first, width - first - HD + behind
        if above:
            pieces.insert(0, jnp.zeros((above, count), columns.dtype))
        if below:
            pieces.append(jnp.zeros((below, count), columns.dtype))
        groups.append(jnp.concatenate(pieces, axis=0))
    return jnp.concatenate(groups, axis=1)


def causal(scores, count):
    key_row = lax.broadcasted_iota(jnp.int32, scores.shape, 0)
    query_row = lax.broadcasted_iota(jnp.int32, scores.shape, 1) % count
    return jnp.where(key_row <= query_row, scores, NEGATIVE)


def work_items(info, sizes, attend):
    prompts, conts, places, per = sizes
    ctx_index = info[0]

    def prompt_chunks(prompt):
        first = 1 + prompt * 2 * per
        return [info[first + at] for at in range(per)], [info[first + per + at] for at in range(per)]

    def prompt_mask(scores):
        count = per * CHUNK
        parts = [causal(scores[:count], count)]
        for place in range(1, places):
            part = scores[place * count : (place + 1) * count]
            parts.append(jnp.where(place <= ctx_index, part, NEGATIVE))
        return jnp.concatenate(parts, axis=0)

    def cont_mask(scores):
        return jnp.concatenate([causal(scores[:CLEN], CLEN), scores[CLEN:]], axis=0)

    @pl.loop(0, prompts, unroll=2)
    def _(prompt):
        own, far = prompt_chunks(prompt)
        attend(0, prompt, own, own, far, prompt_mask)

    first = 1 + prompts * 2 * per

    @pl.loop(0, conts, unroll=2)
    def _(cont):
        own = [info[first + cont]]
        near, far = prompt_chunks(info[first + conts + cont])
        attend(1, cont, own, own + near, far, cont_mask)


def chunk_lanes(chunk):
    return pl.ds(pl.multiple_of(chunk * CHUNK, CHUNK), CHUNK)


def load_lanes(ref, chunks):
    return jnp.concatenate([ref[:, chunk_lanes(chunk)] for chunk in chunks], axis=1)


def project_local_kernel(query_weight, pair_weight, *rest):
    *rows, query, pairs = rest
    width = query.shape[0]
    query_flip = query_weight[...].T
    at = 0
    for one in rows:
        value = one[...]
        count = value.shape[0]
        pair = low(dot_plain(value, pair_weight[...]))
        pairs[at // CHUNK : (at + count) // CHUNK] = pair.reshape(-1, CHUNK, 2 * width)
        query[:, at : at + count] = low(dot_last(query_flip, value) * 0.125)
        at += count


def project_remote_kernel(pair_weight, *rest):
    *rows, pairs = rest
    at = 0
    for one in rows:
        count = one.shape[0]
        pair = low(dot_plain(one[...], pair_weight[...]))
        pairs[at // CHUNK : (at + count) // CHUNK] = pair.reshape(-1, CHUNK, pairs.shape[2])
        at += count


def project_local(query_weight, pair_weight, rows):
    count = sum(one.shape[0] for one in rows)
    wide = pair_weight.shape[1]
    return pl.pallas_call(
        project_local_kernel,
        out_shape=(shape((query_weight.shape[1], count)), shape((count // CHUNK, CHUNK, wide))),
        in_specs=[VM] * (2 + len(rows)),
        out_specs=(VM,) * 2,
        compiler_params=ROOM,
        cost_estimate=pl.CostEstimate(
            flops=3 * count * pair_weight.size, bytes_accessed=10**7, transcendentals=0
        ),
        name="project_local",
    )(query_weight, pair_weight, *rows)


def project_remote(pair_weight, rows):
    count = sum(one.shape[0] for one in rows)
    return pl.pallas_call(
        project_remote_kernel,
        out_shape=shape((count // CHUNK, CHUNK, pair_weight.shape[1])),
        in_specs=[VM] * (1 + len(rows)),
        out_specs=VM,
        compiler_params=ROOM,
        cost_estimate=pl.CostEstimate(
            flops=2 * count * pair_weight.size, bytes_accessed=4 * 10**6, transcendentals=0
        ),
        name="project_remote",
    )(pair_weight, *rows)


def load_block(local, remote, near, far):
    blocks = [local[chunk] for chunk in near]
    blocks += [one[chunk] for one in remote for chunk in far]
    return jnp.concatenate(blocks, axis=0)


def attend_forward_kernel(sizes, info, query, local, *rest):
    remote, (*outs, lse_prompt, lse_cont, mixed) = rest[: sizes[2] - 1], rest[sizes[2] - 1 :]
    lse = (lse_prompt, lse_cont)
    width = query.shape[0]
    pad = (-width) % 128

    def attend(kind, index, own, near, far, mask):
        count = len(own) * CHUNK
        block = load_block(local, remote, near, far)
        spread = spread_heads(load_lanes(query, own), 0, pad)
        scores = mask(dot_plain(key_lanes(block, width), spread))
        peak = jnp.max(scores, axis=0, keepdims=True)
        shifted = jnp.exp(scores - peak)
        total = jnp.sum(shifted, axis=0, keepdims=True)
        weights = low(shifted)
        flip = value_lanes(block, width).T
        for head in range(width // HD):
            group = slice(head * count, (head + 1) * count)
            part = slice(pad + head * HD, pad + (head + 1) * HD)
            result = low(dot_plain(flip[part], weights[:, group]) / total[:, group])
            for place, chunk in enumerate(own):
                mixed[head * HD : (head + 1) * HD, chunk_lanes(chunk)] = result[
                    :, place * CHUNK : (place + 1) * CHUNK
                ]
        lse[kind][index] = peak + jnp.log(total)

    work_items(info, sizes, attend)
    each = outs[0].shape[1]
    for place, out in enumerate(outs):
        out[...] = mixed[:, place * each : (place + 1) * each]


def attend_backward_kernel(sizes, info, query, lse_prompt, lse_cont, local, *rest):
    count_remote = sizes[2] - 1
    remote, rest = rest[:count_remote], rest[count_remote:]
    query_weight, pair_weight, *rest = rest
    grads, mixed, rest = rest[:4], rest[4:8], rest[8:]
    grad_query, grad_local, *rest, grad, centre, sum_local, sum_remote = rest
    grad_remote, rest = rest[:count_remote], rest[count_remote:]
    *rest, keep_local, send_local = rest
    keep_remote, send_remote = rest[: len(rest) // 2], rest[len(rest) // 2 :]
    lse = (lse_prompt, lse_cont)
    width = query.shape[0]
    pad = (-width) % 128
    each = grads[0].shape[1]
    for place, (one, result) in enumerate(zip(grads, mixed)):
        columns = slice(place * each, (place + 1) * each)
        grad[:, columns] = one[...]
        product = one[...].astype(F32) * result[...].astype(F32)
        for head in range(width // HD):
            centre[head : head + 1, columns] = jnp.sum(
                product[head * HD : (head + 1) * HD], axis=0, keepdims=True
            )

    def attend(kind, index, own, near, far, mask):
        count = len(own) * CHUNK
        block = load_block(local, remote, near, far)
        query_spread = spread_heads(load_lanes(query, own), 0, pad)
        grad_spread = spread_heads(load_lanes(grad, own), pad, 0)
        keys = key_lanes(block, width)
        weights = jnp.exp(mask(dot_plain(keys, query_spread)) - lse[kind][index])
        slopes = dot_plain(value_lanes(block, width), grad_spread)
        middle = load_lanes(centre, own)
        middle = jnp.concatenate([middle[head : head + 1] for head in range(width // HD)], axis=1)
        grad_scores = low(weights * (slopes - middle))
        flip = keys.T
        for head in range(width // HD):
            group = slice(head * count, (head + 1) * count)
            part = slice(head * HD, (head + 1) * HD)
            result = low(dot_plain(flip[part], grad_scores[:, group]) * 0.125)
            for place, chunk in enumerate(own):
                grad_query[part, chunk_lanes(chunk)] = result[
                    :, place * CHUNK : (place + 1) * CHUNK
                ]
        key_part = dot_last(grad_scores, query_spread)
        value_part = dot_last(low(weights), grad_spread)
        if pad:
            edge = width - pad
            shared = key_part[:, edge:] + value_part[:, : 2 * pad]
            joined = [key_part[:, :edge], shared, value_part[:, 2 * pad :]]
        else:
            joined = [key_part, value_part]
        result = jnp.concatenate(joined, axis=1)
        spots = [(sum_local, chunk) for chunk in near]
        spots += [(sum_remote.at[place], chunk) for place in range(count_remote) for chunk in far]
        for at, (sums, chunk) in enumerate(spots):
            part = result[at * CHUNK : (at + 1) * CHUNK]
            if kind == 0 or at == 0:
                sums[chunk] = part
            else:
                sums[chunk] += part

    work_items(info, sizes, attend)

    half = remote[0].shape[0] // 2
    for place in range(count_remote):
        for side, outs in enumerate((keep_remote, send_remote)):
            chunks = slice(side * half, (side + 1) * half)
            part = low(sum_remote[place, chunks])
            grad_remote[place][chunks] = part
            if outs:
                flat = part.reshape(half * CHUNK, 2 * width)
                outs[place][...] = low(dot_last(flat, pair_weight[...]))
    for at, out in enumerate((keep_local.at[1], send_local.at[1], keep_local.at[0], send_local.at[0])):
        chunks = slice(at * half, (at + 1) * half)
        part = low(sum_local[chunks])
        grad_local[chunks] = part
        flat = part.reshape(half * CHUNK, 2 * width)
        part = grad_query[:, at * each : (at + 1) * each].T
        out[...] = low(dot_last(flat, pair_weight[...]) + dot_last(part, query_weight[...]))


def attend_cost(factor, sizes, heads):
    prompts, conts, places, per = sizes
    scores = heads * places * per * CHUNK * CHUNK * (prompts * per + conts)
    return pl.CostEstimate(flops=factor * HD * scores, bytes_accessed=10**7, transcendentals=scores)


def attend_forward(sizes, info, query, local, remote):
    prompts, conts, places, per = sizes
    width, local_rows = query.shape
    heads = width // HD
    return pl.pallas_call(
        functools.partial(attend_forward_kernel, sizes),
        out_shape=(
            *([shape((width, local_rows // 4))] * 4),
            shape((prompts, 1, heads * per * CHUNK), F32),
            shape((conts, 1, heads * CLEN), F32),
        ),
        in_specs=[SM] + [VM] * (2 + len(remote)),
        out_specs=(VM,) * 6,
        scratch_shapes=[pltpu.VMEM((width, local_rows), BF16)],
        compiler_params=ROOM,
        cost_estimate=attend_cost(16, sizes, heads),
        name="attend_forward",
    )(info, query, local, *remote)


def attend_backward(
    sizes, info, query, lse_prompt, lse_cont, local, remote, query_weight, pair_weight, grads, mixed
):
    pairs = [local] + list(remote)
    remote_rows = 2 * len(remote) if len(remote) <= 4 else 0
    each = shape((grads[0].shape[1], query_weight.shape[0]))
    both = shape((2,) + each.shape)
    count = len(remote)
    return pl.pallas_call(
        functools.partial(attend_backward_kernel, sizes),
        out_shape=(
            shape(query.shape),
            *(shape(one.shape) for one in pairs),
            *([each] * remote_rows),
            both,
            both,
        ),
        in_specs=[SM] + [VM] * (5 + len(pairs) + 2 * len(grads)),
        out_specs=(VM,) * (3 + len(pairs) + remote_rows),
        scratch_shapes=[
            pltpu.VMEM(query.shape, BF16),
            pltpu.VMEM((8, query.shape[1]), F32),
            pltpu.VMEM(local.shape, F32),
            pltpu.VMEM((count,) + remote[0].shape, F32),
        ],
        compiler_params=ROOM,
        cost_estimate=attend_cost(40, sizes, query.shape[0] // HD),
        name="attend_backward",
    )(info, query, lse_prompt, lse_cont, *pairs, query_weight, pair_weight, *grads, *mixed)


def rows_remote_kernel(grad_pairs, pair_weight, keep, send):
    half = grad_pairs.shape[0] // 2
    wide = grad_pairs.shape[2]
    send[...] = low(dot_last(grad_pairs[half:].reshape(half * CHUNK, wide), pair_weight[...]))
    keep[...] = low(dot_last(grad_pairs[:half].reshape(half * CHUNK, wide), pair_weight[...]))


def rows_remote(grad_pairs, pair_weight):
    dims = (grad_pairs.shape[0] // 2 * CHUNK, pair_weight.shape[0])
    return pl.pallas_call(
        rows_remote_kernel,
        in_specs=[VM] * 2,
        out_specs=(VM,) * 2,
        out_shape=(shape(dims), shape(dims)),
        compiler_params=ROOM,
        cost_estimate=pl.CostEstimate(
            flops=4 * dims[0] * pair_weight.size, bytes_accessed=6 * 10**6, transcendentals=0
        ),
        name="rows_remote",
    )(grad_pairs, pair_weight)


def qkv_grad_kernel(places, grad_query, *rest):
    pairs, rows, out = rest[:places], rest[places:-1], rest[-1]
    width, local_rows = grad_query.shape
    total_query = total_pair = None
    spots = [(pair, at) for pair in pairs for at in range(0, pair.shape[0] * CHUNK, CHUNK)]
    first = 0
    for one in rows:
        value = one[...]
        count = value.shape[0]
        pair, at = spots[first // CHUNK]
        chunks = slice(at // CHUNK, (at + count) // CHUNK)
        part = dot_plain(pair[chunks].reshape(count, 2 * width).T, value)
        total_pair = part if total_pair is None else total_pair + part
        if first < local_rows:
            part = dot_plain(grad_query[:, first : first + count], value)
            total_query = part if total_query is None else total_query + part
        first += count
    out[...] = low(jnp.concatenate([total_query, total_pair], axis=0).T)


def qkv_grad(grad_query, pairs, rows):
    width = rows[0].shape[1]
    count = sum(one.shape[0] for one in rows)
    return pl.pallas_call(
        functools.partial(qkv_grad_kernel, len(pairs)),
        out_shape=shape((width, 3 * grad_query.shape[0])),
        in_specs=[VM] * (1 + len(pairs) + len(rows)),
        out_specs=VM,
        compiler_params=ROOM,
        cost_estimate=pl.CostEstimate(
            flops=6 * count * width * grad_query.shape[0],
            bytes_accessed=2 * 10**7,
            transcendentals=0,
        ),
        name="qkv_grad",
    )(grad_query, *pairs, *rows)


def final_kernel(first, tokens, gains, grad_middle, kept, beside, one, two, own, far, out):
    unit, factor = rms_unit(tokens[...].astype(F32))
    across = jnp.concatenate([one[one.shape[0] + two.shape[0] - kept.shape[1] :, :], two[...]], axis=0)
    rows = kept[0].astype(F32) + beside[0].astype(F32) + across.astype(F32)
    ring = jnp.concatenate([own[...], far[...]], axis=0).astype(F32)
    rows = plain_order(rows + jnp.where(first[0] == 0, ring, 0.0))
    out[...] = rms_backward(rows, unit, factor, gains[0:1, :]) + grad_middle[...]


def final_rows(side, tokens, gains, grad_middle, kept, beside, one, two, own, far):
    rows, width = tokens.shape
    last = pl.BlockSpec((1, rows, width), lambda at: (1, 0, 0))
    half = pl.BlockSpec((rows // 2, width), lambda at: (0, 0))
    whole = pl.BlockSpec((rows, width), lambda at: (0, 0))
    return pl.pallas_call(
        final_kernel,
        grid=(1,),
        in_specs=[
            SM,
            whole,
            pl.BlockSpec(gains.shape, lambda at: (0, 0)),
            whole,
            last,
            last,
            pl.BlockSpec(one.shape, lambda at: (0, 0)),
            pl.BlockSpec(two.shape, lambda at: (0, 0)),
            half,
            half,
        ],
        out_specs=whole,
        out_shape=shape((rows, width), F32),
        compiler_params=ROOM,
        name="final_rows",
    )(side, tokens, gains, grad_middle, kept, beside, one, two, own, far)


def slot_places(chosen, priority, first, expert_count, capacity):
    tokens = chosen.shape[0]
    expert_range = jnp.arange(expert_count)
    chosen_hot = low(chosen[:, None] == expert_range[None, :])
    order_hot = low(priority[:, None] == jnp.arange(tokens)[None, :])
    sorted_hot = jnp.dot(order_hot, chosen_hot, preferred_element_type=F32)
    places = jnp.arange(tokens)
    before = low(places[:, None] > places[None, :])
    earlier = jnp.dot(before, low(sorted_hot), preferred_element_type=F32)
    sorted_rank = jnp.minimum(jnp.sum(earlier * sorted_hot, axis=1), capacity)
    rank = jnp.einsum("it,i->t", order_hot, low(sorted_rank), preferred_element_type=F32)
    rank = rank.astype(jnp.int32)
    near = chosen ^ first
    block = (near >> 1) + (near & 1) * (expert_count // 2)
    return jnp.where(rank < capacity, block * capacity + rank, -1)


def softmax_rows(logits):
    shifted = jnp.exp(logits - jnp.max(logits, axis=-1, keepdims=True))
    return shifted / jnp.sum(shifted, axis=-1, keepdims=True)


def one_hot_experts(ids, expert_count):
    return ids == lax.broadcasted_iota(jnp.int32, (ids.shape[0], expert_count), 1)


def middle_kernel(
    parts, tokens, cotangent, gains, router, ids, place_row, *rest
):
    attended, proj = rest[:parts], rest[parts : 2 * parts]
    even_rows, odd_rows, even_grads, odd_grads, middle, normed, probs = rest[2 * parts :]
    mixed = plain_order(jnp.concatenate([one[...] for one in attended], axis=0), 1)
    branch = dot_plain(mixed.T, jnp.concatenate([one[...] for one in proj], axis=0))
    total = tokens[...].astype(F32) + branch
    middle[...] = total
    unit, _ = rms_unit(total)
    normed_rows = low(gains[1:2, :] * unit)
    normed[...] = normed_rows
    chances = softmax_rows(dot_plain(normed_rows, router[...]))
    probs[...] = chances
    hot = one_hot_experts(ids[...], chances.shape[1])
    gate = jnp.sum(jnp.where(hot, chances, 0.0), axis=1, keepdims=True)
    weighted = low(gate * cotangent[...].astype(F32))
    half = even_rows.shape[0]
    for at, (row_slots, grad_slots) in enumerate(((even_rows, even_grads), (odd_rows, odd_grads))):
        slots = at * half + lax.broadcasted_iota(jnp.int32, (half, tokens.shape[0]), 0)
        dispatch = low(slots == place_row[...])
        row_slots[...] = low(dot_plain(dispatch, normed_rows))
        grad_slots[...] = low(dot_plain(dispatch, weighted))


def middle_rows(tokens, cotangent, gains, router, ids, place, slots, attended, proj):
    rows, width = tokens.shape
    half = shape((slots // 2, width))
    return pl.pallas_call(
        functools.partial(middle_kernel, len(attended)),
        out_shape=(
            half,
            half,
            half,
            half,
            shape((rows, width), F32),
            shape((rows, width)),
            shape((rows, router.shape[1]), F32),
        ),
        in_specs=[VM] * (6 + 2 * len(attended)),
        out_specs=(VM,) * 7,
        compiler_params=ROOM,
        name="middle_rows",
    )(tokens, cotangent, gains, router, ids, place[None, :], *attended, *proj)


def gather_slots(refs, capacity):
    own, beside, *pairs = refs
    even = [own[0:capacity, :]] + [pair[0:capacity, :] for pair in pairs]
    odd = [beside[0:capacity, :]] + [pair[capacity:, :] for pair in pairs]
    return jnp.concatenate(even + odd, axis=0)


def made_kernel(
    capacity, cotangent, ids, place_column, middle, normed, probs, *rest
):
    *row_refs, output, grad_logits, grad_router = rest
    rows, expert_count = probs.shape
    slots = 2 * row_refs[1].shape[0]
    slot_range = lax.broadcasted_iota(jnp.int32, (rows, slots), 1)
    dispatch = low(slot_range == place_column[...])
    routed = dot_plain(dispatch, gather_slots(row_refs, capacity))
    chances = probs[...]
    hot = one_hot_experts(ids[...], expert_count)
    gate = jnp.sum(jnp.where(hot, chances, 0.0), axis=1, keepdims=True)
    output[...] = low(middle[...] + gate * routed)
    grad_gate = jnp.sum(cotangent[...].astype(F32) * routed, axis=1, keepdims=True)
    logits = low((grad_gate * gate) * (hot.astype(F32) - chances))
    grad_logits[...] = logits
    grad_router[...] = dot_plain(logits.T, normed[...])


def made_rows(cotangent, ids, place, middle, normed, probs, row_slots):
    rows, width = middle.shape
    expert_count = probs.shape[1]
    capacity = row_slots[1].shape[0] // (len(row_slots) - 1)
    inputs = [cotangent, ids, place[:, None], middle, normed, probs, *row_slots]
    return pl.pallas_call(
        functools.partial(made_kernel, capacity),
        out_shape=(
            shape((rows, width)),
            shape((rows, expert_count)),
            shape((expert_count, width), F32),
        ),
        in_specs=[VM] * len(inputs),
        out_specs=(VM,) * 3,
        compiler_params=ROOM,
        name="made_rows",
    )(*inputs)


def back_kernel(
    parts, capacity, cotangent, gains, router, place_column, middle, grad_logits, *rest
):
    proj, rest = rest[:parts], rest[parts:]
    *grad_refs, grad_middle, grad_split, gain_two = rest[: -parts]
    near = rest[-parts:]
    rows = middle.shape[0]
    slots = 2 * grad_refs[1].shape[0]
    slot_range = lax.broadcasted_iota(jnp.int32, (rows, slots), 1)
    dispatch = low(slot_range == place_column[...])
    grad_second = dot_plain(dispatch, gather_slots(grad_refs, capacity))
    grad_second = grad_second + dot_last(grad_logits[...], router[...])
    unit, factor = rms_unit(middle[...])
    total = cotangent[...].astype(F32) + rms_backward(grad_second, unit, factor, gains[1:2, :])
    grad_low = split_order(low(total))
    for place in range(parts):
        near[place][...] = low(dot_last(proj[place][...], grad_low))
    grad_middle[...] = total
    grad_split[...] = grad_low
    summed = jnp.sum(grad_second * unit, axis=0, keepdims=True)
    gain_two[...] = jnp.broadcast_to(summed, gain_two.shape)


def back_rows(cotangent, gains, router, place, middle, grad_logits, proj, grad_slots):
    rows, width = middle.shape
    parts = len(proj)
    capacity = grad_slots[1].shape[0] // (len(grad_slots) - 1)
    inputs = [cotangent, gains, router, place[:, None], middle, grad_logits, *proj, *grad_slots]
    return pl.pallas_call(
        functools.partial(back_kernel, parts, capacity),
        out_shape=(
            shape((rows, width), F32),
            shape((rows, width)),
            shape((8, width), F32),
            *([shape((proj[0].shape[0], rows))] * parts),
        ),
        in_specs=[VM] * len(inputs),
        out_specs=(VM,) * (3 + parts),
        compiler_params=ROOM,
        name="back_rows",
    )(*inputs)


def proj_grad_kernel(grad_rows, *rest):
    *attended, keep, send = rest
    for place, one in enumerate(attended):
        part = dot_plain(one[...], grad_rows[...])
        if place % 2:
            send[place // 2] = low(part)
        else:
            keep[place // 2] = part


def proj_grad(grad_rows, attended):
    dims = (len(attended) // 2, attended[0].shape[0], grad_rows.shape[1])
    return pl.pallas_call(
        proj_grad_kernel,
        out_shape=(shape(dims, F32), shape(dims)),
        in_specs=[VM] * (1 + len(attended)),
        out_specs=(VM,) * 2,
        compiler_params=ROOM,
        name="proj_grad",
    )(grad_rows, *attended)


def expert_up_kernel(capacity, *refs):
    *parts, up, hidden, slope, rows_flip, rows = refs

    @pl.when(pl.program_id(0) == 0)
    def _():
        arrived = gather_slots(parts, capacity)
        rows[...] = arrived
        rows_flip[...] = arrived.T

    pre = dot_plain(rows[...], up[...])
    square = pre * pre
    bend = jnp.tanh(ROOT * (pre + CUBE * (square * pre)))
    half = 0.5 * (1.0 + bend)
    hidden[...] = low(pre * half)
    bent = (0.5 * ROOT) * pre * (1.0 - bend * bend) * (1.0 + (3.0 * CUBE) * square)
    slope[...] = low(half + bent)


def expert_out_kernel(hidden, down, even, odd):
    part = low(dot_plain(hidden[...], down[...]))

    @pl.when(pl.program_id(0) < 2)
    def _():
        even[...] = part

    @pl.when(pl.program_id(0) >= 2)
    def _():
        odd[...] = part


def expert_down_kernel(capacity, *refs):
    *parts, hidden, grad_down, grads, grads_flip = refs

    @pl.when(pl.program_id(0) == 0)
    def _():
        arrived = gather_slots(parts, capacity)
        grads[...] = arrived
        grads_flip[...] = arrived.T

    grad_down[...] = low(dot_plain(grads_flip[...], hidden[...]))


def expert_back_kernel(grads, slope, up, down, even, odd, grad_pre, total):
    step = pl.program_id(0)
    inner = low(dot_last(grads[...], down[...]) * slope[...].astype(F32))
    grad_pre[...] = inner
    part = dot_last(inner, up[...])

    @pl.when(step == 0)
    def _():
        total[...] = part

    @pl.when(step > 0)
    def _():
        total[...] += part

    @pl.when(step == pl.num_programs(0) - 1)
    def _():
        half = even.shape[0]
        even[...] = low(total[:half])
        odd[...] = low(total[half:])


def whole_spec(dims):
    return pl.BlockSpec(dims, lambda at: (0, 0))


def column_spec(rows):
    return pl.BlockSpec((rows, UNITS), lambda at: (0, at))


def row_spec(width):
    return pl.BlockSpec((UNITS, width), lambda at: (at, 0))


def expert_cost(products, slots, width, units):
    return pl.CostEstimate(
        flops=2 * products * slots * width * units,
        bytes_accessed=4 * slots * units + 2 * products * width * units,
        transcendentals=slots * units,
    )


def expert_hidden(parts, up):
    width, units = up.shape
    half = parts[1].shape[0]
    slots = 2 * half
    return pl.pallas_call(
        functools.partial(expert_up_kernel, half // (len(parts) - 1)),
        grid=(units // UNITS,),
        in_specs=[whole_spec(one.shape) for one in parts] + [column_spec(width)],
        out_specs=(column_spec(slots), column_spec(slots), whole_spec((width, slots))),
        out_shape=(shape((slots, units)), shape((slots, units)), shape((width, slots))),
        scratch_shapes=[pltpu.VMEM((slots, width), BF16)],
        compiler_params=ROOM,
        cost_estimate=expert_cost(1, slots, width, units),
        name="expert_hidden",
    )(*parts, up)


def expert_out(hidden, down):
    slots, units = hidden.shape
    width = down.shape[1]
    return pl.pallas_call(
        expert_out_kernel,
        grid=(4,),
        in_specs=[
            pl.BlockSpec((slots // 4, units), lambda at: (at, 0)),
            pl.BlockSpec((units, width), lambda at: (0, 0), pipeline_mode=pl.Buffered(1)),
        ],
        out_specs=(
            pl.BlockSpec((slots // 4, width), lambda at: (jnp.minimum(at, 1), 0)),
            pl.BlockSpec((slots // 4, width), lambda at: (jnp.maximum(at - 2, 0), 0)),
        ),
        out_shape=(shape((slots // 2, width)), shape((slots // 2, width))),
        compiler_params=ROOM,
        cost_estimate=expert_cost(1, slots, width, units),
        name="expert_out",
    )(hidden, down)


def expert_down_grad(parts, hidden):
    slots, units = hidden.shape
    half, width = parts[1].shape
    return pl.pallas_call(
        functools.partial(expert_down_kernel, half // (len(parts) - 1)),
        grid=(units // UNITS,),
        in_specs=[whole_spec(one.shape) for one in parts] + [column_spec(slots)],
        out_specs=(column_spec(width), whole_spec((slots, width))),
        out_shape=(shape((width, units)), shape((slots, width))),
        scratch_shapes=[pltpu.VMEM((width, slots), BF16)],
        compiler_params=ROOM,
        cost_estimate=expert_cost(1, slots, width, units),
        name="expert_down_grad",
    )(*parts, hidden)


def expert_back(grads, slope, up, down):
    slots, units = slope.shape
    width = grads.shape[1]
    block = whole_spec((slots // 2, width))
    return pl.pallas_call(
        expert_back_kernel,
        grid=(units // UNITS,),
        in_specs=[
            whole_spec(grads.shape),
            column_spec(slots),
            column_spec(width),
            row_spec(width),
        ],
        out_specs=(block, block, column_spec(slots)),
        out_shape=(
            shape((slots // 2, width)),
            shape((slots // 2, width)),
            shape((slots, units)),
        ),
        scratch_shapes=[pltpu.VMEM((slots, width), F32)],
        compiler_params=ROOM,
        cost_estimate=expert_cost(2, slots, width, units),
        name="expert_back",
    )(grads, slope, up, down)


def expert_up_grad_kernel(rows_flip, grad_pre, grad_up):
    grad_up[...] = low(dot_plain(rows_flip[...], grad_pre[...]))


def expert_up_grad(rows_flip, grad_pre):
    slots, units = grad_pre.shape
    width = rows_flip.shape[0]
    return pl.pallas_call(
        expert_up_grad_kernel,
        grid=(units // UNITS,),
        in_specs=[whole_spec(rows_flip.shape), column_spec(slots)],
        out_specs=column_spec(width),
        out_shape=shape((width, units)),
        compiler_params=ROOM,
        cost_estimate=expert_cost(1, slots, width, units),
        name="expert_up_grad",
    )(rows_flip, grad_pre)


def shards(
    tokens,
    cotangent,
    gains,
    qkv_weight,
    proj_weight,
    router_weight,
    expert_up,
    expert_down,
    expert_ids,
    slot_order,
    segment_ids,
):
    dp_count, ctx_count, tp_count = (lax.axis_size(name) for name in ("dp", "ctx", "tp"))
    dp_index, ctx_index, tp_index = (lax.axis_index(name) for name in ("dp", "ctx", "tp"))
    group = dp_count * tp_count
    group_index = dp_index * tp_count + tp_index
    tok_dev, width = tokens.shape
    half_rows = tok_dev // 2
    expert_count = router_weight.shape[1]
    capacity = 5 * tok_dev // (4 * expert_count)
    slots = expert_count * capacity
    per = PLEN // ctx_count // CHUNK
    conts_here = segment_ids.shape[0]
    prompts_here = conts_here * ctx_count // CONTS
    local_width = qkv_weight.shape[2]
    shard_rows = qkv_weight.shape[1]
    side, core = tp_index >> 1, tp_index & 1

    def across(value):
        return xor_swap(value, "tp", tp_count, 2)

    def beside(value):
        return xor_swap(value, "tp", tp_count, 1)

    packed = jnp.concatenate(
        [
            qkv_weight.transpose(1, 0, 2).reshape(shard_rows, 3 * local_width),
            proj_weight.T,
            router_weight,
        ],
        axis=1,
    )
    by_ctx = xor_exchange([packed] * ctx_count, "ctx", ctx_count)
    own, own_second = normalize(tokens, gains)
    far_second = across(own_second)
    carried = jnp.where(side == 0, own[:half_rows], far_second)
    by_ctx, carried = lax.optimization_barrier((by_ctx, carried))
    by_dp = xor_gather(jnp.stack(by_ctx), "dp", dp_count)
    far_first = across(own[:half_rows])
    arrived = ring_step(carried, "ctx", ctx_count, 1)
    arrived, far_first, by_dp = lax.optimization_barrier((arrived, far_first, by_dp))
    rows = [own, beside(own), far_first, far_second, beside(far_first), beside(far_second)]
    local_count = len(rows)

    by_dp = jnp.stack(by_dp).reshape((-1,) + packed.shape)
    shard_index = dp_index * ctx_count + ctx_index
    weights = jnp.concatenate(
        [pick(by_dp, shard_index ^ place) for place in range(dp_count * ctx_count)], axis=0
    )
    query_weight = weights[:, :local_width]
    pair_weight = weights[:, local_width : 3 * local_width]
    router = weights[:, 4 * local_width :]

    query, local = project_local(query_weight, pair_weight, rows)
    remote = []
    blocks = []
    for place in range(1, ctx_count):
        other = across(arrived)
        if place < ctx_count - 1:
            following = ring_step(arrived, "ctx", ctx_count, 1)
            if place == 1:
                expert_up, expert_down, following = lax.optimization_barrier(
                    (expert_up, expert_down, following)
                )
                full_up = lax.all_gather(expert_up, "ctx", axis=2, tiled=True)[0]
                full_down = lax.all_gather(expert_down, "ctx", axis=1, tiled=True)[0]
            if place == ctx_count - 2:
                following, query, local = lax.optimization_barrier((following, query, local))
            following, other = lax.optimization_barrier((following, other))
        blocks.append([arrived, other, beside(arrived), beside(other)])
        arrived = following
    rows += [one for block in blocks for one in block]
    remote = [project_remote(pair_weight, block) for block in blocks]
    proj_part, _ = lax.optimization_barrier(
        (weights[:, 3 * local_width : 4 * local_width].T, blocks[-1][1])
    )
    proj = xor_gather(proj_part, "tp", tp_count, [2, 1])

    device_chunks = tok_dev // CHUNK

    def split_place(at):
        return (at % 2) * (device_chunks // 2) + at // 2

    at = jnp.arange(prompts_here * per)
    owner, inside = at // device_chunks, at % device_chunks
    local_at = (owner ^ tp_index) * device_chunks + split_place(inside)
    remote_at = ((owner ^ core) * 2 + ((inside % 2) ^ side)) * (device_chunks // 2) + inside // 2
    prompt_at = jnp.concatenate(
        [local_at.reshape(prompts_here, per), remote_at.reshape(prompts_here, per)], axis=1
    )
    at = jnp.arange(conts_here)
    cont_at = ((2 + at // device_chunks) ^ tp_index) * device_chunks + split_place(
        at % device_chunks
    )
    info = jnp.concatenate([ctx_index[None], prompt_at.reshape(-1), cont_at, segment_ids])
    info = info.astype(jnp.int32)
    sizes = (prompts_here, conts_here, ctx_count, per)

    *attended, lse_prompt, lse_cont = attend_forward(sizes, info, query, local, remote)
    mixed = attended
    attended = xor_exchange(attended, "tp", tp_count)
    place = slot_places(expert_ids[:, 0], slot_order[0], group_index, expert_count, capacity)

    def start_exchange(odd):
        return xor_swap(odd, ("dp", "tp"), group, 1)

    def finish_exchange(even, other):
        moved = [even, other]
        for at in range(1, group // 2):
            block = slice(at * capacity, (at + 1) * capacity)
            pair = jnp.concatenate([even[block], other[block]], axis=0)
            moved.append(xor_swap(pair, ("dp", "tp"), group, 2 * at))
        return moved

    even_rows, odd_rows, even_grads, odd_grads, middle, normed_two, probs = middle_rows(
        tokens, cotangent, gains, router, expert_ids, place, slots, attended, proj
    )
    row_slots = finish_exchange(even_rows, start_exchange(odd_rows))
    other_grads = start_exchange(odd_grads)
    row_slots, even_grads, other_grads = lax.optimization_barrier(
        (row_slots, even_grads, other_grads)
    )
    grad_slots = finish_exchange(even_grads, other_grads)
    hidden, slope, rows_flip = expert_hidden(row_slots, full_up)
    grad_down, arrived_grads = expert_down_grad(grad_slots, hidden)
    hidden, arrived_grads = lax.optimization_barrier((hidden, arrived_grads))
    even, odd = expert_out(hidden, full_down)
    even, other, slope = lax.optimization_barrier((even, start_exchange(odd), slope))
    made_slots = finish_exchange(even, other)
    even, odd, grad_pre = expert_back(arrived_grads, slope, full_up, full_down)
    even, odd, made_slots, grad_pre = lax.optimization_barrier((even, odd, made_slots, grad_pre))
    back_slots = finish_exchange(even, start_exchange(odd))
    grad_down = lax.psum_scatter(grad_down, "ctx", scatter_dimension=1, tiled=True)
    grad_down = grad_down.T.astype(F32)[None]
    grad_up = expert_up_grad(rows_flip, grad_pre)

    output, grad_logits, router_part = made_rows(
        cotangent, expert_ids, place, middle, normed_two, probs, made_slots
    )
    grad_middle, grad_split, gain_two, *grad_near = back_rows(
        cotangent, gains, router, place, middle, grad_logits, proj, back_slots
    )
    grad_near = xor_exchange(grad_near, "tp", tp_count)
    proj_keep, proj_send = proj_grad(grad_split, attended)
    grad_near, proj_keep, proj_send, grad_up = lax.optimization_barrier(
        (grad_near, proj_keep, proj_send, grad_up)
    )
    grad_up = lax.psum_scatter(grad_up, "ctx", scatter_dimension=1, tiled=True).astype(F32)[None]
    grad_query, grad_local, *grads = attend_backward(
        sizes,
        info,
        query,
        lse_prompt,
        lse_cont,
        local,
        remote,
        query_weight,
        pair_weight,
        grad_near,
        mixed,
    )
    count = ctx_count - 1
    grad_remote, (*remote_rows, local_keep, local_send) = grads[:count], grads[count:]
    if remote_rows:
        remote_rows = list(zip(remote_rows[:count], remote_rows[count:]))
    else:
        remote_rows = [rows_remote(one, pair_weight) for one in grad_remote]

    remote_rows = remote_rows[::-1]

    def chip_rows(keep, send):
        chip = keep.astype(F32) + beside(send).astype(F32)
        return chip[:half_rows], low(chip[half_rows:])

    def scatter_sum(values, axis, size, me):
        parts = xor_exchange([pick(values, me ^ k) for k in range(size)], axis, size)
        return add_all([piece.astype(F32) for piece in parts])

    piece, message = chip_rows(*remote_rows[0])
    following = chip_rows(*remote_rows[1])
    near = across(message)
    grad_pairs, message = lax.optimization_barrier(([grad_local, *grad_remote], message))
    qkv_part = qkv_grad(grad_query, grad_pairs, rows)
    near, qkv_part, following, local_send, proj_send, remote_rows[2:] = lax.optimization_barrier(
        (near, qkv_part, following, local_send, proj_send, remote_rows[2:])
    )
    running = low(piece + near.astype(F32))
    for place in range(1, count):
        piece, message = following
        message, running = lax.optimization_barrier((message, running))
        moved = ring_step(running, "ctx", ctx_count, -1)
        near = across(message)
        if place < count - 1:
            following = chip_rows(*remote_rows[place + 1])
        if place == 1:
            local_send = beside(local_send)
            far_message = low(local_keep[0].astype(F32) + local_send[0].astype(F32))
            first_rows = (tok_dev - local_width) // 2
            proj_chip = proj_keep + beside(proj_send).astype(F32)
            far_first = jnp.concatenate([low(proj_chip[1]), far_message[:first_rows]], axis=0)
            near, far_first = lax.optimization_barrier((near, far_first))
            far_first = across(far_first)
            moved, near, far_first, following = lax.optimization_barrier(
                (moved, near, far_first, following)
            )
            proj_sum = proj_chip[0] + far_first[:local_width].astype(F32)
            early = jnp.concatenate([low(proj_sum), low(router_part), low(gain_two[:1])], axis=0)
            packed = jnp.concatenate([qkv_part, early.T], axis=1)
            packed = packed.reshape(dp_count, ctx_count, shard_rows, -1)
        if place == count - 1:
            summed = low(scatter_sum(packed, "dp", dp_count, dp_index))
            near, far_second = lax.optimization_barrier((near, far_message[first_rows:]))
            far_second = across(far_second)
            moved, near, summed, grad_up, grad_down = lax.optimization_barrier(
                (moved, near, summed, grad_up, grad_down)
            )
        running = low(piece + near.astype(F32) + moved.astype(F32))
    running, summed = lax.optimization_barrier((running, summed))
    hops = [[], []]
    for ctx_from in range(ctx_count):
        for tp_from in range(tp_count):
            target = (ctx_from - 1) % ctx_count * tp_count + (tp_from & 1)
            hops[tp_from >> 1].append((ctx_from * tp_count + tp_from, target))
    own_rows, other_rows = (lax.ppermute(running, ("ctx", "tp"), hop) for hop in hops)
    summed = scatter_sum(summed, "ctx", ctx_count, ctx_index)
    grad_tokens = final_rows(
        side.astype(jnp.int32).reshape(1),
        tokens,
        gains,
        grad_middle,
        local_keep,
        local_send,
        far_first,
        far_second,
        own_rows,
        other_rows,
    )

    qkv_width = 3 * local_width
    grad_qkv = summed[:, :qkv_width].reshape(shard_rows, 3, local_width).transpose(1, 0, 2)
    grad_proj = summed[:, qkv_width : qkv_width + local_width].T
    gain_range = lax.dynamic_slice_in_dim(gains[0], shard_index * shard_rows, shard_rows)
    gain_one = jnp.sum(qkv_weight.astype(F32) * grad_qkv, axis=(0, 2))
    small = jnp.concatenate([summed[:, qkv_width + local_width :], gain_one[:, None]], axis=1)
    parts = xor_exchange([low(small)] * tp_count, "tp", tp_count)
    parts, grad_tokens = lax.optimization_barrier((parts, grad_tokens))
    small = small + add_all([part.astype(F32) for part in parts[1:]])
    grad_router = small[:, :expert_count]
    grad_gains = jnp.stack([small[:, expert_count + 1] / gain_range, small[:, expert_count]])
    return (output, grad_tokens, grad_gains, grad_qkv, grad_proj, grad_router, grad_up, grad_down)


def solution(mesh):
    in_specs = (
        P(("dp", "ctx", "tp"), None),
        P(("dp", "ctx", "tp"), None),
        P(),
        P(None, ("dp", "ctx"), "tp"),
        P("tp", ("dp", "ctx")),
        P(("dp", "ctx"), None),
        P(("dp", "tp"), None, "ctx"),
        P(("dp", "tp"), "ctx", None),
        P(("dp", "ctx", "tp"), None),
        P(("dp", "ctx", "tp"), None),
        P(("dp", "ctx")),
    )
    out_specs = (
        P(("dp", "ctx", "tp"), None),
        P(("dp", "ctx", "tp"), None),
        P(None, ("dp", "ctx")),
        P(None, ("dp", "ctx"), "tp"),
        P("tp", ("dp", "ctx")),
        P(("dp", "ctx"), None),
        P(("dp", "tp"), None, "ctx"),
        P(("dp", "tp"), "ctx", None),
    )
    return jax.shard_map(shards, mesh=mesh, in_specs=in_specs, out_specs=out_specs, check_vma=False)
```

```python
import functools

import jax
import jax.numpy as jnp
from jax import lax
from jax.experimental import pallas as pl
from jax.experimental.pallas import tpu as pltpu
from jax.sharding import PartitionSpec as P

HD = 64
PLEN = 1024
CLEN = 128
CONTS = 8
CHUNK = 128
UNITS = 768

EPSILON = 1e-06
NEGATIVE = -1e30
ROOT = 0.7978845608028654
CUBE = 0.044715
F32 = jnp.float32
BF16 = jnp.bfloat16
VM = pl.BlockSpec(memory_space=pltpu.VMEM)
SM = pl.BlockSpec(memory_space=pltpu.SMEM)
ROOM = pltpu.CompilerParams(vmem_limit_bytes=60 * 2**20)


def shape(dims, dtype=BF16):
    return jax.ShapeDtypeStruct(dims, dtype)


def low(value):
    return value.astype(BF16)


def dot_last(left, right):
    return lax.dot_general(left, right, (((1,), (1,)), ((), ())), preferred_element_type=F32)


def dot_plain(left, right):
    return lax.dot_general(left, right, (((1,), (0,)), ((), ())), preferred_element_type=F32)


def add_all(parts):
    return functools.reduce(jnp.add, parts)


def xor_swap(value, axis, size, mask):
    return lax.ppermute(value, axis, [(place, place ^ mask) for place in range(size)])


def ring_step(value, axis, size, shift):
    return lax.ppermute(value, axis, [(place, (place + shift) % size) for place in range(size)])


def pick(stacked, index):
    return lax.dynamic_index_in_dim(stacked, index, 0, keepdims=False)


def xor_gather(value, axis, size, order=None):
    if order is None:
        order = [1 << bit for bit in range(size.bit_length() - 1)]
    have = {0: value}
    for mask in order:
        keys = sorted(have)
        moved = xor_swap(jnp.stack([have[key] for key in keys]), axis, size, mask)
        for place, key in enumerate(keys):
            have[key ^ mask] = moved[place]
    return [have[key] for key in range(size)]


def xor_exchange(pieces, axis, size):
    return [pieces[0]] + [xor_swap(pieces[mask], axis, size, mask) for mask in range(1, size)]


def chunk_list(value, axis):
    return [
        lax.slice_in_dim(value, first, first + CHUNK, axis=axis)
        for first in range(0, value.shape[axis], CHUNK)
    ]


def split_order(value, axis=0):
    parts = chunk_list(value, axis)
    return jnp.concatenate(parts[0::2] + parts[1::2], axis=axis)


def plain_order(value, axis=0):
    parts = chunk_list(value, axis)
    half = len(parts) // 2
    return jnp.concatenate([parts[(at % 2) * half + at // 2] for at in range(2 * half)], axis=axis)


def rms_unit(values):
    factor = lax.rsqrt(jnp.mean(values * values, axis=-1, keepdims=True) + EPSILON)
    return (values * factor, factor)


def rms_backward(grad_normed, unit_part, factor, gain):
    scaled = grad_normed * gain
    inner = jnp.mean(scaled * unit_part, axis=-1, keepdims=True)
    return factor * (scaled - unit_part * inner)


def normalize_kernel(tokens, gains, own, second):
    unit, _ = rms_unit(tokens[...].astype(F32))
    own[...] = split_order(low(gains[0:1, :] * unit))
    second[...] = own[own.shape[0] // 2 :, :]


def normalize(tokens, gains):
    rows, width = tokens.shape
    return pl.pallas_call(
        normalize_kernel,
        out_shape=(shape((rows, width)), shape((rows // 2, width))),
        in_specs=[VM] * 2,
        out_specs=(VM,) * 2,
        compiler_params=ROOM,
        name="normalize",
    )(tokens, gains)


def key_lanes(rows, width):
    return rows[:, : width + (-width) % 128]


def value_lanes(rows, width):
    return rows[:, width - (-width) % 128 :]


def spread_heads(columns, ahead, behind):
    width, count = columns.shape
    groups = []
    for first in range(0, width, HD):
        pieces = [columns[first : first + HD]]
        above, below = ahead + first, width - first - HD + behind
        if above:
            pieces.insert(0, jnp.zeros((above, count), columns.dtype))
        if below:
            pieces.append(jnp.zeros((below, count), columns.dtype))
        groups.append(jnp.concatenate(pieces, axis=0))
    return jnp.concatenate(groups, axis=1)


def causal(scores, count):
    key_row = lax.broadcasted_iota(jnp.int32, scores.shape, 0)
    query_row = lax.broadcasted_iota(jnp.int32, scores.shape, 1) % count
    return jnp.where(key_row <= query_row, scores, NEGATIVE)


def work_items(info, sizes, attend):
    prompts, conts, places, per = sizes
    ctx_index = info[0]

    def prompt_chunks(prompt):
        first = 1 + prompt * 2 * per
        return [info[first + at] for at in range(per)], [info[first + per + at] for at in range(per)]

    def prompt_mask(scores):
        count = per * CHUNK
        parts = [causal(scores[:count], count)]
        for place in range(1, places):
            part = scores[place * count : (place + 1) * count]
            parts.append(jnp.where(place <= ctx_index, part, NEGATIVE))
        return jnp.concatenate(parts, axis=0)

    def cont_mask(scores):
        return jnp.concatenate([causal(scores[:CLEN], CLEN), scores[CLEN:]], axis=0)

    @pl.loop(0, prompts, unroll=2)
    def _(prompt):
        own, far = prompt_chunks(prompt)
        attend(0, prompt, own, own, far, prompt_mask)

    first = 1 + prompts * 2 * per

    @pl.loop(0, conts, unroll=2)
    def _(cont):
        own = [info[first + cont]]
        near, far = prompt_chunks(info[first + conts + cont])
        attend(1, cont, own, own + near, far, cont_mask)


def chunk_lanes(chunk):
    return pl.ds(pl.multiple_of(chunk * CHUNK, CHUNK), CHUNK)


def load_lanes(ref, chunks):
    return jnp.concatenate([ref[:, chunk_lanes(chunk)] for chunk in chunks], axis=1)


def project_local_kernel(query_weight, pair_weight, *rest):
    *rows, query, pairs = rest
    width = query.shape[0]
    query_flip = query_weight[...].T
    at = 0
    for one in rows:
        value = one[...]
        count = value.shape[0]
        pair = low(dot_plain(value, pair_weight[...]))
        pairs[at // CHUNK : (at + count) // CHUNK] = pair.reshape(-1, CHUNK, 2 * width)
        query[:, at : at + count] = low(dot_last(query_flip, value) * 0.125)
        at += count


def project_remote_kernel(pair_weight, *rest):
    *rows, pairs = rest
    at = 0
    for one in rows:
        count = one.shape[0]
        pair = low(dot_plain(one[...], pair_weight[...]))
        pairs[at // CHUNK : (at + count) // CHUNK] = pair.reshape(-1, CHUNK, pairs.shape[2])
        at += count


def project_local(query_weight, pair_weight, rows):
    count = sum(one.shape[0] for one in rows)
    wide = pair_weight.shape[1]
    return pl.pallas_call(
        project_local_kernel,
        out_shape=(shape((query_weight.shape[1], count)), shape((count // CHUNK, CHUNK, wide))),
        in_specs=[VM] * (2 + len(rows)),
        out_specs=(VM,) * 2,
        compiler_params=ROOM,
        cost_estimate=pl.CostEstimate(
            flops=3 * count * pair_weight.size, bytes_accessed=10**7, transcendentals=0
        ),
        name="project_local",
    )(query_weight, pair_weight, *rows)


def project_remote(pair_weight, rows):
    count = sum(one.shape[0] for one in rows)
    return pl.pallas_call(
        project_remote_kernel,
        out_shape=shape((count // CHUNK, CHUNK, pair_weight.shape[1])),
        in_specs=[VM] * (1 + len(rows)),
        out_specs=VM,
        compiler_params=ROOM,
        cost_estimate=pl.CostEstimate(
            flops=2 * count * pair_weight.size, bytes_accessed=4 * 10**6, transcendentals=0
        ),
        name="project_remote",
    )(pair_weight, *rows)


def load_block(local, remote, near, far):
    blocks = [local[chunk] for chunk in near]
    blocks += [one[chunk] for one in remote for chunk in far]
    return jnp.concatenate(blocks, axis=0)


def attend_forward_kernel(sizes, info, query, local, *rest):
    remote, (*outs, lse_prompt, lse_cont, mixed) = rest[: sizes[2] - 1], rest[sizes[2] - 1 :]
    lse = (lse_prompt, lse_cont)
    width = query.shape[0]
    pad = (-width) % 128

    def attend(kind, index, own, near, far, mask):
        count = len(own) * CHUNK
        block = load_block(local, remote, near, far)
        spread = spread_heads(load_lanes(query, own), 0, pad)
        scores = mask(dot_plain(key_lanes(block, width), spread))
        peak = jnp.max(scores, axis=0, keepdims=True)
        shifted = jnp.exp(scores - peak)
        total = jnp.sum(shifted, axis=0, keepdims=True)
        weights = low(shifted)
        flip = value_lanes(block, width).T
        for head in range(width // HD):
            group = slice(head * count, (head + 1) * count)
            part = slice(pad + head * HD, pad + (head + 1) * HD)
            result = low(dot_plain(flip[part], weights[:, group]) / total[:, group])
            for place, chunk in enumerate(own):
                mixed[head * HD : (head + 1) * HD, chunk_lanes(chunk)] = result[
                    :, place * CHUNK : (place + 1) * CHUNK
                ]
        lse[kind][index] = peak + jnp.log(total)

    work_items(info, sizes, attend)
    each = outs[0].shape[1]
    for place, out in enumerate(outs):
        out[...] = mixed[:, place * each : (place + 1) * each]


def attend_backward_kernel(sizes, info, query, lse_prompt, lse_cont, local, *rest):
    count_remote = sizes[2] - 1
    remote, rest = rest[:count_remote], rest[count_remote:]
    pair_weight, *rest = rest
    grads, mixed, rest = rest[:4], rest[4:8], rest[8:]
    grad_query, grad_local, *rest, grad, centre, sum_local, sum_remote = rest
    grad_remote, rest = rest[:count_remote], rest[count_remote:]
    keep_remote, send_remote = rest[: len(rest) // 2], rest[len(rest) // 2 :]
    lse = (lse_prompt, lse_cont)
    width = query.shape[0]
    pad = (-width) % 128
    each = grads[0].shape[1]
    for place, (one, result) in enumerate(zip(grads, mixed)):
        columns = slice(place * each, (place + 1) * each)
        grad[:, columns] = one[...]
        product = one[...].astype(F32) * result[...].astype(F32)
        for head in range(width // HD):
            centre[head : head + 1, columns] = jnp.sum(
                product[head * HD : (head + 1) * HD], axis=0, keepdims=True
            )

    def attend(kind, index, own, near, far, mask):
        count = len(own) * CHUNK
        block = load_block(local, remote, near, far)
        query_spread = spread_heads(load_lanes(query, own), 0, pad)
        grad_spread = spread_heads(load_lanes(grad, own), pad, 0)
        keys = key_lanes(block, width)
        weights = jnp.exp(mask(dot_plain(keys, query_spread)) - lse[kind][index])
        slopes = dot_plain(value_lanes(block, width), grad_spread)
        middle = load_lanes(centre, own)
        middle = jnp.concatenate([middle[head : head + 1] for head in range(width // HD)], axis=1)
        grad_scores = low(weights * (slopes - middle))
        flip = keys.T
        for head in range(width // HD):
            group = slice(head * count, (head + 1) * count)
            part = slice(head * HD, (head + 1) * HD)
            result = low(dot_plain(flip[part], grad_scores[:, group]) * 0.125)
            for place, chunk in enumerate(own):
                grad_query[part, chunk_lanes(chunk)] = result[
                    :, place * CHUNK : (place + 1) * CHUNK
                ]
        key_part = dot_last(grad_scores, query_spread)
        value_part = dot_last(low(weights), grad_spread)
        if pad:
            edge = width - pad
            shared = key_part[:, edge:] + value_part[:, : 2 * pad]
            joined = [key_part[:, :edge], shared, value_part[:, 2 * pad :]]
        else:
            joined = [key_part, value_part]
        result = jnp.concatenate(joined, axis=1)
        spots = [(sum_local, chunk) for chunk in near]
        spots += [(sum_remote.at[place], chunk) for place in range(count_remote) for chunk in far]
        for at, (sums, chunk) in enumerate(spots):
            part = result[at * CHUNK : (at + 1) * CHUNK]
            if kind == 0 or at == 0:
                sums[chunk] = part
            else:
                sums[chunk] += part

    work_items(info, sizes, attend)

    half = remote[0].shape[0] // 2
    for place in range(count_remote):
        for side, outs in enumerate((keep_remote, send_remote)):
            chunks = slice(side * half, (side + 1) * half)
            part = low(sum_remote[place, chunks])
            grad_remote[place][chunks] = part
            if outs:
                flat = part.reshape(half * CHUNK, 2 * width)
                outs[place][...] = low(dot_last(flat, pair_weight[...]))
    grad_local[...] = low(sum_local[...])


def attend_cost(factor, sizes, heads):
    prompts, conts, places, per = sizes
    scores = heads * places * per * CHUNK * CHUNK * (prompts * per + conts)
    return pl.CostEstimate(flops=factor * HD * scores, bytes_accessed=10**7, transcendentals=scores)


def attend_forward(sizes, info, query, local, remote):
    prompts, conts, places, per = sizes
    width, local_rows = query.shape
    heads = width // HD
    return pl.pallas_call(
        functools.partial(attend_forward_kernel, sizes),
        out_shape=(
            *([shape((width, local_rows // 4))] * 4),
            shape((prompts, 1, heads * per * CHUNK), F32),
            shape((conts, 1, heads * CLEN), F32),
        ),
        in_specs=[SM] + [VM] * (2 + len(remote)),
        out_specs=(VM,) * 6,
        scratch_shapes=[pltpu.VMEM((width, local_rows), BF16)],
        compiler_params=ROOM,
        cost_estimate=attend_cost(16, sizes, heads),
        name="attend_forward",
    )(info, query, local, *remote)


def attend_backward(
    sizes, info, query, lse_prompt, lse_cont, local, remote, pair_weight, grads, mixed
):
    pairs = [local] + list(remote)
    remote_rows = 2 * len(remote) if len(remote) <= 4 else 0
    each = shape((grads[0].shape[1], pair_weight.shape[0]))
    count = len(remote)
    return pl.pallas_call(
        functools.partial(attend_backward_kernel, sizes),
        out_shape=(
            shape(query.shape),
            *(shape(one.shape) for one in pairs),
            *([each] * remote_rows),
        ),
        in_specs=[SM] + [VM] * (4 + len(pairs) + 2 * len(grads)),
        out_specs=(VM,) * (1 + len(pairs) + remote_rows),
        scratch_shapes=[
            pltpu.VMEM(query.shape, BF16),
            pltpu.VMEM((8, query.shape[1]), F32),
            pltpu.VMEM(local.shape, F32),
            pltpu.VMEM((count,) + remote[0].shape, F32),
        ],
        compiler_params=ROOM,
        cost_estimate=attend_cost(40, sizes, query.shape[0] // HD),
        name="attend_backward",
    )(info, query, lse_prompt, lse_cont, *pairs, pair_weight, *grads, *mixed)


def rows_remote_kernel(grad_pairs, pair_weight, keep, send):
    half = grad_pairs.shape[0] // 2
    wide = grad_pairs.shape[2]
    send[...] = low(dot_last(grad_pairs[half:].reshape(half * CHUNK, wide), pair_weight[...]))
    keep[...] = low(dot_last(grad_pairs[:half].reshape(half * CHUNK, wide), pair_weight[...]))


def rows_remote(grad_pairs, pair_weight):
    dims = (grad_pairs.shape[0] // 2 * CHUNK, pair_weight.shape[0])
    return pl.pallas_call(
        rows_remote_kernel,
        in_specs=[VM] * 2,
        out_specs=(VM,) * 2,
        out_shape=(shape(dims), shape(dims)),
        compiler_params=ROOM,
        cost_estimate=pl.CostEstimate(
            flops=4 * dims[0] * pair_weight.size, bytes_accessed=6 * 10**6, transcendentals=0
        ),
        name="rows_remote",
    )(grad_pairs, pair_weight)


def rows_local_kernel(grad_pairs, grad_query, query_weight, pair_weight, keep, send):
    half = grad_pairs.shape[0] // 2
    wide = grad_pairs.shape[2]
    each = half * CHUNK
    query_rows = grad_query[...].T
    rows = dot_last(grad_pairs[...].reshape(2 * each, wide), pair_weight[...])
    rows = rows + dot_last(query_rows, query_weight[...])
    keep[0] = low(rows[:each])
    send[0] = low(rows[each:])


def rows_local(grad_pairs, grad_query, query_weight, pair_weight, each):
    width = pair_weight.shape[0]
    chunks = 2 * each // CHUNK
    return pl.pallas_call(
        rows_local_kernel,
        grid=(2,),
        in_specs=[
            pl.BlockSpec((chunks,) + grad_pairs.shape[1:], lambda at: (1 - at, 0, 0)),
            pl.BlockSpec((grad_query.shape[0], 2 * each), lambda at: (0, 1 - at)),
            pl.BlockSpec(query_weight.shape, lambda at: (0, 0)),
            pl.BlockSpec(pair_weight.shape, lambda at: (0, 0)),
        ],
        out_specs=(
            pl.BlockSpec((1, each, width), lambda at: (at, 0, 0)),
            pl.BlockSpec((1, each, width), lambda at: (at, 0, 0)),
        ),
        out_shape=(shape((2, each, width)), shape((2, each, width))),
        compiler_params=ROOM,
        cost_estimate=pl.CostEstimate(
            flops=6 * 2 * each * pair_weight.size, bytes_accessed=2 * 10**7, transcendentals=0
        ),
        name="rows_local",
    )(grad_pairs, grad_query, query_weight, pair_weight)


def qkv_grad_kernel(places, grad_query, *rest):
    pairs, rows, out = rest[:places], rest[places:-1], rest[-1]
    width, local_rows = grad_query.shape
    total_query = total_pair = None
    spots = [(pair, at) for pair in pairs for at in range(0, pair.shape[0] * CHUNK, CHUNK)]
    first = 0
    for one in rows:
        value = one[...]
        count = value.shape[0]
        pair, at = spots[first // CHUNK]
        chunks = slice(at // CHUNK, (at + count) // CHUNK)
        part = dot_plain(pair[chunks].reshape(count, 2 * width).T, value)
        total_pair = part if total_pair is None else total_pair + part
        if first < local_rows:
            part = dot_plain(grad_query[:, first : first + count], value)
            total_query = part if total_query is None else total_query + part
        first += count
    out[...] = low(jnp.concatenate([total_query, total_pair], axis=0).T)


def qkv_grad(grad_query, pairs, rows):
    width = rows[0].shape[1]
    count = sum(one.shape[0] for one in rows)
    return pl.pallas_call(
        functools.partial(qkv_grad_kernel, len(pairs)),
        out_shape=shape((width, 3 * grad_query.shape[0])),
        in_specs=[VM] * (1 + len(pairs) + len(rows)),
        out_specs=VM,
        compiler_params=ROOM,
        cost_estimate=pl.CostEstimate(
            flops=6 * count * width * grad_query.shape[0],
            bytes_accessed=2 * 10**7,
            transcendentals=0,
        ),
        name="qkv_grad",
    )(grad_query, *pairs, *rows)


def final_kernel(first, tokens, gains, grad_middle, kept, beside, one, two, own, far, out):
    unit, factor = rms_unit(tokens[...].astype(F32))
    across = jnp.concatenate([one[one.shape[0] + two.shape[0] - kept.shape[1] :, :], two[...]], axis=0)
    rows = kept[0].astype(F32) + beside[0].astype(F32) + across.astype(F32)
    ring = jnp.concatenate([own[...], far[...]], axis=0).astype(F32)
    rows = plain_order(rows + jnp.where(first[0] == 0, ring, 0.0))
    out[...] = rms_backward(rows, unit, factor, gains[0:1, :]) + grad_middle[...]


def final_rows(side, tokens, gains, grad_middle, kept, beside, one, two, own, far):
    rows, width = tokens.shape
    last = pl.BlockSpec((1, rows, width), lambda at: (1, 0, 0))
    half = pl.BlockSpec((rows // 2, width), lambda at: (0, 0))
    whole = pl.BlockSpec((rows, width), lambda at: (0, 0))
    return pl.pallas_call(
        final_kernel,
        grid=(1,),
        in_specs=[
            SM,
            whole,
            pl.BlockSpec(gains.shape, lambda at: (0, 0)),
            whole,
            last,
            last,
            pl.BlockSpec(one.shape, lambda at: (0, 0)),
            pl.BlockSpec(two.shape, lambda at: (0, 0)),
            half,
            half,
        ],
        out_specs=whole,
        out_shape=shape((rows, width), F32),
        compiler_params=ROOM,
        name="final_rows",
    )(side, tokens, gains, grad_middle, kept, beside, one, two, own, far)


def slot_places(chosen, priority, first, expert_count, capacity):
    tokens = chosen.shape[0]
    expert_range = jnp.arange(expert_count)
    chosen_hot = low(chosen[:, None] == expert_range[None, :])
    order_hot = low(priority[:, None] == jnp.arange(tokens)[None, :])
    sorted_hot = jnp.dot(order_hot, chosen_hot, preferred_element_type=F32)
    places = jnp.arange(tokens)
    before = low(places[:, None] > places[None, :])
    earlier = jnp.dot(before, low(sorted_hot), preferred_element_type=F32)
    sorted_rank = jnp.minimum(jnp.sum(earlier * sorted_hot, axis=1), capacity)
    rank = jnp.einsum("it,i->t", order_hot, low(sorted_rank), preferred_element_type=F32)
    rank = rank.astype(jnp.int32)
    near = chosen ^ first
    block = (near >> 1) + (near & 1) * (expert_count // 2)
    return jnp.where(rank < capacity, block * capacity + rank, -1)


def softmax_rows(logits):
    shifted = jnp.exp(logits - jnp.max(logits, axis=-1, keepdims=True))
    return shifted / jnp.sum(shifted, axis=-1, keepdims=True)


def one_hot_experts(ids, expert_count):
    return ids == lax.broadcasted_iota(jnp.int32, (ids.shape[0], expert_count), 1)


def middle_kernel(
    parts, tokens, cotangent, gains, router, ids, place_row, *rest
):
    attended, proj = rest[:parts], rest[parts : 2 * parts]
    even_rows, odd_rows, even_grads, odd_grads, middle, normed, probs = rest[2 * parts :]
    mixed = plain_order(jnp.concatenate([one[...] for one in attended], axis=0), 1)
    branch = dot_plain(mixed.T, jnp.concatenate([one[...] for one in proj], axis=0))
    total = tokens[...].astype(F32) + branch
    middle[...] = total
    unit, _ = rms_unit(total)
    normed_rows = low(gains[1:2, :] * unit)
    normed[...] = normed_rows
    chances = softmax_rows(dot_plain(normed_rows, router[...]))
    probs[...] = chances
    hot = one_hot_experts(ids[...], chances.shape[1])
    gate = jnp.sum(jnp.where(hot, chances, 0.0), axis=1, keepdims=True)
    weighted = low(gate * cotangent[...].astype(F32))
    half = even_rows.shape[0]
    for at, (row_slots, grad_slots) in enumerate(((even_rows, even_grads), (odd_rows, odd_grads))):
        slots = at * half + lax.broadcasted_iota(jnp.int32, (half, tokens.shape[0]), 0)
        dispatch = low(slots == place_row[...])
        row_slots[...] = low(dot_plain(dispatch, normed_rows))
        grad_slots[...] = low(dot_plain(dispatch, weighted))


def middle_rows(tokens, cotangent, gains, router, ids, place, slots, attended, proj):
    rows, width = tokens.shape
    half = shape((slots // 2, width))
    return pl.pallas_call(
        functools.partial(middle_kernel, len(attended)),
        out_shape=(
            half,
            half,
            half,
            half,
            shape((rows, width), F32),
            shape((rows, width)),
            shape((rows, router.shape[1]), F32),
        ),
        in_specs=[VM] * (6 + 2 * len(attended)),
        out_specs=(VM,) * 7,
        compiler_params=ROOM,
        name="middle_rows",
    )(tokens, cotangent, gains, router, ids, place[None, :], *attended, *proj)


def gather_slots(refs, capacity):
    own, beside, *pairs = refs
    even = [own[0:capacity, :]] + [pair[0:capacity, :] for pair in pairs]
    odd = [beside[0:capacity, :]] + [pair[capacity:, :] for pair in pairs]
    return jnp.concatenate(even + odd, axis=0)


def made_kernel(
    capacity, cotangent, ids, place_column, middle, normed, probs, *rest
):
    *row_refs, output, grad_logits, grad_router = rest
    rows, expert_count = probs.shape
    slots = 2 * row_refs[1].shape[0]
    slot_range = lax.broadcasted_iota(jnp.int32, (rows, slots), 1)
    dispatch = low(slot_range == place_column[...])
    routed = dot_plain(dispatch, gather_slots(row_refs, capacity))
    chances = probs[...]
    hot = one_hot_experts(ids[...], expert_count)
    gate = jnp.sum(jnp.where(hot, chances, 0.0), axis=1, keepdims=True)
    output[...] = low(middle[...] + gate * routed)
    grad_gate = jnp.sum(cotangent[...].astype(F32) * routed, axis=1, keepdims=True)
    logits = low((grad_gate * gate) * (hot.astype(F32) - chances))
    grad_logits[...] = logits
    grad_router[...] = dot_plain(logits.T, normed[...])


def made_rows(cotangent, ids, place, middle, normed, probs, row_slots):
    rows, width = middle.shape
    expert_count = probs.shape[1]
    capacity = row_slots[1].shape[0] // (len(row_slots) - 1)
    inputs = [cotangent, ids, place[:, None], middle, normed, probs, *row_slots]
    return pl.pallas_call(
        functools.partial(made_kernel, capacity),
        out_shape=(
            shape((rows, width)),
            shape((rows, expert_count)),
            shape((expert_count, width), F32),
        ),
        in_specs=[VM] * len(inputs),
        out_specs=(VM,) * 3,
        compiler_params=ROOM,
        name="made_rows",
    )(*inputs)


def back_kernel(
    parts, capacity, cotangent, gains, router, place_column, middle, grad_logits, *rest
):
    proj, rest = rest[:parts], rest[parts:]
    *grad_refs, grad_middle, grad_split, gain_two = rest[: -parts]
    near = rest[-parts:]
    rows = middle.shape[0]
    slots = 2 * grad_refs[1].shape[0]
    slot_range = lax.broadcasted_iota(jnp.int32, (rows, slots), 1)
    dispatch = low(slot_range == place_column[...])
    grad_second = dot_plain(dispatch, gather_slots(grad_refs, capacity))
    grad_second = grad_second + dot_last(grad_logits[...], router[...])
    unit, factor = rms_unit(middle[...])
    total = cotangent[...].astype(F32) + rms_backward(grad_second, unit, factor, gains[1:2, :])
    grad_low = split_order(low(total))
    for place in range(parts):
        near[place][...] = low(dot_last(proj[place][...], grad_low))
    grad_middle[...] = total
    grad_split[...] = grad_low
    summed = jnp.sum(grad_second * unit, axis=0, keepdims=True)
    gain_two[...] = jnp.broadcast_to(summed, gain_two.shape)


def back_rows(cotangent, gains, router, place, middle, grad_logits, proj, grad_slots):
    rows, width = middle.shape
    parts = len(proj)
    capacity = grad_slots[1].shape[0] // (len(grad_slots) - 1)
    inputs = [cotangent, gains, router, place[:, None], middle, grad_logits, *proj, *grad_slots]
    return pl.pallas_call(
        functools.partial(back_kernel, parts, capacity),
        out_shape=(
            shape((rows, width), F32),
            shape((rows, width)),
            shape((8, width), F32),
            *([shape((proj[0].shape[0], rows))] * parts),
        ),
        in_specs=[VM] * len(inputs),
        out_specs=(VM,) * (3 + parts),
        compiler_params=ROOM,
        name="back_rows",
    )(*inputs)


def proj_grad_kernel(grad_rows, *rest):
    *attended, keep, send = rest
    for place, one in enumerate(attended):
        part = dot_plain(one[...], grad_rows[...])
        if place % 2:
            send[place // 2] = low(part)
        else:
            keep[place // 2] = part


def proj_grad(grad_rows, attended):
    dims = (len(attended) // 2, attended[0].shape[0], grad_rows.shape[1])
    return pl.pallas_call(
        proj_grad_kernel,
        out_shape=(shape(dims, F32), shape(dims)),
        in_specs=[VM] * (1 + len(attended)),
        out_specs=(VM,) * 2,
        compiler_params=ROOM,
        name="proj_grad",
    )(grad_rows, *attended)


def expert_up_kernel(capacity, *refs):
    *parts, up, hidden, slope, rows_flip, rows = refs

    @pl.when(pl.program_id(0) == 0)
    def _():
        arrived = gather_slots(parts, capacity)
        rows[...] = arrived
        rows_flip[...] = arrived.T

    pre = dot_plain(rows[...], up[...])
    square = pre * pre
    bend = jnp.tanh(ROOT * (pre + CUBE * (square * pre)))
    half = 0.5 * (1.0 + bend)
    hidden[...] = low(pre * half)
    bent = (0.5 * ROOT) * pre * (1.0 - bend * bend) * (1.0 + (3.0 * CUBE) * square)
    slope[...] = low(half + bent)


def expert_out_kernel(hidden, down, even, odd):
    part = low(dot_plain(hidden[...], down[...]))

    @pl.when(pl.program_id(0) < 2)
    def _():
        even[...] = part

    @pl.when(pl.program_id(0) >= 2)
    def _():
        odd[...] = part


def expert_down_kernel(capacity, *refs):
    *parts, hidden, grad_down, grads, grads_flip = refs

    @pl.when(pl.program_id(0) == 0)
    def _():
        arrived = gather_slots(parts, capacity)
        grads[...] = arrived
        grads_flip[...] = arrived.T

    grad_down[...] = low(dot_plain(grads_flip[...], hidden[...]))


def expert_back_kernel(grads, slope, up, down, even, odd, grad_pre, total):
    step = pl.program_id(0)
    inner = low(dot_last(grads[...], down[...]) * slope[...].astype(F32))
    grad_pre[...] = inner
    part = dot_last(inner, up[...])

    @pl.when(step == 0)
    def _():
        total[...] = part

    @pl.when(step > 0)
    def _():
        total[...] += part

    @pl.when(step == pl.num_programs(0) - 1)
    def _():
        half = even.shape[0]
        even[...] = low(total[:half])
        odd[...] = low(total[half:])


def whole_spec(dims):
    return pl.BlockSpec(dims, lambda at: (0, 0))


def column_spec(rows):
    return pl.BlockSpec((rows, UNITS), lambda at: (0, at))


def row_spec(width):
    return pl.BlockSpec((UNITS, width), lambda at: (at, 0))


def expert_cost(products, slots, width, units):
    return pl.CostEstimate(
        flops=2 * products * slots * width * units,
        bytes_accessed=4 * slots * units + 2 * products * width * units,
        transcendentals=slots * units,
    )


def expert_hidden(parts, up):
    width, units = up.shape
    half = parts[1].shape[0]
    slots = 2 * half
    return pl.pallas_call(
        functools.partial(expert_up_kernel, half // (len(parts) - 1)),
        grid=(units // UNITS,),
        in_specs=[whole_spec(one.shape) for one in parts] + [column_spec(width)],
        out_specs=(column_spec(slots), column_spec(slots), whole_spec((width, slots))),
        out_shape=(shape((slots, units)), shape((slots, units)), shape((width, slots))),
        scratch_shapes=[pltpu.VMEM((slots, width), BF16)],
        compiler_params=ROOM,
        cost_estimate=expert_cost(1, slots, width, units),
        name="expert_hidden",
    )(*parts, up)


def expert_out(hidden, down):
    slots, units = hidden.shape
    width = down.shape[1]
    return pl.pallas_call(
        expert_out_kernel,
        grid=(4,),
        in_specs=[
            pl.BlockSpec((slots // 4, units), lambda at: (at, 0)),
            pl.BlockSpec((units, width), lambda at: (0, 0), pipeline_mode=pl.Buffered(1)),
        ],
        out_specs=(
            pl.BlockSpec((slots // 4, width), lambda at: (jnp.minimum(at, 1), 0)),
            pl.BlockSpec((slots // 4, width), lambda at: (jnp.maximum(at - 2, 0), 0)),
        ),
        out_shape=(shape((slots // 2, width)), shape((slots // 2, width))),
        compiler_params=ROOM,
        cost_estimate=expert_cost(1, slots, width, units),
        name="expert_out",
    )(hidden, down)


def expert_down_grad(parts, hidden):
    slots, units = hidden.shape
    half, width = parts[1].shape
    return pl.pallas_call(
        functools.partial(expert_down_kernel, half // (len(parts) - 1)),
        grid=(units // UNITS,),
        in_specs=[whole_spec(one.shape) for one in parts] + [column_spec(slots)],
        out_specs=(column_spec(width), whole_spec((slots, width))),
        out_shape=(shape((width, units)), shape((slots, width))),
        scratch_shapes=[pltpu.VMEM((width, slots), BF16)],
        compiler_params=ROOM,
        cost_estimate=expert_cost(1, slots, width, units),
        name="expert_down_grad",
    )(*parts, hidden)


def expert_back(grads, slope, up, down):
    slots, units = slope.shape
    width = grads.shape[1]
    block = whole_spec((slots // 2, width))
    return pl.pallas_call(
        expert_back_kernel,
        grid=(units // UNITS,),
        in_specs=[
            whole_spec(grads.shape),
            column_spec(slots),
            column_spec(width),
            row_spec(width),
        ],
        out_specs=(block, block, column_spec(slots)),
        out_shape=(
            shape((slots // 2, width)),
            shape((slots // 2, width)),
            shape((slots, units)),
        ),
        scratch_shapes=[pltpu.VMEM((slots, width), F32)],
        compiler_params=ROOM,
        cost_estimate=expert_cost(2, slots, width, units),
        name="expert_back",
    )(grads, slope, up, down)


def expert_up_grad_kernel(rows_flip, grad_pre, grad_up):
    grad_up[...] = low(dot_plain(rows_flip[...], grad_pre[...]))


def expert_up_grad(rows_flip, grad_pre):
    slots, units = grad_pre.shape
    width = rows_flip.shape[0]
    return pl.pallas_call(
        expert_up_grad_kernel,
        grid=(units // UNITS,),
        in_specs=[whole_spec(rows_flip.shape), column_spec(slots)],
        out_specs=column_spec(width),
        out_shape=shape((width, units)),
        compiler_params=ROOM,
        cost_estimate=expert_cost(1, slots, width, units),
        name="expert_up_grad",
    )(rows_flip, grad_pre)


def shards(
    tokens,
    cotangent,
    gains,
    qkv_weight,
    proj_weight,
    router_weight,
    expert_up,
    expert_down,
    expert_ids,
    slot_order,
    segment_ids,
):
    dp_count, ctx_count, tp_count = (lax.axis_size(name) for name in ("dp", "ctx", "tp"))
    dp_index, ctx_index, tp_index = (lax.axis_index(name) for name in ("dp", "ctx", "tp"))
    group = dp_count * tp_count
    group_index = dp_index * tp_count + tp_index
    tok_dev, width = tokens.shape
    half_rows = tok_dev // 2
    expert_count = router_weight.shape[1]
    capacity = 5 * tok_dev // (4 * expert_count)
    slots = expert_count * capacity
    per = PLEN // ctx_count // CHUNK
    conts_here = segment_ids.shape[0]
    prompts_here = conts_here * ctx_count // CONTS
    local_width = qkv_weight.shape[2]
    shard_rows = qkv_weight.shape[1]
    side, core = tp_index >> 1, tp_index & 1

    def across(value):
        return xor_swap(value, "tp", tp_count, 2)

    def beside(value):
        return xor_swap(value, "tp", tp_count, 1)

    packed = jnp.concatenate(
        [
            qkv_weight.transpose(1, 0, 2).reshape(shard_rows, 3 * local_width),
            proj_weight.T,
            router_weight,
        ],
        axis=1,
    )
    by_ctx = xor_exchange([packed] * ctx_count, "ctx", ctx_count)
    own, own_second = normalize(tokens, gains)
    far_second = across(own_second)
    carried = jnp.where(side == 0, own[:half_rows], far_second)
    by_ctx, carried = lax.optimization_barrier((by_ctx, carried))
    by_dp = xor_gather(jnp.stack(by_ctx), "dp", dp_count)
    far_first = across(own[:half_rows])
    arrived = ring_step(carried, "ctx", ctx_count, 1)
    arrived, far_first, by_dp = lax.optimization_barrier((arrived, far_first, by_dp))
    rows = [own, beside(own), far_first, far_second, beside(far_first), beside(far_second)]
    local_count = len(rows)

    by_dp = jnp.stack(by_dp).reshape((-1,) + packed.shape)
    shard_index = dp_index * ctx_count + ctx_index
    weights = jnp.concatenate(
        [pick(by_dp, shard_index ^ place) for place in range(dp_count * ctx_count)], axis=0
    )
    query_weight = weights[:, :local_width]
    pair_weight = weights[:, local_width : 3 * local_width]
    router = weights[:, 4 * local_width :]

    query, local = project_local(query_weight, pair_weight, rows)
    remote = []
    blocks = []
    for place in range(1, ctx_count):
        other = across(arrived)
        if place < ctx_count - 1:
            following = ring_step(arrived, "ctx", ctx_count, 1)
            if place == 1:
                expert_up, expert_down, following = lax.optimization_barrier(
                    (expert_up, expert_down, following)
                )
                full_up = lax.all_gather(expert_up, "ctx", axis=2, tiled=True)[0]
                full_down = lax.all_gather(expert_down, "ctx", axis=1, tiled=True)[0]
            if place == ctx_count - 2:
                following, query, local = lax.optimization_barrier((following, query, local))
            following, other = lax.optimization_barrier((following, other))
        blocks.append([arrived, other, beside(arrived), beside(other)])
        arrived = following
    rows += [one for block in blocks for one in block]
    remote = [project_remote(pair_weight, block) for block in blocks]
    proj_part, _ = lax.optimization_barrier(
        (weights[:, 3 * local_width : 4 * local_width].T, blocks[-1][1])
    )
    proj = xor_gather(proj_part, "tp", tp_count, [2, 1])

    device_chunks = tok_dev // CHUNK

    def split_place(at):
        return (at % 2) * (device_chunks // 2) + at // 2

    at = jnp.arange(prompts_here * per)
    owner, inside = at // device_chunks, at % device_chunks
    local_at = (owner ^ tp_index) * device_chunks + split_place(inside)
    remote_at = ((owner ^ core) * 2 + ((inside % 2) ^ side)) * (device_chunks // 2) + inside // 2
    prompt_at = jnp.concatenate(
        [local_at.reshape(prompts_here, per), remote_at.reshape(prompts_here, per)], axis=1
    )
    at = jnp.arange(conts_here)
    cont_at = ((2 + at // device_chunks) ^ tp_index) * device_chunks + split_place(
        at % device_chunks
    )
    info = jnp.concatenate([ctx_index[None], prompt_at.reshape(-1), cont_at, segment_ids])
    info = info.astype(jnp.int32)
    sizes = (prompts_here, conts_here, ctx_count, per)

    *attended, lse_prompt, lse_cont = attend_forward(sizes, info, query, local, remote)
    mixed = attended
    attended = xor_exchange(attended, "tp", tp_count)
    place = slot_places(expert_ids[:, 0], slot_order[0], group_index, expert_count, capacity)

    def start_exchange(odd):
        return xor_swap(odd, ("dp", "tp"), group, 1)

    def finish_exchange(even, other):
        moved = [even, other]
        for at in range(1, group // 2):
            block = slice(at * capacity, (at + 1) * capacity)
            pair = jnp.concatenate([even[block], other[block]], axis=0)
            moved.append(xor_swap(pair, ("dp", "tp"), group, 2 * at))
        return moved

    even_rows, odd_rows, even_grads, odd_grads, middle, normed_two, probs = middle_rows(
        tokens, cotangent, gains, router, expert_ids, place, slots, attended, proj
    )
    row_slots = finish_exchange(even_rows, start_exchange(odd_rows))
    other_grads = start_exchange(odd_grads)
    row_slots, even_grads, other_grads = lax.optimization_barrier(
        (row_slots, even_grads, other_grads)
    )
    grad_slots = finish_exchange(even_grads, other_grads)
    hidden, slope, rows_flip = expert_hidden(row_slots, full_up)
    grad_down, arrived_grads = expert_down_grad(grad_slots, hidden)
    hidden, arrived_grads = lax.optimization_barrier((hidden, arrived_grads))
    even, odd = expert_out(hidden, full_down)
    even, other, slope = lax.optimization_barrier((even, start_exchange(odd), slope))
    made_slots = finish_exchange(even, other)
    even, odd, grad_pre = expert_back(arrived_grads, slope, full_up, full_down)
    even, odd, made_slots, grad_pre = lax.optimization_barrier((even, odd, made_slots, grad_pre))
    back_slots = finish_exchange(even, start_exchange(odd))
    grad_down = lax.psum_scatter(grad_down, "ctx", scatter_dimension=1, tiled=True)
    grad_down = grad_down.T.astype(F32)[None]
    grad_up = expert_up_grad(rows_flip, grad_pre)

    output, grad_logits, router_part = made_rows(
        cotangent, expert_ids, place, middle, normed_two, probs, made_slots
    )
    grad_middle, grad_split, gain_two, *grad_near = back_rows(
        cotangent, gains, router, place, middle, grad_logits, proj, back_slots
    )
    grad_near = xor_exchange(grad_near, "tp", tp_count)
    proj_keep, proj_send = proj_grad(grad_split, attended)
    grad_near, proj_keep, proj_send, grad_up = lax.optimization_barrier(
        (grad_near, proj_keep, proj_send, grad_up)
    )
    grad_up = lax.psum_scatter(grad_up, "ctx", scatter_dimension=1, tiled=True).astype(F32)[None]
    grad_query, grad_local, *grads = attend_backward(
        sizes,
        info,
        query,
        lse_prompt,
        lse_cont,
        local,
        remote,
        pair_weight,
        grad_near,
        mixed,
    )
    count = ctx_count - 1
    grad_remote, remote_rows = grads[:count], grads[count:]
    if remote_rows:
        remote_rows = list(zip(remote_rows[:count], remote_rows[count:]))
    else:
        remote_rows = [rows_remote(one, pair_weight) for one in grad_remote]

    remote_rows = remote_rows[::-1]

    def chip_rows(keep, send):
        chip = keep.astype(F32) + beside(send).astype(F32)
        return chip[:half_rows], low(chip[half_rows:])

    def scatter_sum(values, axis, size, me):
        parts = xor_exchange([pick(values, me ^ k) for k in range(size)], axis, size)
        return add_all([piece.astype(F32) for piece in parts])

    piece, message = chip_rows(*remote_rows[0])
    following = chip_rows(*remote_rows[1])
    near = across(message)
    grad_pairs, message = lax.optimization_barrier(([grad_local, *grad_remote], message))
    qkv_part = qkv_grad(grad_query, grad_pairs, rows)
    near, qkv_part, following, grad_local, proj_send, remote_rows[2:] = lax.optimization_barrier(
        (near, qkv_part, following, grad_local, proj_send, remote_rows[2:])
    )
    running = low(piece + near.astype(F32))
    for place in range(1, count):
        piece, message = following
        message, running = lax.optimization_barrier((message, running))
        moved = ring_step(running, "ctx", ctx_count, -1)
        near = across(message)
        if place < count - 1:
            following = chip_rows(*remote_rows[place + 1])
        if place == 1:
            local_keep, local_send = rows_local(
                grad_local, grad_query, query_weight, pair_weight, tok_dev
            )
            local_send = beside(local_send)
            far_message = low(local_keep[0].astype(F32) + local_send[0].astype(F32))
            first_rows = (tok_dev - local_width) // 2
            proj_chip = proj_keep + beside(proj_send).astype(F32)
            far_first = jnp.concatenate([low(proj_chip[1]), far_message[:first_rows]], axis=0)
            near, far_first = lax.optimization_barrier((near, far_first))
            far_first = across(far_first)
            moved, near, far_first, following = lax.optimization_barrier(
                (moved, near, far_first, following)
            )
            proj_sum = proj_chip[0] + far_first[:local_width].astype(F32)
            early = jnp.concatenate([low(proj_sum), low(router_part), low(gain_two[:1])], axis=0)
            packed = jnp.concatenate([qkv_part, early.T], axis=1)
            packed = packed.reshape(dp_count, ctx_count, shard_rows, -1)
        if place == count - 1:
            summed = low(scatter_sum(packed, "dp", dp_count, dp_index))
            near, far_second = lax.optimization_barrier((near, far_message[first_rows:]))
            far_second = across(far_second)
            moved, near, summed, grad_up, grad_down = lax.optimization_barrier(
                (moved, near, summed, grad_up, grad_down)
            )
        running = low(piece + near.astype(F32) + moved.astype(F32))
    running, summed = lax.optimization_barrier((running, summed))
    hops = [[], []]
    for ctx_from in range(ctx_count):
        for tp_from in range(tp_count):
            target = (ctx_from - 1) % ctx_count * tp_count + (tp_from & 1)
            hops[tp_from >> 1].append((ctx_from * tp_count + tp_from, target))
    own_rows, other_rows = (lax.ppermute(running, ("ctx", "tp"), hop) for hop in hops)
    summed = scatter_sum(summed, "ctx", ctx_count, ctx_index)
    grad_tokens = final_rows(
        side.astype(jnp.int32).reshape(1),
        tokens,
        gains,
        grad_middle,
        local_keep,
        local_send,
        far_first,
        far_second,
        own_rows,
        other_rows,
    )

    qkv_width = 3 * local_width
    grad_qkv = summed[:, :qkv_width].reshape(shard_rows, 3, local_width).transpose(1, 0, 2)
    grad_proj = summed[:, qkv_width : qkv_width + local_width].T
    gain_range = lax.dynamic_slice_in_dim(gains[0], shard_index * shard_rows, shard_rows)
    gain_one = jnp.sum(qkv_weight.astype(F32) * grad_qkv, axis=(0, 2))
    small = jnp.concatenate([summed[:, qkv_width + local_width :], gain_one[:, None]], axis=1)
    parts = xor_exchange([low(small)] * tp_count, "tp", tp_count)
    parts, grad_tokens = lax.optimization_barrier((parts, grad_tokens))
    small = small + add_all([part.astype(F32) for part in parts[1:]])
    grad_router = small[:, :expert_count]
    grad_gains = jnp.stack([small[:, expert_count + 1] / gain_range, small[:, expert_count]])
    return (output, grad_tokens, grad_gains, grad_qkv, grad_proj, grad_router, grad_up, grad_down)


def solution(mesh):
    in_specs = (
        P(("dp", "ctx", "tp"), None),
        P(("dp", "ctx", "tp"), None),
        P(),
        P(None, ("dp", "ctx"), "tp"),
        P("tp", ("dp", "ctx")),
        P(("dp", "ctx"), None),
        P(("dp", "tp"), None, "ctx"),
        P(("dp", "tp"), "ctx", None),
        P(("dp", "ctx", "tp"), None),
        P(("dp", "ctx", "tp"), None),
        P(("dp", "ctx")),
    )
    out_specs = (
        P(("dp", "ctx", "tp"), None),
        P(("dp", "ctx", "tp"), None),
        P(None, ("dp", "ctx")),
        P(None, ("dp", "ctx"), "tp"),
        P("tp", ("dp", "ctx")),
        P(("dp", "ctx"), None),
        P(("dp", "tp"), None, "ctx"),
        P(("dp", "tp"), "ctx", None),
    )
    return jax.shard_map(shards, mesh=mesh, in_specs=in_specs, out_specs=out_specs, check_vma=False)
```
